32 devices in a mesh: seq: 16 (over z, x, core), fsdp: 2 (over y).
Axes of the slice: x: 2, y: 2, z: 4, core: 2. Of those that a mesh axis runs over, the one named last changes fastest.
Arguments:
- tokens: bfloat16 [2, 2048, 2048], P('fsdp', 'seq'), may hold values from -6 to 6
- cotangent: bfloat16 [2, 2048, 2048], P('fsdp', 'seq'), may hold values from -6 to 6
- segments: int32 [2, 2048], P('fsdp'), may hold values from 0 to 2047, as said below
- routes: int32 [2, 2048, 6], P('fsdp', 'seq'), may hold values from 0 to 15, all different within a row; in each aligned block of 128 rows (0 to 127, 128 to 255, ..., all dimensions but the last counted through in order) at most 64 rows name the same one
- norm_attn: float32 [2048], P(('seq', 'fsdp')), may hold values from 0.5 to 1.5
- w_query: float32 [2048, 3072], P(('seq', 'fsdp')), may hold values from -0.25 to 0.25
- w_latent: float32 [2048, 576], P(('seq', 'fsdp')), may hold values from -0.125 to 0.125
- norm_latent: float32 [512], P(('seq', 'fsdp')), may hold values from 0.5 to 1.5
- w_expand: float32 [512, 4096], P(('seq', 'fsdp')), may hold values from -0.25 to 0.25
- w_output: float32 [2048, 2048], P(('seq', 'fsdp')), may hold values from -0.75 to 0.75
- norm_ffn: float32 [2048], P(('seq', 'fsdp')), may hold values from 0.5 to 1.5
- w_router: float32 [2048, 16], P(('seq', 'fsdp')), may hold values from -0.0625 to 0.0625
- w_shared_gate: float32 [2048, 2816], P('fsdp', 'seq'), may hold values from -0.125 to 0.125
- w_shared_up: float32 [2048, 2816], P('fsdp', 'seq'), may hold values from -0.125 to 0.125
- w_shared_down: float32 [2816, 2048], P(('seq', 'fsdp')), may hold values from -0.15625 to 0.15625
- w_expert_gate: float32 [16, 2048, 1408], P('seq', 'fsdp'), may hold values from -0.125 to 0.125
- w_expert_up: float32 [16, 2048, 1408], P('seq', 'fsdp'), may hold values from -0.125 to 0.125
- w_expert_down: float32 [16, 1408, 2048], P('seq', 'fsdp'), may hold values from -1.25 to 1.25
Outputs:
- output: bfloat16 [2, 2048, 2048], P('fsdp', 'seq')
- input_grad: bfloat16 [2, 2048, 2048], P('fsdp', 'seq')
- grad_norm_attn: float32 [2048], P(('seq', 'fsdp'))
- grad_w_query: float32 [2048, 3072], P(('seq', 'fsdp'))
- grad_w_latent: float32 [2048, 576], P(('seq', 'fsdp'))
- grad_norm_latent: float32 [512], P(('seq', 'fsdp'))
- grad_w_expand: float32 [512, 4096], P(('seq', 'fsdp'))
- grad_w_output: float32 [2048, 2048], P(('seq', 'fsdp'))
- grad_norm_ffn: float32 [2048], P(('seq', 'fsdp'))
- grad_w_router: float32 [2048, 16], P(('seq', 'fsdp'))
- grad_w_shared_gate: float32 [2048, 2816], P('fsdp', 'seq')
- grad_w_shared_up: float32 [2048, 2816], P('fsdp', 'seq')
- grad_w_shared_down: float32 [2816, 2048], P(('seq', 'fsdp'))
- grad_w_expert_gate: float32 [16, 2048, 1408], P('seq', 'fsdp')
- grad_w_expert_up: float32 [16, 2048, 1408], P('seq', 'fsdp')
- grad_w_expert_down: float32 [16, 1408, 2048], P('seq', 'fsdp')
The draws below stay inside these ranges and needn't reach their ends.
Inputs may be any that keep to these rules, and one draw needn't show every extreme that they name: `routes`: each row names 6 different experts. In the rows of one device (aligned blocks of 128 rows of a sequence) no expert is named by more than 64 rows, a bound that some block reaches. `segments`: never falling along a sequence; equal numbers mark one document.
All inputs are finite; a program needn't handle non-finite values.
Results may differ from the reference program's by a relative error of at most 0.02.
The reference program's roundings to bfloat16 on the way count: a program that leaves them out, or rounds other values in their place, can miss the bound.
Values may be sent and summed in bfloat16 or wider, within the bound.
A program may use at most 448 MiB of HBM per device.

```python
import math
import jax
import jax.numpy as jnp
import numpy as np
from jax import lax

D = 2048
H = 16
NOPE = 128
ROPE = 64
VD = 128
LAT = 512
FF = 1408
TOP = 6
TOK_DEV = 128
FS = 2816
EXPERTS = 16
CAP = 64
LEN = 2048
SEQS = 2


def draw_segments(key, part):
    key = jax.random.fold_in(key, 11)
    key_pick, key_first, key_last, key_power, key_extra, key_shift = jax.random.split(key, 6)
    places = jnp.arange(LEN, dtype=jnp.int32)
    top_power = max(5, int(math.log2(LEN)))
    doc_count = LEN // 16 + 1
    powers = jax.random.randint(key_power, (SEQS, doc_count), 4, top_power)
    bases = jnp.left_shift(jnp.ones_like(powers), powers)
    extra = jax.random.randint(key_extra, (SEQS, doc_count), 0, 1 << 20) % bases
    lengths = (bases + extra).astype(jnp.int32)
    shift = jax.random.randint(key_shift, (SEQS, 1), 0, 16)
    bounds = jnp.cumsum(lengths, axis=1).astype(jnp.int32) - shift
    heavy = jnp.sum((bounds[:, None, :] <= places[None, :, None]).astype(jnp.int32), axis=2)
    first_start = jax.random.randint(key_first, (SEQS, 1), 1, TOK_DEV // 2 + 1)
    last_start = LEN - jax.random.randint(key_last, (SEQS, 1), 1, TOK_DEV // 2 + 1)
    spanning = (places[None, :] >= first_start).astype(jnp.int32) + (places[None, :] >= last_start).astype(jnp.int32)
    chosen = jax.random.randint(key_pick, (), 0, SEQS)
    which = jnp.arange(SEQS, dtype=jnp.int32)[:, None] == chosen
    order_ids = jnp.where(which, spanning, heavy).astype(jnp.int32)
    following = jnp.concatenate([order_ids[:, 1:], jnp.full((SEQS, 1), -1, jnp.int32)], axis=1)
    ending = order_ids != following
    marks = jnp.where(ending, jnp.broadcast_to(places[None, :], (SEQS, LEN)), LEN).astype(jnp.int32)
    return lax.cummin(marks, axis=1, reverse=True).astype(jnp.int32)


def strengthened(array, stream_key, source, target, parts, factor):
    owner, partner = [(jnp.arange(array.shape[axis_at]) // (array.shape[axis_at] // parts)).reshape([-1 if axis == axis_at else 1 for axis in range(array.ndim)]) for axis_at in (source, target)]
    chosen = jax.random.permutation(stream_key, parts)[partner]
    strong = (owner == chosen) | (owner == (partner + parts // 2) % parts)
    return jnp.where(strong, factor * array, array)


def block_levels(key, shape, cuts, least, largest):
    factor_of = 1.0
    for axis_at, blocks in cuts:
        steps = jax.random.uniform(jax.random.fold_in(jax.random.fold_in(key, 6), axis_at), (blocks,), jnp.float32, least / len(cuts), largest / len(cuts))
        factor_of = factor_of * jnp.repeat(jnp.exp(steps), shape[axis_at] // blocks).reshape((-1,) + (1,) * (len(shape) - 1 - axis_at))
    return factor_of


def assign_block(key, own, number, rows, count, top, limit, slope):
    order = jax.random.permutation(key, count)
    packed, common = portions_of(count, rows * top, limit, slope, True), portions_of(count, rows * top, limit, slope, False)
    places = jnp.arange(count)

    def named(sizes, turn):
        used = int((sizes > 0).sum())
        fixed = max(1, used // 4)
        shifted = fixed + (places - fixed + turn * (used - fixed)) % max(1, count - fixed)
        return jnp.zeros((count,), jnp.int32).at[order[jnp.where(places < fixed, places, shifted)]].set(jnp.asarray(sizes, jnp.int32))

    sizes = jnp.where(number % 4 == 0, named(packed, number // 4), named(common, number - number // 4 - 1))
    mixed = jax.random.permutation(jax.random.fold_in(own, 3), count)
    source_of, taker = mixed[0:count // 2 * 2:2], mixed[1:count // 2 * 2:2]
    room = jnp.minimum(sizes[source_of] - 1, limit - sizes[taker]) // 2
    room = jnp.where((source_of == order[0]) | (taker == order[0]) | (sizes[taker] == 0), 0, jnp.maximum(room, 0))
    shifted = jax.random.randint(jax.random.fold_in(own, 4), (count // 2,), 0, 1 << 20) % (room + 1)
    sizes = sizes.at[source_of].add(-shifted).at[taker].add(shifted)
    labels = jnp.searchsorted(jnp.cumsum(sizes), jnp.arange(rows * top), side="right").astype(jnp.int32)
    table = labels.reshape(top, rows).T
    table = table[jax.random.permutation(jax.random.fold_in(own, 1), rows)]
    turn = jax.random.randint(jax.random.fold_in(own, 2), (rows, 1), 0, top)
    return jnp.take_along_axis(table, (jnp.arange(top)[None, :] + turn) % top, axis=1)


def portions_of(amount, total, bound, skew, full):
    weights = [(1 << 20) // math.isqrt(standing ** skew) + 1 for standing in range(1, amount + 1)]
    largest = bound if full else min(bound, max(-(-total // amount), total * weights[0] // sum(weights)))
    least = 1 if total - largest >= amount - 1 else 0
    holding, surplus = [largest] + [least] * (amount - 1), total - largest - least * (amount - 1)
    while surplus > 0:
        candidates = [i for i in range(1, amount) if holding[i] < largest] or [i for i in range(1, amount) if holding[i] < bound]
        pool, budget = sum([weights[i] for i in candidates]), surplus
        for i in candidates:
            addition = min(bound - holding[i], max(1, budget * weights[i] // pool), surplus)
            holding[i] = holding[i] + addition
            surplus = surplus - addition
    return np.array(holding)


def normal_values(stream_key, dims, spread, reach, cuts=(), kind=jnp.bfloat16):
    values = jax.random.normal(stream_key, dims, jnp.float32) * spread
    if len(cuts) > 0:
        values = block_levels(stream_key, dims, cuts, -0.22, 0.18) * values
    return jnp.clip(values, min=-reach, max=reach).astype(kind)


def heavy_noise(rng, dims, deviation, limit, cuts, heavy, held_as=jnp.bfloat16):
    entries = deviation * jax.random.normal(rng, dims, jnp.float32)
    if cuts:
        entries = entries * block_levels(rng, dims, cuts, -0.22, 0.18)
    return jnp.clip(strengthened(entries, jax.random.fold_in(rng, 3), *heavy), -limit, limit).astype(held_as)


def setup_inputs(seed: int = 0) -> dict:
    key_list = jax.random.split(jax.random.key(seed), 19)
    tokens = normal_values(key_list[0], (SEQS, LEN, D), 1.0, 6.0, ((0, 2), (1, 16)))
    cotangent = heavy_noise(key_list[1], (SEQS, LEN, D), 1.0, 6.0, ((0, 2), (1, 16)), (1, 2, 16, 2.0))
    segments = draw_segments(jax.random.fold_in(key_list[18], 71), 0)
    routes_keys = jax.random.split(jax.random.fold_in(key_list[3], 1), SEQS * LEN // TOK_DEV)
    routes_turns = jax.random.permutation(jax.random.fold_in(key_list[3], 3), SEQS * LEN // TOK_DEV)
    routes = jax.vmap(lambda own, number: assign_block(jax.random.fold_in(key_list[3], 2), own, number, TOK_DEV, EXPERTS, TOP, CAP, 1))(routes_keys, routes_turns).reshape((SEQS, LEN, TOP))
    norm_attn = jnp.clip(1.0 + 0.1 * jax.random.normal(key_list[4], (D,), jnp.float32), 0.5, 1.5)
    w_query = normal_values(key_list[5], (D, H * (NOPE + ROPE)), (D // 4) ** -0.5, 0.25, ((0, 32),), jnp.float32)
    w_latent = normal_values(key_list[6], (D, LAT + ROPE), D ** -0.5, 0.125, ((0, 32),), jnp.float32)
    norm_latent = jnp.clip(1.0 + 0.1 * jax.random.normal(key_list[7], (LAT,), jnp.float32), 0.5, 1.5)
    w_expand = normal_values(key_list[8], (LAT, H * (NOPE + VD)), LAT ** -0.5, 0.25, ((0, 32),), jnp.float32)
    w_output = normal_values(key_list[9], (H * VD, D), (H * VD // 32) ** -0.5, 0.75, ((0, 32),), jnp.float32)
    norm_ffn = jnp.clip(1.0 + 0.1 * jax.random.normal(key_list[10], (D,), jnp.float32), 0.5, 1.5)
    w_router = normal_values(key_list[11], (D, EXPERTS), (4 * D) ** -0.5, 0.0625, ((0, 32),), jnp.float32)
    w_shared_gate = normal_values(key_list[12], (D, FS), D ** -0.5, 0.125, ((0, 2), (1, 16)), jnp.float32)
    w_shared_up = normal_values(key_list[13], (D, FS), D ** -0.5, 0.125, ((0, 2), (1, 16)), jnp.float32)
    w_shared_down = normal_values(key_list[14], (FS, D), (FS // 2) ** -0.5, 0.15625, ((0, 32),), jnp.float32)
    w_expert_gate = normal_values(key_list[15], (EXPERTS, D, FF), D ** -0.5, 0.125, ((0, 16), (1, 2)), jnp.float32)
    w_expert_up = normal_values(key_list[16], (EXPERTS, D, FF), D ** -0.5, 0.125, ((0, 16), (1, 2)), jnp.float32)
    w_expert_down = normal_values(key_list[17], (EXPERTS, FF, D), (FF // 64) ** -0.5, 1.25, ((0, 16), (1, 2)), jnp.float32)
    return {"tokens": tokens, "cotangent": cotangent, "segments": segments, "routes": routes, "norm_attn": norm_attn, "w_query": w_query, "w_latent": w_latent, "norm_latent": norm_latent, "w_expand": w_expand, "w_output": w_output, "norm_ffn": norm_ffn, "w_router": w_router, "w_shared_gate": w_shared_gate, "w_shared_up": w_shared_up, "w_shared_down": w_shared_down, "w_expert_gate": w_expert_gate, "w_expert_up": w_expert_up, "w_expert_down": w_expert_down}


EPSILON = 1e-06
HIGHEST = lax.Precision.HIGHEST

@jax.custom_vjp
def low(v):
    return lax.optimization_barrier(v.astype(jnp.bfloat16)).astype(jnp.float32)

@jax.custom_vjp
def low_back(v):
    return v

def low_keep(v):
    return (low(v), None)

def low_pass(kept, grad):
    return (grad,)

def back_keep(v):
    return (v, None)

def back_low(kept, grad):
    return (low(grad),)
low.defvjp(low_keep, low_pass)
low_back.defvjp(back_keep, back_low)

def product(left, right):
    return jnp.dot(left, right, precision=HIGHEST, preferred_element_type=jnp.float32)

def rms_norm(values, gain):
    factor = lax.rsqrt(lax.optimization_barrier(jnp.mean(values * values, axis=-1, keepdims=True)) + EPSILON)
    return values * factor * gain

def softmax_rows(scores):
    peak = lax.optimization_barrier(jnp.max(scores, axis=-1, keepdims=True))
    raised = jnp.exp(scores - peak)
    return raised / lax.optimization_barrier(jnp.sum(raised, axis=-1, keepdims=True))

def swish(values):
    return values * jax.nn.sigmoid(values)

def rotary_tables(count, offset):
    places = (offset + jnp.arange(count, dtype=jnp.int32)).astype(jnp.float32)
    powers = jnp.arange(ROPE // 2, dtype=jnp.int32).astype(jnp.float32) * (2.0 / ROPE)
    inverse = jnp.exp(powers * -math.log(10000.0))
    angles = places[:, None] * inverse[None, :]
    return (jnp.cos(angles), jnp.sin(angles))

def rotate(values, cosine_table, sine_table):
    halfway = values.shape[-1] // 2
    former = values[..., :halfway]
    latter = values[..., halfway:]
    return jnp.concatenate([former * cosine_table - latter * sine_table, latter * cosine_table + former * sine_table], axis=-1)

def one_sequence(hidden_in, doc_ids, expert_ids, weights):
    gain_attn, query_w, latent_w, gain_latent, expand_w, output_w, gain_ffn, router_w, shared_gate_w, shared_up_w, shared_down_w, expert_gate_w, expert_up_w, expert_down_w = weights
    cosine_table, sine_table = rotary_tables(LEN, 0)
    normed_one = low(rms_norm(hidden_in, gain_attn))
    query_proj = low_back(product(normed_one, query_w)).reshape(LEN, H, NOPE + ROPE)
    latent_proj = low_back(product(normed_one, latent_w))
    latent_normed = low(rms_norm(latent_proj[:, :LAT], gain_latent))
    expanded = product(latent_normed, expand_w).reshape(LEN, H, NOPE + VD)
    queries = jnp.concatenate([query_proj[..., :NOPE], rotate(query_proj[..., NOPE:], cosine_table[:, None, :], sine_table[:, None, :])], axis=-1)
    queries = low_back(low(queries))
    key_rope = rotate(latent_proj[:, LAT:], cosine_table, sine_table)
    key_rows = jnp.concatenate([expanded[..., :NOPE], jnp.broadcast_to(key_rope[:, None, :], (LEN, H, ROPE))], axis=-1)
    key_rows = low_back(low(key_rows))
    values = low_back(low(expanded[..., NOPE:]))
    places = jnp.arange(LEN, dtype=jnp.int32)
    allowed = (doc_ids[:, None] == doc_ids[None, :]) & (places[:, None] >= places[None, :])
    score_scale = (NOPE + ROPE) ** (-0.5)

    def one_head(triple):
        head_q, head_k, head_v = triple
        scores = low_back(product(head_q, head_k.T) * score_scale)
        scores = jnp.where(allowed, scores, -1e+30)
        attention = low(softmax_rows(scores))
        return low_back(low(product(attention, head_v)))
    attended = lax.map(jax.checkpoint(one_head), (jnp.transpose(queries, (1, 0, 2)), jnp.transpose(key_rows, (1, 0, 2)), jnp.transpose(values, (1, 0, 2))))
    merged = jnp.transpose(attended, (1, 0, 2)).reshape(LEN, H * VD)
    residual = hidden_in + low_back(product(merged, output_w))
    normed_two = low(rms_norm(residual, gain_ffn))
    router_p = softmax_rows(product(normed_two, router_w))
    gate_values = jnp.take_along_axis(router_p, expert_ids, axis=-1)
    blocks = LEN // TOK_DEV
    routed_ids = expert_ids.reshape(blocks, TOK_DEV * TOP)
    onehot = (routed_ids[..., None] == jnp.arange(EXPERTS, dtype=jnp.int32)).astype(jnp.int32)
    slot_rank = lax.optimization_barrier(jnp.sum((jnp.cumsum(onehot, axis=1) - 1) * onehot, axis=-1)).astype(jnp.int32)
    block_ids = jnp.arange(blocks, dtype=jnp.int32)[:, None]
    copies = low_back(jnp.broadcast_to(normed_two[:, None, :], (LEN, TOP, D))).reshape(blocks, TOK_DEV * TOP, D)
    buffer = jnp.zeros((EXPERTS, blocks, CAP, D), jnp.float32).at[routed_ids, block_ids, slot_rank].set(copies)

    def one_expert(members):
        expert_rows, gate_w, up_w, down_w = members
        expert_rows = expert_rows.reshape(blocks * CAP, D)
        gate_proj = low_back(product(expert_rows, gate_w))
        up_proj = low_back(product(expert_rows, up_w))
        inner_act = low(swish(gate_proj) * up_proj)
        return low_back(low(product(inner_act, down_w))).reshape(blocks, CAP, D)
    expert_out = lax.map(jax.checkpoint(one_expert), (buffer, expert_gate_w, expert_up_w, expert_down_w))
    picked = expert_out[routed_ids, block_ids, slot_rank].reshape(LEN, TOP, D)
    routed = lax.optimization_barrier(jnp.sum(gate_values[..., None] * picked, axis=1))
    shared_gate = low_back(product(normed_two, shared_gate_w))
    shared_up = low_back(product(normed_two, shared_up_w))
    shared_inner = low(swish(shared_gate) * shared_up)
    return residual + product(shared_inner, shared_down_w) + routed

def reference(tokens, cotangent, segments, routes, norm_attn, w_query, w_latent, norm_latent, w_expand, w_output, norm_ffn, w_router, w_shared_gate, w_shared_up, w_shared_down, w_expert_gate, w_expert_up, w_expert_down):
    masters = (norm_attn, w_query, w_latent, norm_latent, w_expand, w_output, norm_ffn, w_router, w_shared_gate, w_shared_up, w_shared_down, w_expert_gate, w_expert_up, w_expert_down)

    def forward(hidden, weights):
        rounded = tuple((low(weight) for weight in weights))

        def run(member):
            return one_sequence(member[0], member[1], member[2], rounded)
        return lax.map(jax.checkpoint(run), (hidden, segments, routes))
    result, pull = jax.vjp(forward, tokens.astype(jnp.float32), masters)
    hidden_grad, weight_grads = pull(cotangent.astype(jnp.float32))
    return (result.astype(jnp.bfloat16), hidden_grad.astype(jnp.bfloat16), weight_grads[0], weight_grads[1], weight_grads[2], weight_grads[3], weight_grads[4], weight_grads[5], weight_grads[6], weight_grads[7], weight_grads[8], weight_grads[9], weight_grads[10], weight_grads[11], weight_grads[12], weight_grads[13])
```

```python
import math

import jax
import jax.numpy as jnp
from jax import lax
from jax.sharding import PartitionSpec as P

H = 16
NOPE = 128
ROPE = 64
VD = 128
LAT = 512
TOP = 6
EPSILON = 1e-06
HIGHEST = lax.Precision.HIGHEST
LOW = jnp.bfloat16
F32 = jnp.float32


def rotary_tables(count, offset):
    places = (offset + jnp.arange(count, dtype=jnp.int32)).astype(F32)
    powers = jnp.arange(ROPE // 2, dtype=jnp.int32).astype(F32) * (2.0 / ROPE)
    inverse = jnp.exp(powers * -math.log(10000.0))
    angles = places[:, None] * inverse[None, :]
    return jnp.cos(angles), jnp.sin(angles)


def rotate(values, cosine, sine):
    half = values.shape[-1] // 2
    former, latter = values[..., :half], values[..., half:]
    return jnp.concatenate(
        [former * cosine - latter * sine, latter * cosine + former * sine], axis=-1
    )


def rotate_back(values, cosine, sine):
    return rotate(values, cosine, -sine)


def dot(left, right):
    return jnp.dot(left, right, preferred_element_type=F32)


def dot_t(left, right):
    return lax.dot_general(left, right, (((1,), (1,)), ((), ())), preferred_element_type=F32)


def t_dot(left, right):
    return lax.dot_general(left, right, (((0,), (0,)), ((), ())), preferred_element_type=F32)


def exact_t_dot(left, right):
    return lax.dot_general(
        left, right, (((0,), (0,)), ((), ())), precision=HIGHEST, preferred_element_type=F32
    )


def exact_dot_t(left, right):
    return lax.dot_general(
        left, right, (((1,), (1,)), ((), ())), precision=HIGHEST, preferred_element_type=F32
    )


def norm_forward(values, gain):
    factor = lax.rsqrt(jnp.mean(values * values, axis=-1, keepdims=True) + EPSILON)
    normed = values * factor
    return normed * gain, normed, factor


def norm_backward(grad_in, normed, factor, gain):
    inner = grad_in * gain
    gain_grad = jnp.sum(grad_in * normed, axis=0)
    back = factor * (inner - normed * jnp.mean(inner * normed, axis=-1, keepdims=True))
    return back, gain_grad


def swish_slope(value, sigmoid):
    return sigmoid * (1.0 + value * (1.0 - sigmoid))


def gather_rows(block):
    return lax.all_gather(block, "seq", axis=0, tiled=True)


def scatter_rows(partial):
    return lax.psum_scatter(partial, "seq", scatter_dimension=0, tiled=True)


def attend_forward(head_q, head_k, head_v, doc_ids):
    seq_len = head_q.shape[0]
    block_rows = min(512, seq_len)
    places = jnp.arange(seq_len, dtype=jnp.int32)
    scale = (NOPE + ROPE) ** (-0.5)

    def attend(index):
        start = index * block_rows
        query = lax.dynamic_slice_in_dim(head_q, start, block_rows, 0)
        docs = lax.dynamic_slice_in_dim(doc_ids, start, block_rows, 0)
        rows = start + jnp.arange(block_rows, dtype=jnp.int32)
        allowed = (docs[:, None] == doc_ids[None, :]) & (rows[:, None] >= places[None, :])
        scores = jnp.where(allowed, dot_t(query, head_k) * scale, -1e30)
        peak = jnp.max(scores, axis=-1, keepdims=True)
        raised = jnp.exp(scores - peak)
        totals = jnp.sum(raised, axis=-1, keepdims=True)
        out = dot((raised / totals).astype(LOW), head_v)
        return out.astype(LOW), peak + jnp.log(totals)

    out, logs = lax.map(attend, jnp.arange(seq_len // block_rows, dtype=jnp.int32))
    return out.reshape(seq_len, VD), logs.reshape(seq_len, 1)


def attend_backward(head_q, head_k, head_v, doc_ids, logs, head_g):
    seq_len = head_q.shape[0]
    block_rows = min(512, seq_len)
    places = jnp.arange(seq_len, dtype=jnp.int32)
    scale = (NOPE + ROPE) ** (-0.5)

    def back(carry, index):
        key_grad, value_grad = carry
        start = index * block_rows
        query = lax.dynamic_slice_in_dim(head_q, start, block_rows, 0)
        grad = lax.dynamic_slice_in_dim(head_g, start, block_rows, 0)
        log = lax.dynamic_slice_in_dim(logs, start, block_rows, 0)
        docs = lax.dynamic_slice_in_dim(doc_ids, start, block_rows, 0)
        rows = start + jnp.arange(block_rows, dtype=jnp.int32)
        allowed = (docs[:, None] == doc_ids[None, :]) & (rows[:, None] >= places[None, :])
        scores = jnp.where(allowed, dot_t(query, head_k) * scale, -1e30)
        attention = jnp.exp(scores - log)
        value_grad = value_grad + t_dot(attention.astype(LOW), grad)
        weight_grad = dot_t(grad, head_v)
        inner = jnp.sum(attention * weight_grad, axis=-1, keepdims=True)
        score_grad = (attention * (weight_grad - inner)).astype(LOW)
        query_grad = dot(score_grad, head_k) * scale
        key_grad = key_grad + t_dot(score_grad, query) * scale
        return (key_grad, value_grad), query_grad.astype(LOW)

    start = (
        jnp.zeros((seq_len, NOPE + ROPE), F32),
        jnp.zeros((seq_len, VD), F32),
    )
    (key_grad, value_grad), query_grad = lax.scan(
        back, start, jnp.arange(seq_len // block_rows, dtype=jnp.int32)
    )
    return query_grad.reshape(seq_len, NOPE + ROPE), key_grad.astype(LOW), value_grad.astype(LOW)


def body(
    tokens,
    cotangent,
    segments,
    routes,
    norm_attn,
    w_query,
    w_latent,
    norm_latent,
    w_expand,
    w_output,
    norm_ffn,
    w_router,
    w_shared_gate,
    w_shared_up,
    w_shared_down,
    w_expert_gate,
    w_expert_up,
    w_expert_down,
):
    groups = lax.axis_size("seq")
    layers = lax.axis_size("fsdp")
    both = ("seq", "fsdp")
    place = lax.axis_index("seq")
    tok_rows, width = tokens.shape[1], tokens.shape[2]
    seq_len = segments.shape[1]
    own_rows = w_query.shape[0]
    lat_rows = w_expand.shape[0]
    experts = w_router.shape[1]
    capacity = tok_rows // 2
    query_width = NOPE + ROPE
    hidden_own = tokens[0].astype(F32)
    grad_own = cotangent[0].astype(F32)
    doc_ids = segments[0]

    lat_column = jnp.pad(norm_latent[:, None], ((0, own_rows - lat_rows), (0, 0)))
    packed_small = jnp.concatenate(
        [w_latent, w_router, norm_attn[:, None], norm_ffn[:, None], lat_column], axis=1
    ).astype(LOW)
    used = packed_small.shape[1]
    packed_small = jnp.pad(packed_small, ((0, 0), (0, -used % 128)))
    small = lax.all_gather(packed_small, both, axis=0, tiled=True)
    latent_w = small[:, : LAT + ROPE]
    router_w = small[:, LAT + ROPE : LAT + ROPE + experts]
    gains = small[:, LAT + ROPE + experts : LAT + ROPE + experts + 3].astype(F32).T
    gain_attn, gain_ffn = gains[0], gains[1]
    gain_latent = gains[2].reshape(groups * layers, own_rows)[:, :lat_rows].reshape(LAT)

    fold = lat_rows * (NOPE + VD) // own_rows
    query_parts = w_query.astype(LOW).reshape(own_rows, H, query_width).transpose(1, 0, 2)
    expand_parts = (
        w_expand.astype(LOW)
        .reshape(lat_rows, H, NOPE + VD)
        .transpose(1, 0, 2)
        .reshape(H, own_rows, fold)
    )
    head_parts = jnp.concatenate([query_parts, expand_parts], axis=2)
    head_parts = lax.all_to_all(head_parts, "seq", split_axis=0, concat_axis=0, tiled=True)
    head_parts = lax.all_gather(head_parts, "fsdp", axis=1, tiled=False)
    query_w = head_parts[..., :query_width].reshape(width, query_width)
    expand_w = head_parts[..., query_width:].reshape(LAT, NOPE + VD)
    output_w = lax.all_gather(w_output.astype(LOW), "fsdp", axis=0, tiled=True)

    expert_gate_w = lax.all_gather(w_expert_gate[0].astype(LOW), "fsdp", axis=0, tiled=True)
    expert_up_w = lax.all_gather(w_expert_up[0].astype(LOW), "fsdp", axis=0, tiled=True)
    expert_down_w = lax.all_gather(w_expert_down[0].astype(LOW), "fsdp", axis=0, tiled=True)
    shared_in = jnp.concatenate([w_shared_gate, w_shared_up], axis=1).astype(LOW)
    shared_in_w = lax.all_gather(shared_in, "fsdp", axis=0, tiled=True)
    shared_down_w = lax.all_gather(w_shared_down.astype(LOW), "fsdp", axis=0, tiled=True)
    units = w_shared_gate.shape[1]

    hidden_low = gather_rows(tokens[0])
    grad_low = gather_rows(cotangent[0])
    all_routes = gather_rows(routes[0])

    scaled_one, _, _ = norm_forward(hidden_low.astype(F32), gain_attn)
    normed_low = scaled_one.astype(LOW)
    query_proj = dot(normed_low, query_w)
    latent_proj = dot(normed_low, latent_w)
    cosine, sine = rotary_tables(seq_len, 0)
    head_q = jnp.concatenate(
        [query_proj[:, :NOPE], rotate(query_proj[:, NOPE:], cosine, sine)], axis=-1
    ).astype(LOW)
    latent_scaled, _, _ = norm_forward(latent_proj[:, :LAT], gain_latent)
    latent_low = latent_scaled.astype(LOW)
    expanded = dot(latent_low, expand_w)
    key_rope = rotate(latent_proj[:, LAT:], cosine, sine)
    head_k = jnp.concatenate([expanded[:, :NOPE], key_rope], axis=-1).astype(LOW)
    head_v = expanded[:, NOPE:].astype(LOW)

    head_out, logs = attend_forward(head_q, head_k, head_v, doc_ids)
    residual = hidden_own + scatter_rows(dot(head_out, output_w).astype(LOW)).astype(F32)
    scaled_two, normed_two, factor_two = norm_forward(residual, gain_ffn)
    own_two_low = scaled_two.astype(LOW)
    two_low = gather_rows(own_two_low)

    logits = dot(two_low, router_w)
    raised = jnp.exp(logits - jnp.max(logits, axis=-1, keepdims=True))
    router_p = raised / jnp.sum(raised, axis=-1, keepdims=True)
    own_p = lax.dynamic_slice_in_dim(router_p, place * tok_rows, tok_rows, 0)
    mine = (jnp.arange(experts, dtype=jnp.int32) == place).astype(F32)
    gate = jnp.sum(router_p * mine[None, :], axis=-1).reshape(groups, tok_rows)
    named = jnp.any(all_routes == place, axis=-1).reshape(groups, tok_rows)
    rank = jnp.cumsum(named.astype(jnp.int32), axis=1) - 1
    slots = jnp.arange(capacity, dtype=jnp.int32)
    chosen = named[:, None, :] & (rank[:, None, :] == slots[None, :, None])
    chosen_low = chosen.astype(LOW)
    slot_gate = jnp.sum(jnp.where(chosen, gate[:, None, :], 0.0), axis=-1)
    slot_gate = slot_gate.reshape(groups * capacity, 1)

    def dispatch(rows):
        picked = jnp.einsum(
            "brt,btd->brd",
            chosen_low,
            rows.reshape(groups, tok_rows, width),
            preferred_element_type=F32,
        )
        return picked.reshape(groups * capacity, width).astype(LOW)

    def combine(rows):
        spread = jnp.einsum(
            "brt,brd->btd",
            chosen_low,
            rows.reshape(groups, capacity, width),
            preferred_element_type=F32,
        )
        return spread.reshape(seq_len, width)

    expert_in = dispatch(two_low)
    expert_g = dispatch(grad_low)
    made_grad = (slot_gate * expert_g.astype(F32)).astype(LOW)
    gate_proj = dot(expert_in, expert_gate_w)
    up_proj = dot(expert_in, expert_up_w)
    sigmoid = jax.nn.sigmoid(gate_proj)
    inner_low = (gate_proj * sigmoid * up_proj).astype(LOW)
    made = dot(inner_low, expert_down_w).astype(LOW)
    inner_grad = dot_t(made_grad, expert_down_w)
    gate_grad = (inner_grad * up_proj * swish_slope(gate_proj, sigmoid)).astype(LOW)
    up_grad = (inner_grad * gate_proj * sigmoid).astype(LOW)
    row_grad = (dot_t(gate_grad, expert_gate_w) + dot_t(up_grad, expert_up_w)).astype(LOW)
    slot_score = jnp.sum(expert_g.astype(F32) * made.astype(F32), axis=-1)
    score_grad = jnp.sum(
        jnp.where(chosen, slot_score.reshape(groups, capacity, 1), 0.0), axis=1
    )
    prob_grad = lax.all_to_all(score_grad, "seq", split_axis=0, concat_axis=0, tiled=True).T

    shared_proj = dot(two_low, shared_in_w)
    shared_gate, shared_up = shared_proj[:, :units], shared_proj[:, units:]
    shared_sigmoid = jax.nn.sigmoid(shared_gate)
    shared_low = (shared_gate * shared_sigmoid * shared_up).astype(LOW)
    shared_back = dot_t(grad_low, shared_down_w)
    shared_grads = jnp.concatenate(
        [
            shared_back * shared_up * swish_slope(shared_gate, shared_sigmoid),
            shared_back * shared_gate * shared_sigmoid,
        ],
        axis=1,
    ).astype(LOW)

    part_grad = combine(row_grad) + dot_t(shared_grads, shared_in_w)
    two_grad = scatter_rows(part_grad.astype(LOW)).astype(F32)
    part_out = combine((slot_gate * made.astype(F32)).astype(LOW)) + dot(shared_low, shared_down_w)
    ffn_out = scatter_rows(part_out.astype(LOW)).astype(F32)
    output = (residual + ffn_out).astype(LOW)

    def spread_grad(grad):
        return lax.psum_scatter(
            grad.astype(LOW), "fsdp", scatter_dimension=0, tiled=True
        ).astype(F32)

    grad_expert_down = spread_grad(t_dot(inner_low, made_grad))
    grad_expert_gate = spread_grad(t_dot(expert_in, gate_grad))
    grad_expert_up = spread_grad(t_dot(expert_in, up_grad))
    grad_shared_in = spread_grad(t_dot(two_low, shared_grads))
    grad_shared_down = spread_grad(t_dot(shared_low, grad_low))

    logit_grad = own_p * (prob_grad - jnp.sum(own_p * prob_grad, axis=-1, keepdims=True))
    grad_router = exact_t_dot(own_two_low.astype(F32), logit_grad)
    two_grad = two_grad + exact_dot_t(logit_grad, router_w.astype(F32))
    residual_part, grad_gain_ffn = norm_backward(two_grad, normed_two, factor_two, gain_ffn)
    residual_grad = grad_own + residual_part
    attn_grad = gather_rows(residual_grad.astype(LOW))

    grad_output = spread_grad(t_dot(head_out, attn_grad))
    head_g = dot_t(attn_grad, output_w).astype(LOW)
    query_grad, key_grad, value_grad = attend_backward(
        head_q, head_k, head_v, doc_ids, logs, head_g
    )
    query_back = jnp.concatenate(
        [
            query_grad[:, :NOPE],
            rotate_back(query_grad[:, NOPE:].astype(F32), cosine, sine).astype(LOW),
        ],
        axis=-1,
    )
    expand_back = jnp.concatenate([key_grad[:, :NOPE], value_grad], axis=-1)
    part_rows = jnp.concatenate(
        [
            dot_t(query_back, query_w).astype(LOW),
            dot_t(expand_back, expand_w).astype(LOW),
            key_grad[:, NOPE:],
            jnp.zeros((seq_len, 64), LOW),
        ],
        axis=1,
    )
    own_parts = scatter_rows(part_rows).astype(F32)

    grad_query_head = t_dot(normed_low, query_back).reshape(
        groups, layers, own_rows, query_width
    )
    grad_expand_head = t_dot(latent_low, expand_back).reshape(groups, layers, own_rows, fold)
    head_grads = jnp.concatenate([grad_query_head, grad_expand_head], axis=3).astype(LOW)
    head_grads = lax.psum_scatter(head_grads, "fsdp", scatter_dimension=1, tiled=False)
    head_grads = lax.all_to_all(head_grads, "seq", split_axis=0, concat_axis=0, tiled=True)
    grad_query = (
        head_grads[..., :query_width].transpose(1, 0, 2).reshape(own_rows, H * query_width)
    ).astype(F32)
    grad_expand = (
        head_grads[..., query_width:]
        .reshape(H, lat_rows, NOPE + VD)
        .transpose(1, 0, 2)
        .reshape(lat_rows, H * (NOPE + VD))
    ).astype(F32)

    own_low = lax.dynamic_slice_in_dim(normed_low, place * tok_rows, tok_rows, 0)
    own_latent = lax.dynamic_slice_in_dim(latent_proj, place * tok_rows, tok_rows, 0)
    own_cosine = lax.dynamic_slice_in_dim(cosine, place * tok_rows, tok_rows, 0)
    own_sine = lax.dynamic_slice_in_dim(sine, place * tok_rows, tok_rows, 0)
    _, latent_normed, latent_factor = norm_forward(own_latent[:, :LAT], gain_latent)
    latent_back, grad_gain_latent = norm_backward(
        own_parts[:, width : width + LAT], latent_normed, latent_factor, gain_latent
    )
    rope_back = rotate_back(
        own_parts[:, width + LAT : width + LAT + ROPE], own_cosine, own_sine
    )
    latent_grad = jnp.concatenate([latent_back, rope_back], axis=-1).astype(LOW)
    grad_latent = t_dot(own_low, latent_grad)
    one_grad = own_parts[:, :width] + dot_t(latent_grad, latent_w)
    _, normed_one, factor_one = norm_forward(hidden_own, gain_attn)
    input_part, grad_gain_attn = norm_backward(one_grad, normed_one, factor_one, gain_attn)
    input_grad = (residual_grad + input_part).astype(LOW)

    lat_spread = jnp.pad(
        grad_gain_latent.reshape(groups * layers, lat_rows), ((0, 0), (0, own_rows - lat_rows))
    ).reshape(width)
    gain_columns = jnp.stack([grad_gain_attn, grad_gain_ffn, lat_spread]).T
    packed = jnp.concatenate([grad_latent, grad_router, gain_columns], axis=1)
    packed = jnp.pad(packed, ((0, 0), (0, -used % 128)))
    packed = lax.psum_scatter(packed, both, scatter_dimension=0, tiled=True)
    at = LAT + ROPE + experts
    return (
        output[None],
        input_grad[None],
        packed[:, at],
        grad_query,
        packed[:, : LAT + ROPE],
        packed[:lat_rows, at + 2],
        grad_expand,
        grad_output,
        packed[:, at + 1],
        packed[:, LAT + ROPE : at],
        grad_shared_in[:, :units],
        grad_shared_in[:, units:],
        grad_shared_down,
        grad_expert_gate[None],
        grad_expert_up[None],
        grad_expert_down[None],
    )


def solution(mesh):
    flat = P(("seq", "fsdp"))
    rows = P(("seq", "fsdp"), None)
    tokens = P("fsdp", "seq", None)
    expert = P("seq", "fsdp", None)
    weights = (
        flat,
        rows,
        rows,
        flat,
        rows,
        rows,
        flat,
        rows,
        P("fsdp", "seq"),
        P("fsdp", "seq"),
        rows,
        expert,
        expert,
        expert,
    )
    return jax.shard_map(
        body,
        mesh=mesh,
        in_specs=(tokens, tokens, P("fsdp", None), tokens) + weights,
        out_specs=(tokens, tokens) + weights,
        check_vma=False,
    )
```

```python
import functools
import math

import jax
import jax.numpy as jnp
from jax import lax
from jax.experimental import pallas as pl
from jax.experimental.pallas import tpu as pltpu
from jax.sharding import PartitionSpec as P

H = 16
NOPE = 128
ROPE = 64
VD = 128
LAT = 512
TOP = 6
EPSILON = 1e-06
HIGHEST = lax.Precision.HIGHEST
LOW = jnp.bfloat16
F32 = jnp.float32
MESH = pl.DeviceIdType.MESH


def rotary_tables(count, offset):
    places = (offset + jnp.arange(count, dtype=jnp.int32)).astype(F32)
    powers = jnp.arange(ROPE // 2, dtype=jnp.int32).astype(F32) * (2.0 / ROPE)
    inverse = jnp.exp(powers * -math.log(10000.0))
    angles = places[:, None] * inverse[None, :]
    return jnp.cos(angles), jnp.sin(angles)


def rotate(values, cosine, sine):
    half = values.shape[-1] // 2
    former, latter = values[..., :half], values[..., half:]
    return jnp.concatenate(
        [former * cosine - latter * sine, latter * cosine + former * sine], axis=-1
    )


def rotate_back(values, cosine, sine):
    return rotate(values, cosine, -sine)


def dot(left, right):
    return jnp.dot(left, right, preferred_element_type=F32)


def dot_t(left, right):
    return lax.dot_general(left, right, (((1,), (1,)), ((), ())), preferred_element_type=F32)


def t_dot(left, right):
    return lax.dot_general(left, right, (((0,), (0,)), ((), ())), preferred_element_type=F32)


def exact_t_dot(left, right):
    return lax.dot_general(
        left, right, (((0,), (0,)), ((), ())), precision=HIGHEST, preferred_element_type=F32
    )


def exact_dot_t(left, right):
    return lax.dot_general(
        left, right, (((1,), (1,)), ((), ())), precision=HIGHEST, preferred_element_type=F32
    )


def norm_forward(values, gain):
    factor = lax.rsqrt(jnp.mean(values * values, axis=-1, keepdims=True) + EPSILON)
    normed = values * factor
    return normed * gain, normed, factor


def norm_backward(grad_in, normed, factor, gain):
    inner = grad_in * gain
    gain_grad = jnp.sum(grad_in * normed, axis=0)
    back = factor * (inner - normed * jnp.mean(inner * normed, axis=-1, keepdims=True))
    return back, gain_grad


def swish_slope(value, sigmoid):
    return sigmoid * (1.0 + value * (1.0 - sigmoid))


def whole_over_layers(own):
    if lax.axis_size("fsdp") != 2:
        return lax.all_gather(own, "fsdp", axis=0, tiled=True)
    other = lax.ppermute(own, "fsdp", ((0, 1), (1, 0)))
    first = lax.axis_index("fsdp") == 0
    return jnp.concatenate([jnp.where(first, own, other), jnp.where(first, other, own)], axis=0)


def gather_rows(block):
    return lax.all_gather(block, "seq", axis=0, tiled=True)


def scatter_rows(partial):
    return lax.psum_scatter(partial, "seq", scatter_dimension=0, tiled=True)


def ring_places(groups):
    ring = groups // 2
    me = lax.axis_index("seq")
    chip, core = me // 2, lax.rem(me, 2)
    odd = lax.rem(chip, 2)
    spot = (1 - odd) * (chip // 2) + odd * (ring - 1 - chip // 2)

    def chip_at(place):
        place = lax.rem(place + 2 * ring, ring)
        late = place // (ring // 2)
        return (1 - late) * (2 * place) + late * (2 * ring - 1 - 2 * place)

    def index_at(place, which):
        return 2 * chip_at(place) + which

    return spot, core, index_at


def enter(neighbours):
    barrier = pltpu.get_barrier_semaphore()
    for index in neighbours:
        pl.semaphore_signal(barrier, inc=1, device_id={"seq": index}, device_id_type=MESH)
    pl.semaphore_wait(barrier, len(neighbours))


class Gather:
    def __init__(self, groups, chunks, rows, source, out_ref, sems):
        self.groups, self.chunks, self.size = groups, chunks, rows // chunks
        self.source, self.out = source, out_ref
        self.send, self.recv, self.side_send, self.side_recv = sems
        self.spot, self.core, self.at = ring_places(groups)
        self.ring = groups // 2
        self.steps = groups // 4
        self.started = []

    def block(self, way, step):
        return self.at(self.spot - step if way == 0 else self.spot + step, self.core)

    def slice(self, ref, chunk):
        return ref.at[pl.ds(chunk * self.size, self.size)]

    def forward(self, step, chunk, way):
        index = self.block(way, step)
        own = self.slice(self.source if step == 0 else self.out.at[index], chunk)
        copy = pltpu.make_async_remote_copy(
            src_ref=own,
            dst_ref=self.slice(self.out.at[index], chunk),
            send_sem=self.send.at[way, step, chunk],
            recv_sem=self.recv.at[way, step, chunk],
            device_id={"seq": self.at(self.spot + (1 if way == 0 else -1), self.core)},
            device_id_type=MESH,
        )
        copy.start()
        self.started.append(copy)

    def arrived(self, step, chunk, way):
        index = self.block(way, step + 1)
        here = self.slice(self.out.at[index], chunk)
        pltpu.make_async_remote_copy(
            src_ref=here,
            dst_ref=here,
            send_sem=self.send.at[way, step, chunk],
            recv_sem=self.recv.at[way, step, chunk],
            device_id={"seq": self.at(self.spot, 1 - self.core)},
            device_id_type=MESH,
        ).wait_recv()

    def aside(self, distance, chunk):
        index = self.at(self.spot - distance, self.core)
        own = self.slice(self.source if distance == 0 else self.out.at[index], chunk)
        copy = pltpu.make_async_remote_copy(
            src_ref=own,
            dst_ref=self.slice(self.out.at[index], chunk),
            send_sem=self.side_send.at[distance, chunk],
            recv_sem=self.side_recv.at[distance, chunk],
            device_id={"seq": self.at(self.spot, 1 - self.core)},
            device_id_type=MESH,
        )
        copy.start()
        self.started.append(copy)

    def begin(self, chunk):
        for way in range(2):
            if self.steps > 1 or (chunk < self.chunks // 2) == (way == 0):
                self.forward(0, chunk, way)
        self.aside(0, chunk)

    def run(self):
        last = self.steps - 1
        for step in range(self.steps):
            for chunk in range(self.chunks):
                for way in range(2):
                    half = (chunk < self.chunks // 2) == (way == 0)
                    if step == last and not half:
                        continue
                    self.arrived(step, chunk, way)
                    if step < last and (step + 1 < last or half):
                        self.forward(step + 1, chunk, way)
                    self.aside(step + 1 if way == 0 else self.ring - 1 - step, chunk)

    def finish(self):
        for distance in range(self.ring):
            for chunk in range(self.chunks):
                here = self.slice(self.out.at[self.at(self.spot - distance, 1 - self.core)], chunk)
                pltpu.make_async_remote_copy(
                    src_ref=here,
                    dst_ref=here,
                    send_sem=self.side_send.at[distance, chunk],
                    recv_sem=self.side_recv.at[distance, chunk],
                    device_id={"seq": self.at(self.spot, 1 - self.core)},
                    device_id_type=MESH,
                ).wait_recv()
        for copy in self.started:
            copy.wait_send()


def gather_sems(groups, chunks):
    steps, ring = groups // 4, groups // 2
    return [
        pltpu.SemaphoreType.DMA((2, steps, chunks)),
        pltpu.SemaphoreType.DMA((2, steps, chunks)),
        pltpu.SemaphoreType.DMA((ring, chunks)),
        pltpu.SemaphoreType.DMA((ring, chunks)),
    ]


def gather_kernel(groups, chunks, in_ref, out_ref, own_sem, *sems):
    ring = Gather(groups, chunks, in_ref.shape[0], in_ref, out_ref, sems)
    spot, core, at = ring.spot, ring.core, ring.at
    enter((at(spot - 1, core), at(spot + 1, core), at(spot, 1 - core)))
    for chunk in range(chunks):
        ring.begin(chunk)
    own = pltpu.make_async_copy(in_ref, out_ref.at[at(spot, core)], own_sem)
    own.start()
    ring.run()
    ring.finish()
    own.wait()


def ring_gather(block, groups, collective_id, chunks=4):
    rows, columns = block.shape
    gathered = pl.pallas_call(
        functools.partial(gather_kernel, groups, chunks),
        out_shape=jax.ShapeDtypeStruct((groups, rows, columns), block.dtype),
        in_specs=[pl.BlockSpec(memory_space=pl.ANY)],
        out_specs=pl.BlockSpec(memory_space=pl.ANY),
        scratch_shapes=[pltpu.SemaphoreType.DMA] + gather_sems(groups, chunks),
        compiler_params=pltpu.CompilerParams(collective_id=collective_id, has_side_effects=True),
        cost_estimate=pl.CostEstimate(flops=0, bytes_accessed=150 << 20, transcendentals=0),
    )(block)
    return gathered.reshape(groups * rows, columns)


def reduce_kernel(groups, chunks, extras, outs, rowfn, gathers, *refs):
    parts_ref = refs[0]
    extra_refs = refs[1 : 1 + extras]
    out_refs = refs[1 + extras : 1 + extras + outs]
    rest = list(refs[1 + extras + outs :])
    gather_ref = rest.pop(0) if gathers else None
    own, side, came, sent = rest[:4]
    own_sem, side_send, side_recv, send_sem, recv_sem = rest[4:9]
    ready = rest[9] if gathers else None
    rows = own.shape[1]
    size = rows // chunks
    ring, steps = groups // 2, groups // 4
    spot, core, at = ring_places(groups)
    sibling = {"seq": at(spot, 1 - core)}
    enter((at(spot - 1, core), at(spot + 1, core), at(spot, 1 - core)))

    order = []
    for step in range(steps):
        order.append(steps - step)
        if step:
            order.append(ring - steps + step)
    order.append(0)
    started = []
    loads = {}
    for far in order:
        copy = pltpu.make_async_remote_copy(
            src_ref=parts_ref.at[at(spot + far, 1 - core)],
            dst_ref=side.at[far],
            send_sem=side_send.at[far],
            recv_sem=side_recv.at[far],
            device_id=sibling,
            device_id_type=MESH,
        )
        copy.start()
        started.append(copy)
        load = pltpu.make_async_copy(
            parts_ref.at[at(spot + far, core)], own.at[far], own_sem.at[far]
        )
        load.start()
        loads[far] = (load, copy)

    here = set()

    def both(far, chunk):
        if far not in here:
            here.add(far)
            loads[far][0].wait()
            loads[far][1].wait_recv()
        part = pl.ds(chunk * size, size)
        return own[far, part].astype(F32) + side[far, part].astype(F32)

    def neighbour_copy(way, step, chunk):
        part = pl.ds(chunk * size, size)
        return pltpu.make_async_remote_copy(
            src_ref=sent.at[way, step, part],
            dst_ref=came.at[way, step, part],
            send_sem=send_sem.at[way, step, chunk],
            recv_sem=recv_sem.at[way, step, chunk],
            device_id={"seq": at(spot + (1 if way == 0 else -1), core)},
            device_id_type=MESH,
        )

    def half(way, chunk):
        return (chunk < chunks // 2) == (way == 0)

    for step in range(steps):
        for chunk in range(chunks):
            for way in range(2):
                if step == 0 and not half(way, chunk):
                    continue
                far = steps - step if way == 0 else ring - (steps - step)
                part = pl.ds(chunk * size, size)
                total = both(far, chunk)
                if step > 1 or (step == 1 and half(way, chunk)):
                    neighbour_copy(way, step - 1, chunk).wait_recv()
                    total = total + came[way, step - 1, part].astype(F32)
                sent[way, step, part] = total.astype(sent.dtype)
                copy = neighbour_copy(way, step, chunk)
                copy.start()
                started.append(copy)
    gather = Gather(groups, chunks, rows, ready, gather_ref, rest[10:14]) if gathers else None
    for chunk in range(chunks):
        part = pl.ds(chunk * size, size)
        total = both(0, chunk)
        for way in range(2):
            if steps > 1 or half(way, chunk):
                neighbour_copy(way, steps - 1, chunk).wait_recv()
                total = total + came[way, steps - 1, part].astype(F32)
        made = rowfn(total, part, extra_refs, out_refs)
        if gathers:
            ready[part] = made
            gather.begin(chunk)
    if gathers:
        local = pltpu.make_async_copy(ready, gather_ref.at[at(spot, core)], rest[14])
        local.start()
        gather.run()
        gather.finish()
        local.wait()
    for copy in started:
        copy.wait_send()


def ring_reduce(parts, extras, outs, rowfn, groups, collective_id, gathers=None, chunks=4):
    _, rows, columns = parts.shape
    ring, steps = groups // 2, groups // 4
    scratch = [
        pltpu.VMEM((ring, rows, columns), LOW),
        pltpu.VMEM((ring, rows, columns), LOW),
        pltpu.VMEM((2, steps, rows, columns), LOW),
        pltpu.VMEM((2, steps, rows, columns), LOW),
        pltpu.SemaphoreType.DMA((ring,)),
        pltpu.SemaphoreType.DMA((ring,)),
        pltpu.SemaphoreType.DMA((ring,)),
        pltpu.SemaphoreType.DMA((2, steps, chunks)),
        pltpu.SemaphoreType.DMA((2, steps, chunks)),
    ]
    shapes = list(outs)
    specs = [pl.BlockSpec(memory_space=pltpu.VMEM)] * len(outs)
    if gathers is not None:
        shapes.append(jax.ShapeDtypeStruct((groups, rows, gathers), LOW))
        specs.append(pl.BlockSpec(memory_space=pl.ANY))
        scratch.append(pltpu.VMEM((rows, gathers), LOW))
        scratch += gather_sems(groups, chunks)
        scratch.append(pltpu.SemaphoreType.DMA)
    return pl.pallas_call(
        functools.partial(
            reduce_kernel, groups, chunks, len(extras), len(outs), rowfn, gathers is not None
        ),
        out_shape=shapes,
        in_specs=[pl.BlockSpec(memory_space=pl.ANY)]
        + [pl.BlockSpec(memory_space=pltpu.VMEM)] * len(extras),
        out_specs=specs,
        scratch_shapes=scratch,
        compiler_params=pltpu.CompilerParams(
            collective_id=collective_id, has_side_effects=True, vmem_limit_bytes=50 << 20
        ),
        cost_estimate=pl.CostEstimate(
            flops=0, bytes_accessed=(300 if gathers else 150) << 20, transcendentals=0
        ),
    )(parts, *extras)


def attend_kernel(blocks, q_ref, k_ref, v_ref, col_ref, row_ref, out_ref, log_ref):
    size = q_ref.shape[0] // blocks
    scale = (NOPE + ROPE) ** (-0.5)
    for index in range(blocks):
        part = pl.ds(index * size, size)
        reach = (index + 1) * size
        scores = dot_t(q_ref[part], k_ref[:reach]) * scale
        rows = index * size + lax.broadcasted_iota(jnp.int32, (size, reach), 0)
        columns = lax.broadcasted_iota(jnp.int32, (size, reach), 1)
        allowed = (col_ref[part] == row_ref[:, :reach]) & (rows >= columns)
        scores = jnp.where(allowed, scores, -1e30)
        peak = jnp.max(scores, axis=-1, keepdims=True)
        raised = jnp.exp(scores - peak)
        total = jnp.sum(raised, axis=-1, keepdims=True)
        weights = (raised * (1.0 / total)).astype(LOW)
        out_ref[part] = dot(weights, v_ref[:reach]).astype(LOW)
        log_ref[part] = peak + jnp.log(total)


def attend_forward(head_q, head_k, head_v, doc_ids):
    seq_len = head_q.shape[0]
    return pl.pallas_call(
        functools.partial(attend_kernel, seq_len // 256),
        out_shape=[
            jax.ShapeDtypeStruct((seq_len, VD), LOW),
            jax.ShapeDtypeStruct((seq_len, 1), F32),
        ],
        compiler_params=pltpu.CompilerParams(vmem_limit_bytes=50 << 20),
        cost_estimate=pl.CostEstimate(
            flops=seq_len * seq_len * 400, bytes_accessed=4 << 20, transcendentals=seq_len * seq_len // 2
        ),
    )(head_q, head_k, head_v, doc_ids[:, None], doc_ids[None, :])


def attend_back_kernel(
    blocks, q_ref, k_ref, v_ref, g_ref, col_ref, row_ref, log_ref, dq_ref, dk_ref, dv_ref, ksum, vsum
):
    size = q_ref.shape[0] // blocks
    scale = (NOPE + ROPE) ** (-0.5)
    ksum[...] = jnp.zeros_like(ksum)
    vsum[...] = jnp.zeros_like(vsum)
    for index in range(blocks):
        part = pl.ds(index * size, size)
        reach = (index + 1) * size
        query, grad = q_ref[part], g_ref[part]
        scores = dot_t(k_ref[:reach], query) * scale
        keys = lax.broadcasted_iota(jnp.int32, (reach, size), 0)
        rows = index * size + lax.broadcasted_iota(jnp.int32, (reach, size), 1)
        allowed = (col_ref[:reach] == row_ref[:, part]) & (rows >= keys)
        weights = jnp.exp(jnp.where(allowed, scores, -1e30) - log_ref[:, part])
        vsum[:reach] += dot(weights.astype(LOW), grad)
        slopes = dot_t(v_ref[:reach], grad)
        inner = jnp.sum(weights * slopes, axis=0, keepdims=True)
        back = (weights * (slopes - inner)).astype(LOW)
        ksum[:reach] += dot(back, query)
        dq_ref[part] = (t_dot(back, k_ref[:reach]) * scale).astype(LOW)
    dk_ref[...] = (ksum[...] * scale).astype(LOW)
    dv_ref[...] = vsum[...].astype(LOW)


def attend_backward(head_q, head_k, head_v, doc_ids, logs, head_g):
    seq_len = head_q.shape[0]
    return pl.pallas_call(
        functools.partial(attend_back_kernel, seq_len // 256),
        out_shape=[
            jax.ShapeDtypeStruct((seq_len, NOPE + ROPE), LOW),
            jax.ShapeDtypeStruct((seq_len, NOPE + ROPE), LOW),
            jax.ShapeDtypeStruct((seq_len, VD), LOW),
        ],
        scratch_shapes=[
            pltpu.VMEM((seq_len, NOPE + ROPE), F32),
            pltpu.VMEM((seq_len, VD), F32),
        ],
        compiler_params=pltpu.CompilerParams(vmem_limit_bytes=56 << 20),
        cost_estimate=pl.CostEstimate(
            flops=seq_len * seq_len * 1000, bytes_accessed=6 << 20, transcendentals=seq_len * seq_len // 2
        ),
    )(head_q, head_k, head_v, head_g, doc_ids[:, None], doc_ids[None, :], logs.reshape(1, seq_len))


def body(
    tokens,
    cotangent,
    segments,
    routes,
    norm_attn,
    w_query,
    w_latent,
    norm_latent,
    w_expand,
    w_output,
    norm_ffn,
    w_router,
    w_shared_gate,
    w_shared_up,
    w_shared_down,
    w_expert_gate,
    w_expert_up,
    w_expert_down,
):
    groups = lax.axis_size("seq")
    layers = lax.axis_size("fsdp")
    both = ("seq", "fsdp")
    place = lax.axis_index("seq")
    tok_rows, width = tokens.shape[1], tokens.shape[2]
    seq_len = segments.shape[1]
    own_rows = w_query.shape[0]
    lat_rows = w_expand.shape[0]
    experts = w_router.shape[1]
    capacity = tok_rows // 2
    query_width = NOPE + ROPE
    hidden_own = tokens[0].astype(F32)
    grad_own = cotangent[0].astype(F32)
    doc_ids = segments[0]

    lat_column = jnp.pad(norm_latent[:, None], ((0, own_rows - lat_rows), (0, 0)))
    packed_small = jnp.concatenate(
        [w_latent, w_router, norm_attn[:, None], norm_ffn[:, None], lat_column], axis=1
    ).astype(LOW)
    used = packed_small.shape[1]
    packed_small = jnp.pad(packed_small, ((0, 0), (0, -used % 128)))
    small = lax.all_gather(packed_small, both, axis=0, tiled=True)
    latent_w = small[:, : LAT + ROPE]
    router_w = small[:, LAT + ROPE : LAT + ROPE + experts]
    gains = small[:, LAT + ROPE + experts : LAT + ROPE + experts + 3].astype(F32).T
    gain_attn, gain_ffn = gains[0], gains[1]
    gain_latent = gains[2].reshape(groups * layers, own_rows)[:, :lat_rows].reshape(LAT)

    fold = lat_rows * (NOPE + VD) // own_rows
    query_parts = w_query.astype(LOW).reshape(own_rows, H, query_width).transpose(1, 0, 2)
    expand_parts = (
        w_expand.astype(LOW)
        .reshape(lat_rows, H, NOPE + VD)
        .transpose(1, 0, 2)
        .reshape(H, own_rows, fold)
    )
    head_parts = jnp.concatenate([query_parts, expand_parts], axis=2)
    head_parts = lax.all_to_all(head_parts, "seq", split_axis=0, concat_axis=0, tiled=True)
    head_parts = lax.all_gather(head_parts, "fsdp", axis=1, tiled=False)
    query_w = head_parts[..., :query_width].reshape(width, query_width)
    expand_w = head_parts[..., query_width:].reshape(LAT, NOPE + VD)
    output_w = lax.all_gather(w_output.astype(LOW), "fsdp", axis=0, tiled=True)

    expert_gate_w = whole_over_layers(w_expert_gate[0].astype(LOW))
    expert_up_w = whole_over_layers(w_expert_up[0].astype(LOW))
    expert_down_w = whole_over_layers(w_expert_down[0].astype(LOW))
    shared_in = jnp.concatenate([w_shared_gate, w_shared_up], axis=1).astype(LOW)
    shared_in_w = lax.all_gather(shared_in, "fsdp", axis=0, tiled=True)
    shared_down_w = lax.all_gather(w_shared_down.astype(LOW), "fsdp", axis=0, tiled=True)
    units = w_shared_gate.shape[1]

    hidden_low = ring_gather(tokens[0], groups, 1)
    grad_low = gather_rows(cotangent[0])
    all_routes = gather_rows(routes[0])

    scaled_one, _, _ = norm_forward(hidden_low.astype(F32), gain_attn)
    normed_low = scaled_one.astype(LOW)
    query_proj = dot(normed_low, query_w)
    latent_proj = dot(normed_low, latent_w)
    cosine, sine = rotary_tables(seq_len, 0)
    head_q = jnp.concatenate(
        [query_proj[:, :NOPE], rotate(query_proj[:, NOPE:], cosine, sine)], axis=-1
    ).astype(LOW)
    latent_scaled, _, _ = norm_forward(latent_proj[:, :LAT], gain_latent)
    latent_low = latent_scaled.astype(LOW)
    expanded = dot(latent_low, expand_w)
    key_rope = rotate(latent_proj[:, LAT:], cosine, sine)
    head_k = jnp.concatenate([expanded[:, :NOPE], key_rope], axis=-1).astype(LOW)
    head_v = expanded[:, NOPE:].astype(LOW)

    head_out, logs = attend_forward(head_q, head_k, head_v, doc_ids)
    part_residual = dot(head_out, output_w).astype(LOW).reshape(groups, tok_rows, width)

    def make_two(total, part, extras, outs):
        row_sum = extras[0][part].astype(F32) + total
        outs[0][part] = row_sum
        return norm_forward(row_sum, extras[1][...])[0].astype(LOW)

    own_shape = jax.ShapeDtypeStruct((tok_rows, width), F32)
    residual, two_low = ring_reduce(
        part_residual, [tokens[0], gain_ffn[None]], [own_shape], make_two, groups, 2, width
    )
    two_low = two_low.reshape(seq_len, width)
    own_two_low = lax.dynamic_slice_in_dim(two_low, place * tok_rows, tok_rows, 0)

    logits = dot(two_low, router_w)
    raised = jnp.exp(logits - jnp.max(logits, axis=-1, keepdims=True))
    router_p = raised / jnp.sum(raised, axis=-1, keepdims=True)
    own_p = lax.dynamic_slice_in_dim(router_p, place * tok_rows, tok_rows, 0)
    mine = (jnp.arange(experts, dtype=jnp.int32) == place).astype(F32)
    gate = jnp.sum(router_p * mine[None, :], axis=-1).reshape(groups, tok_rows)
    named = jnp.any(all_routes == place, axis=-1).reshape(groups, tok_rows)
    rank = jnp.cumsum(named.astype(jnp.int32), axis=1) - 1
    slots = jnp.arange(capacity, dtype=jnp.int32)
    chosen = named[:, None, :] & (rank[:, None, :] == slots[None, :, None])
    chosen_low = chosen.astype(LOW)
    slot_gate = jnp.sum(jnp.where(chosen, gate[:, None, :], 0.0), axis=-1)
    slot_gate = slot_gate.reshape(groups * capacity, 1)

    def dispatch(rows):
        picked = jnp.einsum(
            "brt,btd->brd",
            chosen_low,
            rows.reshape(groups, tok_rows, width),
            preferred_element_type=F32,
        )
        return picked.reshape(groups * capacity, width).astype(LOW)

    def combine(rows):
        spread = jnp.einsum(
            "brt,brd->btd",
            chosen_low,
            rows.reshape(groups, capacity, width),
            preferred_element_type=F32,
        )
        return spread.reshape(seq_len, width)

    expert_in = dispatch(two_low)
    expert_g = dispatch(grad_low)
    made_grad = (slot_gate * expert_g.astype(F32)).astype(LOW)
    gate_proj = dot(expert_in, expert_gate_w)
    up_proj = dot(expert_in, expert_up_w)
    sigmoid = jax.nn.sigmoid(gate_proj)
    inner_low = (gate_proj * sigmoid * up_proj).astype(LOW)
    made = dot(inner_low, expert_down_w).astype(LOW)
    inner_grad = dot_t(made_grad, expert_down_w)
    gate_grad = (inner_grad * up_proj * swish_slope(gate_proj, sigmoid)).astype(LOW)
    up_grad = (inner_grad * gate_proj * sigmoid).astype(LOW)
    row_grad = (dot_t(gate_grad, expert_gate_w) + dot_t(up_grad, expert_up_w)).astype(LOW)
    slot_score = jnp.sum(expert_g.astype(F32) * made.astype(F32), axis=-1)
    score_grad = jnp.sum(
        jnp.where(chosen, slot_score.reshape(groups, capacity, 1), 0.0), axis=1
    )
    prob_grad = lax.all_to_all(score_grad, "seq", split_axis=0, concat_axis=0, tiled=True).T

    shared_proj = dot(two_low, shared_in_w)
    shared_gate, shared_up = shared_proj[:, :units], shared_proj[:, units:]
    shared_sigmoid = jax.nn.sigmoid(shared_gate)
    shared_low = (shared_gate * shared_sigmoid * shared_up).astype(LOW)
    shared_back = dot_t(grad_low, shared_down_w)
    shared_grads = jnp.concatenate(
        [
            shared_back * shared_up * swish_slope(shared_gate, shared_sigmoid),
            shared_back * shared_gate * shared_sigmoid,
        ],
        axis=1,
    ).astype(LOW)

    part_grad = combine(row_grad) + dot_t(shared_grads, shared_in_w)
    part_out = combine((slot_gate * made.astype(F32)).astype(LOW)) + dot(shared_low, shared_down_w)
    ffn_out = scatter_rows(part_out.astype(LOW)).astype(F32)
    output = (residual + ffn_out).astype(LOW)

    def spread_grad(grad):
        if layers != 2:
            return lax.psum_scatter(
                grad.astype(LOW), "fsdp", scatter_dimension=0, tiled=True
            ).astype(F32)
        layer, half = lax.axis_index("fsdp"), grad.shape[0] // 2
        sent = lax.dynamic_slice_in_dim(grad, (1 - layer) * half, half, 0).astype(LOW)
        kept = lax.dynamic_slice_in_dim(grad, layer * half, half, 0)
        return kept + lax.ppermute(sent, "fsdp", ((0, 1), (1, 0))).astype(F32)

    grad_expert_down = spread_grad(t_dot(inner_low, made_grad))
    grad_expert_gate = spread_grad(t_dot(expert_in, gate_grad))
    grad_expert_up = spread_grad(t_dot(expert_in, up_grad))
    grad_shared_in = spread_grad(t_dot(two_low, shared_grads))
    grad_shared_down = spread_grad(t_dot(shared_low, grad_low))

    logit_grad = own_p * (prob_grad - jnp.sum(own_p * prob_grad, axis=-1, keepdims=True))
    grad_router = exact_t_dot(own_two_low.astype(F32), logit_grad)
    router_back = exact_dot_t(logit_grad, router_w.astype(F32))

    def make_attn(total, part, extras, outs):
        grad = total + extras[0][part]
        gain = extras[1][...]
        _, normed, factor = norm_forward(extras[2][part], gain)
        inner = grad * gain
        back = factor * (inner - normed * jnp.mean(inner * normed, axis=-1, keepdims=True))
        back = extras[3][part].astype(F32) + back
        outs[0][part] = back
        outs[1][part] = grad * normed
        return back.astype(LOW)

    residual_grad, gain_parts, attn_grad = ring_reduce(
        part_grad.astype(LOW).reshape(groups, tok_rows, width),
        [router_back, gain_ffn[None], residual, cotangent[0]],
        [own_shape, own_shape],
        make_attn,
        groups,
        3,
        width,
    )
    grad_gain_ffn = jnp.sum(gain_parts, axis=0)
    attn_grad = attn_grad.reshape(seq_len, width)

    grad_output = spread_grad(t_dot(head_out, attn_grad))
    head_g = dot_t(attn_grad, output_w).astype(LOW)
    query_grad, key_grad, value_grad = attend_backward(
        head_q, head_k, head_v, doc_ids, logs, head_g
    )
    query_back = jnp.concatenate(
        [
            query_grad[:, :NOPE],
            rotate_back(query_grad[:, NOPE:].astype(F32), cosine, sine).astype(LOW),
        ],
        axis=-1,
    )
    expand_back = jnp.concatenate([key_grad[:, :NOPE], value_grad], axis=-1)
    part_rows = jnp.concatenate(
        [
            dot_t(query_back, query_w).astype(LOW),
            dot_t(expand_back, expand_w).astype(LOW),
            key_grad[:, NOPE:],
            jnp.zeros((seq_len, 64), LOW),
        ],
        axis=1,
    )

    def keep(total, part, extras, outs):
        outs[0][part] = total

    wide = part_rows.shape[1]
    own_parts = ring_reduce(
        part_rows.reshape(groups, tok_rows, wide),
        [],
        [jax.ShapeDtypeStruct((tok_rows, wide), F32)],
        keep,
        groups,
        4,
    )[0]

    grad_query_head = t_dot(normed_low, query_back).reshape(
        groups, layers, own_rows, query_width
    )
    grad_expand_head = t_dot(latent_low, expand_back).reshape(groups, layers, own_rows, fold)
    head_grads = jnp.concatenate([grad_query_head, grad_expand_head], axis=3).astype(LOW)
    head_grads = lax.psum_scatter(head_grads, "fsdp", scatter_dimension=1, tiled=False)
    head_grads = lax.all_to_all(head_grads, "seq", split_axis=0, concat_axis=0, tiled=True)
    grad_query = (
        head_grads[..., :query_width].transpose(1, 0, 2).reshape(own_rows, H * query_width)
    ).astype(F32)
    grad_expand = (
        head_grads[..., query_width:]
        .reshape(H, lat_rows, NOPE + VD)
        .transpose(1, 0, 2)
        .reshape(lat_rows, H * (NOPE + VD))
    ).astype(F32)

    own_low = lax.dynamic_slice_in_dim(normed_low, place * tok_rows, tok_rows, 0)
    own_latent = lax.dynamic_slice_in_dim(latent_proj, place * tok_rows, tok_rows, 0)
    own_cosine = lax.dynamic_slice_in_dim(cosine, place * tok_rows, tok_rows, 0)
    own_sine = lax.dynamic_slice_in_dim(sine, place * tok_rows, tok_rows, 0)
    _, latent_normed, latent_factor = norm_forward(own_latent[:, :LAT], gain_latent)
    latent_back, grad_gain_latent = norm_backward(
        own_parts[:, width : width + LAT], latent_normed, latent_factor, gain_latent
    )
    rope_back = rotate_back(
        own_parts[:, width + LAT : width + LAT + ROPE], own_cosine, own_sine
    )
    latent_grad = jnp.concatenate([latent_back, rope_back], axis=-1).astype(LOW)
    grad_latent = t_dot(own_low, latent_grad)
    one_grad = own_parts[:, :width] + dot_t(latent_grad, latent_w)
    _, normed_one, factor_one = norm_forward(hidden_own, gain_attn)
    input_part, grad_gain_attn = norm_backward(one_grad, normed_one, factor_one, gain_attn)
    input_grad = (residual_grad + input_part).astype(LOW)

    lat_spread = jnp.pad(
        grad_gain_latent.reshape(groups * layers, lat_rows), ((0, 0), (0, own_rows - lat_rows))
    ).reshape(width)
    gain_columns = jnp.stack([grad_gain_attn, grad_gain_ffn, lat_spread]).T
    packed = jnp.concatenate([grad_latent, grad_router, gain_columns], axis=1)
    packed = jnp.pad(packed, ((0, 0), (0, -used % 128)))
    packed = lax.psum_scatter(packed, both, scatter_dimension=0, tiled=True)
    at = LAT + ROPE + experts
    return (
        output[None],
        input_grad[None],
        packed[:, at],
        grad_query,
        packed[:, : LAT + ROPE],
        packed[:lat_rows, at + 2],
        grad_expand,
        grad_output,
        packed[:, at + 1],
        packed[:, LAT + ROPE : at],
        grad_shared_in[:, :units],
        grad_shared_in[:, units:],
        grad_shared_down,
        grad_expert_gate[None],
        grad_expert_up[None],
        grad_expert_down[None],
    )


def solution(mesh):
    flat = P(("seq", "fsdp"))
    rows = P(("seq", "fsdp"), None)
    tokens = P("fsdp", "seq", None)
    expert = P("seq", "fsdp", None)
    weights = (
        flat,
        rows,
        rows,
        flat,
        rows,
        rows,
        flat,
        rows,
        P("fsdp", "seq"),
        P("fsdp", "seq"),
        rows,
        expert,
        expert,
        expert,
    )
    return jax.shard_map(
        body,
        mesh=mesh,
        in_specs=(tokens, tokens, P("fsdp", None), tokens) + weights,
        out_specs=(tokens, tokens) + weights,
        check_vma=False,
    )
```

```python
import functools
import math

import jax
import jax.numpy as jnp
from jax import lax
from jax.experimental import pallas as pl
from jax.experimental.pallas import tpu as pltpu
from jax.sharding import PartitionSpec as P

H = 16
NOPE = 128
ROPE = 64
VD = 128
LAT = 512
TOP = 6
EPSILON = 1e-06
HIGHEST = lax.Precision.HIGHEST
LOW = jnp.bfloat16
F32 = jnp.float32
MESH = pl.DeviceIdType.MESH


def rotary_tables(count, offset):
    places = (offset + jnp.arange(count, dtype=jnp.int32)).astype(F32)
    powers = jnp.arange(ROPE // 2, dtype=jnp.int32).astype(F32) * (2.0 / ROPE)
    inverse = jnp.exp(powers * -math.log(10000.0))
    angles = places[:, None] * inverse[None, :]
    return jnp.cos(angles), jnp.sin(angles)


def rotate(values, cosine, sine):
    half = values.shape[-1] // 2
    former, latter = values[..., :half], values[..., half:]
    return jnp.concatenate(
        [former * cosine - latter * sine, latter * cosine + former * sine], axis=-1
    )


def rotate_back(values, cosine, sine):
    return rotate(values, cosine, -sine)


def dot(left, right):
    return jnp.dot(left, right, preferred_element_type=F32)


def dot_t(left, right):
    return lax.dot_general(left, right, (((1,), (1,)), ((), ())), preferred_element_type=F32)


def t_dot(left, right):
    return lax.dot_general(left, right, (((0,), (0,)), ((), ())), preferred_element_type=F32)


def exact_t_dot(left, right):
    return lax.dot_general(
        left, right, (((0,), (0,)), ((), ())), precision=HIGHEST, preferred_element_type=F32
    )


def exact_dot_t(left, right):
    return lax.dot_general(
        left, right, (((1,), (1,)), ((), ())), precision=HIGHEST, preferred_element_type=F32
    )


def norm_forward(values, gain):
    factor = lax.rsqrt(jnp.mean(values * values, axis=-1, keepdims=True) + EPSILON)
    normed = values * factor
    return normed * gain, normed, factor


def norm_backward(grad_in, normed, factor, gain):
    inner = grad_in * gain
    gain_grad = jnp.sum(grad_in * normed, axis=0)
    back = factor * (inner - normed * jnp.mean(inner * normed, axis=-1, keepdims=True))
    return back, gain_grad


def swish_slope(value, sigmoid):
    return sigmoid * (1.0 + value * (1.0 - sigmoid))


def after(value, *others):
    return lax.optimization_barrier((value,) + others)[0]


def swap_layers(own):
    return lax.ppermute(own, "fsdp", ((0, 1), (1, 0)))


def layers_in_order(own, other, axis=0):
    first = lax.axis_index("fsdp") == 0
    return jnp.concatenate([jnp.where(first, own, other), jnp.where(first, other, own)], axis=axis)


def whole_over_layers(own):
    if lax.axis_size("fsdp") != 2:
        return lax.all_gather(own, "fsdp", axis=0, tiled=True)
    return layers_in_order(own, swap_layers(own))


def spread_start(grad, kind=LOW):
    layers = lax.axis_size("fsdp")
    if layers != 2:
        return grad.astype(kind), None
    layer, half = lax.axis_index("fsdp"), grad.shape[0] // 2
    sent = lax.dynamic_slice_in_dim(grad, (1 - layer) * half, half, 0).astype(kind)
    return lax.dynamic_slice_in_dim(grad, layer * half, half, 0), sent


def spread_end(kept, sent):
    if sent is None:
        return lax.psum_scatter(kept, "fsdp", scatter_dimension=0, tiled=True).astype(F32)
    return kept + swap_layers(sent).astype(F32)


def spread_grad(grad, kind=LOW):
    return spread_end(*spread_start(grad, kind))


def gather_rows(block):
    return lax.all_gather(block, "seq", axis=0, tiled=True)


def scatter_rows(partial):
    return lax.psum_scatter(partial, "seq", scatter_dimension=0, tiled=True)


def ring_places(groups):
    ring = groups // 2
    me = lax.axis_index("seq")
    chip, core = me // 2, lax.rem(me, 2)
    odd = lax.rem(chip, 2)
    spot = (1 - odd) * (chip // 2) + odd * (ring - 1 - chip // 2)

    def chip_at(place):
        place = lax.rem(place + 2 * ring, ring)
        late = place // (ring // 2)
        return (1 - late) * (2 * place) + late * (2 * ring - 1 - 2 * place)

    def index_at(place, which):
        return 2 * chip_at(place) + which

    return spot, core, index_at


def enter(neighbours):
    barrier = pltpu.get_barrier_semaphore()
    for index in neighbours:
        pl.semaphore_signal(barrier, inc=1, device_id={"seq": index}, device_id_type=MESH)
    pl.semaphore_wait(barrier, len(neighbours))


class Gather:
    def __init__(self, groups, chunks, rows, source, out_ref, sems):
        self.groups, self.chunks, self.size = groups, chunks, rows // chunks
        self.source, self.out = source, out_ref
        self.send, self.recv, self.side_send, self.side_recv = sems
        self.spot, self.core, self.at = ring_places(groups)
        self.ring = groups // 2
        self.steps = groups // 4
        self.started = []

    def block(self, way, step):
        return self.at(self.spot - step if way == 0 else self.spot + step, self.core)

    def slice(self, ref, chunk):
        return ref.at[pl.ds(chunk * self.size, self.size)]

    def forward(self, step, chunk, way):
        index = self.block(way, step)
        own = self.slice(self.source if step == 0 else self.out.at[index], chunk)
        copy = pltpu.make_async_remote_copy(
            src_ref=own,
            dst_ref=self.slice(self.out.at[index], chunk),
            send_sem=self.send.at[way, step, chunk],
            recv_sem=self.recv.at[way, step, chunk],
            device_id={"seq": self.at(self.spot + (1 if way == 0 else -1), self.core)},
            device_id_type=MESH,
        )
        copy.start()
        self.started.append(copy)

    def arrived(self, step, chunk, way):
        index = self.block(way, step + 1)
        here = self.slice(self.out.at[index], chunk)
        pltpu.make_async_remote_copy(
            src_ref=here,
            dst_ref=here,
            send_sem=self.send.at[way, step, chunk],
            recv_sem=self.recv.at[way, step, chunk],
            device_id={"seq": self.at(self.spot, 1 - self.core)},
            device_id_type=MESH,
        ).wait_recv()

    def aside(self, distance, chunk):
        index = self.at(self.spot - distance, self.core)
        own = self.slice(self.source if distance == 0 else self.out.at[index], chunk)
        copy = pltpu.make_async_remote_copy(
            src_ref=own,
            dst_ref=self.slice(self.out.at[index], chunk),
            send_sem=self.side_send.at[distance, chunk],
            recv_sem=self.side_recv.at[distance, chunk],
            device_id={"seq": self.at(self.spot, 1 - self.core)},
            device_id_type=MESH,
        )
        copy.start()
        self.started.append(copy)

    def begin(self, chunk):
        for way in range(2):
            if self.steps > 1 or (chunk < self.chunks // 2) == (way == 0):
                self.forward(0, chunk, way)
        self.aside(0, chunk)

    def run(self):
        last = self.steps - 1
        for step in range(self.steps):
            for chunk in range(self.chunks):
                for way in range(2):
                    half = (chunk < self.chunks // 2) == (way == 0)
                    if step == last and not half:
                        continue
                    self.arrived(step, chunk, way)
                    if step < last and (step + 1 < last or half):
                        self.forward(step + 1, chunk, way)
                    self.aside(step + 1 if way == 0 else self.ring - 1 - step, chunk)

    def finish(self):
        for distance in range(self.ring):
            for chunk in range(self.chunks):
                here = self.slice(self.out.at[self.at(self.spot - distance, 1 - self.core)], chunk)
                pltpu.make_async_remote_copy(
                    src_ref=here,
                    dst_ref=here,
                    send_sem=self.side_send.at[distance, chunk],
                    recv_sem=self.side_recv.at[distance, chunk],
                    device_id={"seq": self.at(self.spot, 1 - self.core)},
                    device_id_type=MESH,
                ).wait_recv()
        for copy in self.started:
            copy.wait_send()


def gather_sems(groups, chunks):
    steps, ring = groups // 4, groups // 2
    return [
        pltpu.SemaphoreType.DMA((2, steps, chunks)),
        pltpu.SemaphoreType.DMA((2, steps, chunks)),
        pltpu.SemaphoreType.DMA((ring, chunks)),
        pltpu.SemaphoreType.DMA((ring, chunks)),
    ]


def gather_kernel(groups, chunks, in_ref, out_ref, own_sem, *sems):
    ring = Gather(groups, chunks, in_ref.shape[0], in_ref, out_ref, sems)
    spot, core, at = ring.spot, ring.core, ring.at
    enter((at(spot - 1, core), at(spot + 1, core), at(spot, 1 - core)))
    for chunk in range(chunks):
        ring.begin(chunk)
    own = pltpu.make_async_copy(in_ref, out_ref.at[at(spot, core)], own_sem)
    own.start()
    ring.run()
    ring.finish()
    own.wait()


def ring_gather(block, groups, collective_id, chunks=4):
    rows, columns = block.shape
    gathered = pl.pallas_call(
        functools.partial(gather_kernel, groups, chunks),
        out_shape=jax.ShapeDtypeStruct((groups, rows, columns), block.dtype),
        in_specs=[pl.BlockSpec(memory_space=pl.ANY)],
        out_specs=pl.BlockSpec(memory_space=pl.ANY),
        scratch_shapes=[pltpu.SemaphoreType.DMA] + gather_sems(groups, chunks),
        compiler_params=pltpu.CompilerParams(collective_id=collective_id, has_side_effects=True),
        cost_estimate=pl.CostEstimate(flops=0, bytes_accessed=150 << 20, transcendentals=0),
    )(block)
    return gathered.reshape(groups * rows, columns)


def reduce_kernel(groups, chunks, extras, outs, rowfn, gathers, *refs):
    parts_ref = refs[0]
    extra_refs = refs[1 : 1 + extras]
    out_refs = refs[1 + extras : 1 + extras + outs]
    rest = list(refs[1 + extras + outs :])
    gather_ref = rest.pop(0) if gathers else None
    own, side, came, sent = rest[:4]
    own_sem, side_send, side_recv, send_sem, recv_sem = rest[4:9]
    ready = rest[9] if gathers else None
    rows = own.shape[1]
    size = rows // chunks
    ring, steps = groups // 2, groups // 4
    spot, core, at = ring_places(groups)
    sibling = {"seq": at(spot, 1 - core)}
    enter((at(spot - 1, core), at(spot + 1, core), at(spot, 1 - core)))

    order = []
    for step in range(steps):
        order.append(steps - step)
        if step:
            order.append(ring - steps + step)
    order.append(0)
    started = []
    loads = {}
    for far in order:
        copy = pltpu.make_async_remote_copy(
            src_ref=parts_ref.at[at(spot + far, 1 - core)],
            dst_ref=side.at[far],
            send_sem=side_send.at[far],
            recv_sem=side_recv.at[far],
            device_id=sibling,
            device_id_type=MESH,
        )
        copy.start()
        started.append(copy)
        load = pltpu.make_async_copy(
            parts_ref.at[at(spot + far, core)], own.at[far], own_sem.at[far]
        )
        load.start()
        loads[far] = (load, copy)

    here = set()

    def both(far, chunk):
        if far not in here:
            here.add(far)
            loads[far][0].wait()
            loads[far][1].wait_recv()
        part = pl.ds(chunk * size, size)
        return own[far, part].astype(F32) + side[far, part].astype(F32)

    def neighbour_copy(way, step, chunk):
        part = pl.ds(chunk * size, size)
        return pltpu.make_async_remote_copy(
            src_ref=sent.at[way, step, part],
            dst_ref=came.at[way, step, part],
            send_sem=send_sem.at[way, step, chunk],
            recv_sem=recv_sem.at[way, step, chunk],
            device_id={"seq": at(spot + (1 if way == 0 else -1), core)},
            device_id_type=MESH,
        )

    def half(way, chunk):
        return (chunk < chunks // 2) == (way == 0)

    for step in range(steps):
        for chunk in range(chunks):
            for way in range(2):
                if step == 0 and not half(way, chunk):
                    continue
                far = steps - step if way == 0 else ring - (steps - step)
                part = pl.ds(chunk * size, size)
                total = both(far, chunk)
                if step > 1 or (step == 1 and half(way, chunk)):
                    neighbour_copy(way, step - 1, chunk).wait_recv()
                    total = total + came[way, step - 1, part].astype(F32)
                sent[way, step, part] = total.astype(sent.dtype)
                copy = neighbour_copy(way, step, chunk)
                copy.start()
                started.append(copy)
    gather = Gather(groups, chunks, rows, ready, gather_ref, rest[10:14]) if gathers else None
    for chunk in range(chunks):
        part = pl.ds(chunk * size, size)
        total = both(0, chunk)
        for way in range(2):
            if steps > 1 or half(way, chunk):
                neighbour_copy(way, steps - 1, chunk).wait_recv()
                total = total + came[way, steps - 1, part].astype(F32)
        made = rowfn(total, part, extra_refs, out_refs)
        if gathers:
            ready[part] = made
            gather.begin(chunk)
    if gathers:
        local = pltpu.make_async_copy(ready, gather_ref.at[at(spot, core)], rest[14])
        local.start()
        gather.run()
        gather.finish()
        local.wait()
    for copy in started:
        copy.wait_send()


def ring_reduce(parts, extras, outs, rowfn, groups, collective_id, gathers=None, chunks=4):
    _, rows, columns = parts.shape
    ring, steps = groups // 2, groups // 4
    scratch = [
        pltpu.VMEM((ring, rows, columns), LOW),
        pltpu.VMEM((ring, rows, columns), LOW),
        pltpu.VMEM((2, steps, rows, columns), LOW),
        pltpu.VMEM((2, steps, rows, columns), LOW),
        pltpu.SemaphoreType.DMA((ring,)),
        pltpu.SemaphoreType.DMA((ring,)),
        pltpu.SemaphoreType.DMA((ring,)),
        pltpu.SemaphoreType.DMA((2, steps, chunks)),
        pltpu.SemaphoreType.DMA((2, steps, chunks)),
    ]
    shapes = list(outs)
    specs = [pl.BlockSpec(memory_space=pltpu.VMEM)] * len(outs)
    if gathers is not None:
        shapes.append(jax.ShapeDtypeStruct((groups, rows, gathers), LOW))
        specs.append(pl.BlockSpec(memory_space=pl.ANY))
        scratch.append(pltpu.VMEM((rows, gathers), LOW))
        scratch += gather_sems(groups, chunks)
        scratch.append(pltpu.SemaphoreType.DMA)
    return pl.pallas_call(
        functools.partial(
            reduce_kernel, groups, chunks, len(extras), len(outs), rowfn, gathers is not None
        ),
        out_shape=shapes,
        in_specs=[pl.BlockSpec(memory_space=pl.ANY)]
        + [pl.BlockSpec(memory_space=pltpu.VMEM)] * len(extras),
        out_specs=specs,
        scratch_shapes=scratch,
        compiler_params=pltpu.CompilerParams(
            collective_id=collective_id, has_side_effects=True, vmem_limit_bytes=50 << 20
        ),
        cost_estimate=pl.CostEstimate(
            flops=0, bytes_accessed=(300 if gathers else 150) << 20, transcendentals=0
        ),
    )(parts, *extras)


def attend_kernel(blocks, q_ref, k_ref, v_ref, col_ref, row_ref, out_ref, log_ref):
    size = q_ref.shape[0] // blocks
    scale = (NOPE + ROPE) ** (-0.5)
    for index in range(blocks):
        part = pl.ds(index * size, size)
        reach = (index + 1) * size
        scores = dot_t(q_ref[part], k_ref[:reach]) * scale
        rows = index * size + lax.broadcasted_iota(jnp.int32, (size, reach), 0)
        columns = lax.broadcasted_iota(jnp.int32, (size, reach), 1)
        allowed = (col_ref[part] == row_ref[:, :reach]) & (rows >= columns)
        scores = jnp.where(allowed, scores, -1e30)
        peak = jnp.max(scores, axis=-1, keepdims=True)
        raised = jnp.exp(scores - peak)
        total = jnp.sum(raised, axis=-1, keepdims=True)
        weights = (raised * (1.0 / total)).astype(LOW)
        out_ref[part] = dot(weights, v_ref[:reach]).astype(LOW)
        log_ref[part] = peak + jnp.log(total)


def attend_forward(head_q, head_k, head_v, doc_ids):
    seq_len = head_q.shape[0]
    return pl.pallas_call(
        functools.partial(attend_kernel, seq_len // 256),
        out_shape=[
            jax.ShapeDtypeStruct((seq_len, VD), LOW),
            jax.ShapeDtypeStruct((seq_len, 1), F32),
        ],
        compiler_params=pltpu.CompilerParams(vmem_limit_bytes=50 << 20),
        cost_estimate=pl.CostEstimate(
            flops=seq_len * seq_len * 400, bytes_accessed=4 << 20, transcendentals=seq_len * seq_len // 2
        ),
    )(head_q, head_k, head_v, doc_ids[:, None], doc_ids[None, :])


def attend_back_kernel(
    blocks, q_ref, k_ref, v_ref, g_ref, col_ref, row_ref, log_ref, dq_ref, dk_ref, dv_ref, ksum, vsum
):
    size = q_ref.shape[0] // blocks
    scale = (NOPE + ROPE) ** (-0.5)
    ksum[...] = jnp.zeros_like(ksum)
    vsum[...] = jnp.zeros_like(vsum)
    for index in range(blocks):
        part = pl.ds(index * size, size)
        reach = (index + 1) * size
        query, grad = q_ref[part], g_ref[part]
        scores = dot_t(k_ref[:reach], query) * scale
        keys = lax.broadcasted_iota(jnp.int32, (reach, size), 0)
        rows = index * size + lax.broadcasted_iota(jnp.int32, (reach, size), 1)
        allowed = (col_ref[:reach] == row_ref[:, part]) & (rows >= keys)
        weights = jnp.exp(jnp.where(allowed, scores, -1e30) - log_ref[:, part])
        vsum[:reach] += dot(weights.astype(LOW), grad)
        slopes = dot_t(v_ref[:reach], grad)
        inner = jnp.sum(weights * slopes, axis=0, keepdims=True)
        back = (weights * (slopes - inner)).astype(LOW)
        ksum[:reach] += dot(back, query)
        dq_ref[part] = (t_dot(back, k_ref[:reach]) * scale).astype(LOW)
    dk_ref[...] = (ksum[...] * scale).astype(LOW)
    dv_ref[...] = vsum[...].astype(LOW)


def attend_backward(head_q, head_k, head_v, doc_ids, logs, head_g):
    seq_len = head_q.shape[0]
    return pl.pallas_call(
        functools.partial(attend_back_kernel, seq_len // 256),
        out_shape=[
            jax.ShapeDtypeStruct((seq_len, NOPE + ROPE), LOW),
            jax.ShapeDtypeStruct((seq_len, NOPE + ROPE), LOW),
            jax.ShapeDtypeStruct((seq_len, VD), LOW),
        ],
        scratch_shapes=[
            pltpu.VMEM((seq_len, NOPE + ROPE), F32),
            pltpu.VMEM((seq_len, VD), F32),
        ],
        compiler_params=pltpu.CompilerParams(vmem_limit_bytes=56 << 20),
        cost_estimate=pl.CostEstimate(
            flops=seq_len * seq_len * 1000, bytes_accessed=6 << 20, transcendentals=seq_len * seq_len // 2
        ),
    )(head_q, head_k, head_v, head_g, doc_ids[:, None], doc_ids[None, :], logs.reshape(1, seq_len))


def swapped(values):
    half = values.shape[-1] // 2
    return jnp.concatenate([values[:, half:], values[:, :half]], axis=-1)


def project_kernel(
    x_ref, gain_ref, wq_ref, wl_ref, gain_lat_ref, we_ref, table_ref,
    one_ref, q_ref, k_ref, v_ref, m_ref, c_ref,
):
    one = norm_forward(x_ref[...].astype(F32), gain_ref[...])[0].astype(LOW)
    one_ref[...] = one
    cosine, sine = table_ref[:, :ROPE], table_ref[:, ROPE:]
    query = dot(one, wq_ref[...])
    turned = query[:, NOPE:]
    q_ref[:, :NOPE] = query[:, :NOPE].astype(LOW)
    q_ref[:, NOPE:] = (turned * cosine + swapped(turned) * sine).astype(LOW)
    latent = dot(one, wl_ref[...])
    turned = latent[:, LAT : LAT + ROPE]
    k_ref[:, NOPE:] = (turned * cosine + swapped(turned) * sine).astype(LOW)
    c_ref[...] = latent[:, :LAT]
    scaled = norm_forward(latent[:, :LAT], gain_lat_ref[...])[0].astype(LOW)
    m_ref[...] = scaled
    expanded = dot(scaled, we_ref[...])
    k_ref[:, :NOPE] = expanded[:, :NOPE].astype(LOW)
    v_ref[...] = expanded[:, NOPE:].astype(LOW)


def project(rows, gain, query_w, small, gain_latent, expand_w, table, tile=256):
    seq_len, width = rows.shape

    def cut(columns):
        return pl.BlockSpec((tile, columns), lambda i: (i, 0))

    def whole(array):
        return pl.BlockSpec(array.shape, lambda i: (0, 0))

    outs = [(width, LOW), (NOPE + ROPE, LOW), (NOPE + ROPE, LOW), (VD, LOW), (LAT, LOW), (LAT, F32)]
    return pl.pallas_call(
        project_kernel,
        grid=(seq_len // tile,),
        out_shape=[jax.ShapeDtypeStruct((seq_len, c), t) for c, t in outs],
        in_specs=[
            cut(width), whole(gain), whole(query_w), whole(small), whole(gain_latent),
            whole(expand_w), cut(2 * ROPE),
        ],
        out_specs=[cut(c) for c, _ in outs],
        compiler_params=pltpu.CompilerParams(vmem_limit_bytes=50 << 20),
        cost_estimate=pl.CostEstimate(
            flops=seq_len * width * 1800, bytes_accessed=28 << 20, transcendentals=0
        ),
    )(rows, gain, query_w, small, gain_latent, expand_w, table)


def project_back_kernel(
    dq_ref, dk_ref, dv_ref, table_ref, one_ref, m_ref, wq_ref, we_ref,
    parts_ref, gq_ref, ge_ref, dq_low, de_low,
):
    cosine, sine = table_ref[:, :ROPE], table_ref[:, ROPE:]
    turned = dq_ref[:, NOPE:].astype(F32)
    dq_low[:, :NOPE] = dq_ref[:, :NOPE]
    dq_low[:, NOPE:] = (turned * cosine - swapped(turned) * sine).astype(LOW)
    de_low[:, :NOPE] = dk_ref[:, :NOPE]
    de_low[:, NOPE:] = dv_ref[...]
    blocks, rows, wide = parts_ref.shape
    width, last = one_ref.shape[1], LAT + ROPE
    parts_ref[:, :, :width] = dot_t(dq_low[...], wq_ref[...]).astype(LOW).reshape(blocks, rows, width)
    parts_ref[:, :, width : width + LAT] = (
        dot_t(de_low[...], we_ref[...]).astype(LOW).reshape(blocks, rows, LAT)
    )
    parts_ref[:, :, width + LAT : width + last] = dk_ref[:, NOPE:].reshape(blocks, rows, ROPE)
    parts_ref[:, :, width + last :] = jnp.zeros((blocks, rows, wide - width - last), LOW)

    @pl.when(pl.program_id(0) == 0)
    def _():
        gq_ref[...] = jnp.zeros_like(gq_ref)
        ge_ref[...] = jnp.zeros_like(ge_ref)

    gq_ref[...] += t_dot(one_ref[...], dq_low[...])
    ge_ref[...] += t_dot(m_ref[...], de_low[...])


def project_back(grads, table, one_low, latent_low, query_w, expand_w, tok_rows, tile=256):
    seq_len, width = one_low.shape
    wide = width + LAT + 2 * ROPE

    def cut(columns):
        return pl.BlockSpec((tile, columns), lambda i: (i, 0))

    def whole(shape):
        return pl.BlockSpec(shape, lambda i: (0, 0))

    return pl.pallas_call(
        project_back_kernel,
        grid=(seq_len // tile,),
        out_shape=[
            jax.ShapeDtypeStruct((seq_len // tok_rows, tok_rows, wide), LOW),
            jax.ShapeDtypeStruct(query_w.shape, F32),
            jax.ShapeDtypeStruct(expand_w.shape, F32),
        ],
        in_specs=[
            cut(NOPE + ROPE), cut(NOPE + ROPE), cut(VD), cut(2 * ROPE), cut(width), cut(LAT),
            whole(query_w.shape), whole(expand_w.shape),
        ],
        out_specs=[
            pl.BlockSpec((tile // tok_rows, tok_rows, wide), lambda i: (i, 0, 0)),
            whole(query_w.shape),
            whole(expand_w.shape),
        ],
        scratch_shapes=[pltpu.VMEM((tile, NOPE + ROPE), LOW), pltpu.VMEM((tile, NOPE + VD), LOW)],
        compiler_params=pltpu.CompilerParams(vmem_limit_bytes=50 << 20),
        cost_estimate=pl.CostEstimate(
            flops=seq_len * width * 1300, bytes_accessed=28 << 20, transcendentals=0
        ),
    )(*grads, table, one_low, latent_low, query_w, expand_w)


def blocks_of(ref, count):
    size = ref.shape[0] // count
    return [pl.ds(block * size, size) for block in range(count)]


def two_parts(values):
    high = values.astype(LOW)
    return high, (values - high.astype(F32)).astype(LOW)


def ffn_kernel(
    rows_ref, chosen_ref, mine_ref, router_ref, wg_ref, wu_ref, wd_ref, wi_ref, wo_ref,
    probs_ref, slot_gate_ref, in_ref, gate_ref, up_ref, inner_ref, made_ref, proj_ref, hs_ref, out_ref,
    spread,
):
    count = 4
    tokens, slots = blocks_of(rows_ref, count), blocks_of(chosen_ref, count)
    lanes = lax.broadcasted_iota(jnp.int32, mine_ref.shape, 1)
    logits = jnp.where(mine_ref[1:2] > 0, dot(rows_ref[...], router_ref[...]), -1e30)
    raised = jnp.exp(logits - jnp.max(logits, axis=-1, keepdims=True))
    probs = raised / jnp.sum(raised, axis=-1, keepdims=True)
    probs_ref[...] = probs
    high, rest = two_parts(jnp.sum(probs * mine_ref[0:1], axis=-1, keepdims=True))
    high, rest = high.astype(F32), rest.astype(F32)
    columns = jnp.where(lanes[0:1] == 0, high, jnp.where(lanes[0:1] == 1, rest, 0.0)).astype(LOW)
    for token, slot in zip(tokens, slots):
        size = token.size
        picked = columns[token.start : token.start + size]
        chosen = chosen_ref[slot]
        slot_gate_ref[slot] = jnp.sum(dot(chosen, picked), axis=-1, keepdims=True)
        in_ref[slot] = dot(chosen, rows_ref[token]).astype(LOW)
    gate = dot(in_ref[...], wg_ref[...])
    up = dot(in_ref[...], wu_ref[...])
    gate_ref[...] = gate
    up_ref[...] = up
    inner_ref[...] = (gate * jax.nn.sigmoid(gate) * up).astype(LOW)
    made = dot(inner_ref[...], wd_ref[...]).astype(LOW)
    made_ref[...] = made
    spread[...] = (slot_gate_ref[...] * made.astype(F32)).astype(LOW)
    proj = dot(rows_ref[...], wi_ref[...])
    proj_ref[...] = proj
    half = proj.shape[1] // 2
    gate, up = proj[:, :half], proj[:, half:]
    hs_ref[...] = (gate * jax.nn.sigmoid(gate) * up).astype(LOW)
    for token, slot in zip(tokens, slots):
        total = t_dot(chosen_ref[slot], spread[slot]) + dot(hs_ref[token], wo_ref[...])
        out_ref[token] = total.astype(LOW)


def ffn_back_kernel(
    grads_ref, chosen_ref, mine_ref, slot_gate_ref, made_ref, gate_ref, up_ref, proj_ref,
    wg_ref, wu_ref, wd_ref, wi_ref, wo_ref,
    dy_ref, dgate_ref, dup_ref, dproj_ref, parts_ref, spread,
):
    count = 4
    width = grads_ref.shape[1]
    tokens, slots = blocks_of(grads_ref, count), blocks_of(chosen_ref, count)
    mine, shifted = mine_ref[0:1], mine_ref[2:3]
    for token, slot in zip(tokens, slots):
        picked = dot(chosen_ref[slot], grads_ref[token])
        dy_ref[slot] = (slot_gate_ref[slot] * picked).astype(LOW)
        score = jnp.sum(picked * made_ref[slot].astype(F32), axis=-1, keepdims=True)
        high, rest = two_parts(score)
        spread[slot, width:] = (high.astype(F32) * mine + rest.astype(F32) * shifted).astype(LOW)
    inner = dot_t(dy_ref[...], wd_ref[...])
    gate = gate_ref[...]
    sigmoid = jax.nn.sigmoid(gate)
    dgate_ref[...] = (inner * up_ref[...] * swish_slope(gate, sigmoid)).astype(LOW)
    dup_ref[...] = (inner * gate * sigmoid).astype(LOW)
    back = dot_t(dgate_ref[...], wg_ref[...]) + dot_t(dup_ref[...], wu_ref[...])
    spread[:, :width] = back.astype(LOW)
    half = proj_ref.shape[1] // 2
    gate, up = proj_ref[:, :half], proj_ref[:, half:]
    sigmoid = jax.nn.sigmoid(gate)
    inner = dot_t(grads_ref[...], wo_ref[...])
    dproj_ref[:, :half] = (inner * up * swish_slope(gate, sigmoid)).astype(LOW)
    dproj_ref[:, half:] = (inner * gate * sigmoid).astype(LOW)
    for block, (token, slot) in enumerate(zip(tokens, slots)):
        total = t_dot(chosen_ref[slot], spread[slot])
        parts_ref[block, :, :width] = (
            total[:, :width] + dot_t(dproj_ref[token], wi_ref[...])
        ).astype(LOW)
        parts_ref[block, :, width:] = total[:, width:].astype(LOW)


def row_grid(kernel, steps, cuts, outs, scratch, flops):
    def cut(shape):
        rest = (0,) * (len(shape) - 1)
        return pl.BlockSpec((shape[0] // steps,) + tuple(shape[1:]), lambda i: (i,) + rest)

    def whole(shape):
        rest = (0,) * len(shape)
        return pl.BlockSpec(tuple(shape), lambda i: rest, pipeline_mode=pl.Buffered(1))

    operands = [array for array, _ in cuts]
    return pl.pallas_call(
        kernel,
        grid=(steps,),
        out_shape=outs,
        in_specs=[whole(a.shape) if fixed else cut(a.shape) for a, fixed in cuts],
        out_specs=[cut(o.shape) for o in outs],
        scratch_shapes=scratch,
        compiler_params=pltpu.CompilerParams(vmem_limit_bytes=60 << 20),
        cost_estimate=pl.CostEstimate(flops=flops, bytes_accessed=60 << 20, transcendentals=0),
    )(*operands)


def grad_in_kernel(layer_ref, rows_ref, grads_ref, sent_ref, kept_ref):
    made = t_dot(rows_ref[...], grads_ref[...])
    step, half = pl.program_id(0), pl.num_programs(0) // 2

    @pl.when(step < half)
    def _():
        sent_ref[...] = made.astype(LOW)

    @pl.when(step >= half)
    def _():
        kept_ref[...] = made


def grad_in(rows, grads, tile=512):
    count, width = rows.shape
    columns = grads.shape[1]
    half = width // 2 // tile
    layer = lax.axis_index("fsdp").reshape(1)

    def source(i, layer_ref):
        return (0, lax.rem(i + (1 - layer_ref[0]) * half, 2 * half))

    return pl.pallas_call(
        grad_in_kernel,
        grid_spec=pltpu.PrefetchScalarGridSpec(
            num_scalar_prefetch=1,
            grid=(2 * half,),
            in_specs=[
                pl.BlockSpec((count, tile), source),
                pl.BlockSpec((count, columns), lambda i, _: (0, 0)),
            ],
            out_specs=[
                pl.BlockSpec((tile, columns), lambda i, _: (jnp.minimum(i, half - 1), 0)),
                pl.BlockSpec((tile, columns), lambda i, _: (jnp.maximum(i - half, 0), 0)),
            ],
        ),
        out_shape=[
            jax.ShapeDtypeStruct((width // 2, columns), LOW),
            jax.ShapeDtypeStruct((width // 2, columns), F32),
        ],
        compiler_params=pltpu.CompilerParams(vmem_limit_bytes=50 << 20),
        cost_estimate=pl.CostEstimate(
            flops=2 * count * width * columns, bytes_accessed=16 << 20, transcendentals=0
        ),
    )(layer, rows, grads)


def grad_out_kernel(layer_ref, inner_ref, grads_ref, sent_ref, kept_ref, made):
    half = sent_ref.shape[0]
    layer = layer_ref[0]
    made[...] = t_dot(inner_ref[...], grads_ref[...])
    sent_ref[...] = made[pl.ds(pl.multiple_of((1 - layer) * half, 8), half)].astype(LOW)
    kept_ref[...] = made[pl.ds(pl.multiple_of(layer * half, 8), half)]


def grad_out(inner, grads, tile=512):
    count, units = inner.shape
    width = grads.shape[1]
    layer = lax.axis_index("fsdp").reshape(1)
    return pl.pallas_call(
        grad_out_kernel,
        grid_spec=pltpu.PrefetchScalarGridSpec(
            num_scalar_prefetch=1,
            grid=(width // tile,),
            in_specs=[
                pl.BlockSpec((count, units), lambda i, _: (0, 0)),
                pl.BlockSpec((count, tile), lambda i, _: (0, i)),
            ],
            out_specs=[
                pl.BlockSpec((units // 2, tile), lambda i, _: (0, i)),
                pl.BlockSpec((units // 2, tile), lambda i, _: (0, i)),
            ],
            scratch_shapes=[pltpu.VMEM((units, tile), F32)],
        ),
        out_shape=[
            jax.ShapeDtypeStruct((units // 2, width), LOW),
            jax.ShapeDtypeStruct((units // 2, width), F32),
        ],
        compiler_params=pltpu.CompilerParams(vmem_limit_bytes=50 << 20),
        cost_estimate=pl.CostEstimate(
            flops=2 * count * width * units, bytes_accessed=16 << 20, transcendentals=0
        ),
    )(layer, inner, grads)


def body(
    tokens,
    cotangent,
    segments,
    routes,
    norm_attn,
    w_query,
    w_latent,
    norm_latent,
    w_expand,
    w_output,
    norm_ffn,
    w_router,
    w_shared_gate,
    w_shared_up,
    w_shared_down,
    w_expert_gate,
    w_expert_up,
    w_expert_down,
):
    groups = lax.axis_size("seq")
    layers = lax.axis_size("fsdp")
    both = ("seq", "fsdp")
    place = lax.axis_index("seq")
    tok_rows, width = tokens.shape[1], tokens.shape[2]
    seq_len = segments.shape[1]
    own_rows = w_query.shape[0]
    lat_rows = w_expand.shape[0]
    experts = w_router.shape[1]
    capacity = tok_rows // 2
    query_width = NOPE + ROPE
    hidden_own = tokens[0].astype(F32)
    grad_own = cotangent[0].astype(F32)
    doc_ids = segments[0]

    lat_column = jnp.pad(norm_latent[:, None], ((0, own_rows - lat_rows), (0, 0)))
    at = LAT + ROPE
    route_columns = routes.reshape(own_rows, tok_rows * TOP // own_rows).astype(F32)
    packed = [w_latent, w_router, norm_attn[:, None], norm_ffn[:, None], lat_column, route_columns]
    packed = jnp.concatenate(packed, axis=1).astype(LOW)
    used = packed.shape[1]
    last = at + experts
    packed = jnp.pad(packed, ((0, 0), (0, -used % 128)))
    small = lax.all_gather(packed, both, axis=0, tiled=True)
    router_w = jnp.pad(small[:, at:last], ((0, 0), (0, 128 - experts)))
    all_routes = small[:, last + 3 : used].reshape(groups, layers, -1)
    all_routes = lax.dynamic_index_in_dim(all_routes, lax.axis_index("fsdp"), 1, keepdims=False)
    all_routes = all_routes.reshape(groups, tok_rows, TOP)
    gains = small[:, last : last + 3].astype(F32).T
    gain_attn, gain_ffn = gains[0:1], gains[1:2]
    gain_latent = gains[2].reshape(groups * layers, own_rows)[:, :lat_rows].reshape(1, LAT)

    expert_gate_low = w_expert_gate[0].astype(LOW)
    expert_gate_w = whole_over_layers(expert_gate_low)

    fold = lat_rows * (NOPE + VD) // own_rows
    query_parts = w_query.astype(LOW).reshape(own_rows, H, query_width).transpose(1, 0, 2)
    expand_parts = (
        w_expand.astype(LOW)
        .reshape(lat_rows, H, NOPE + VD)
        .transpose(1, 0, 2)
        .reshape(H, own_rows, fold)
    )
    head_parts = jnp.concatenate([query_parts, expand_parts], axis=2)
    head_parts = lax.all_to_all(head_parts, "seq", split_axis=0, concat_axis=0, tiled=True)
    head_parts = whole_over_layers(head_parts[None]).transpose(1, 0, 2, 3)
    query_w = head_parts[..., :query_width].reshape(width, query_width)
    expand_w = head_parts[..., query_width:].reshape(LAT, NOPE + VD)
    output_w = whole_over_layers(w_output.astype(LOW))
    units = w_shared_gate.shape[1]
    padding = -units % 128
    spare = ((0, 0), (0, padding))
    shared_in = jnp.concatenate([jnp.pad(w_shared_gate, spare), jnp.pad(w_shared_up, spare)], axis=1)
    shared_in_w = whole_over_layers(shared_in.astype(LOW))
    shared_down_w = jnp.pad(whole_over_layers(w_shared_down.astype(LOW)), ((0, padding), (0, 0)))

    hidden_low = ring_gather(tokens[0], groups, 1)
    expert_up_w = whole_over_layers(after(w_expert_up[0].astype(LOW), expert_gate_w, hidden_low))
    expert_down_w = whole_over_layers(
        after(w_expert_down[0].astype(LOW), expert_gate_w, hidden_low)
    )
    grad_low = gather_rows(cotangent[0])

    cosine, sine = rotary_tables(seq_len, 0)
    table = jnp.concatenate([cosine, cosine, -sine, sine], axis=1)
    one_low, head_q, head_k, head_v, latent_low, latent_proj = project(
        hidden_low, gain_attn, query_w, small, gain_latent, expand_w, table
    )
    head_out, logs = attend_forward(head_q, head_k, head_v, doc_ids)
    part_residual = dot(head_out, output_w).astype(LOW).reshape(groups, tok_rows, width)

    def make_two(total, part, extras, outs):
        row_sum = extras[0][part].astype(F32) + total
        outs[0][part] = row_sum
        return norm_forward(row_sum, extras[1][...])[0].astype(LOW)

    own_shape = jax.ShapeDtypeStruct((tok_rows, width), F32)
    residual, two_low = ring_reduce(
        part_residual, [tokens[0], gain_ffn], [own_shape], make_two, groups, 2, width
    )
    two_low = two_low.reshape(seq_len, width)

    named = jnp.any(all_routes == place.astype(LOW), axis=-1)
    rank = jnp.cumsum(named.astype(jnp.int32), axis=1) - 1
    slots = jnp.arange(capacity, dtype=jnp.int32)
    chosen = named[:, None, :] & (rank[:, None, :] == slots[None, :, None])
    chosen = chosen.astype(LOW).reshape(groups * capacity, tok_rows)
    lanes = jnp.arange(128, dtype=jnp.int32)
    mine = jnp.stack(
        [(lanes == place), (lanes < experts), (lanes == place + experts)] + [lanes < 0] * 5
    ).astype(F32)
    slot_count, unit_count = groups * capacity, expert_gate_w.shape[1]
    columns = shared_in_w.shape[1]

    def array(rows, columns, kind=LOW):
        return jax.ShapeDtypeStruct((rows, columns), kind)

    steps = groups // 4
    routed_flops = 6 * slot_count * width * unit_count
    probs, slot_gate, expert_in, gate_proj, up_proj, inner_low, made, shared_proj, shared_low, part_out = row_grid(
        ffn_kernel,
        steps,
        [
            (two_low, False), (chosen, False), (mine, True), (router_w, True),
            (expert_gate_w, True), (expert_up_w, True), (expert_down_w, True),
            (shared_in_w, True), (shared_down_w, True),
        ],
        [
            array(seq_len, 128, F32), array(slot_count, 1, F32), array(slot_count, width),
            array(slot_count, unit_count, F32), array(slot_count, unit_count, F32),
            array(slot_count, unit_count), array(slot_count, width), array(seq_len, columns, F32),
            array(seq_len, columns // 2), array(seq_len, width),
        ],
        [pltpu.VMEM((slot_count // steps, width), LOW)],
        routed_flops * 3 // 2,
    )
    ffn_out = scatter_rows(part_out).astype(F32)
    output = (residual + ffn_out).astype(LOW)

    made_grad, gate_grad, up_grad, shared_grads, part_grad = row_grid(
        ffn_back_kernel,
        steps,
        [
            (grad_low, False), (chosen, False), (mine, True), (slot_gate, False), (made, False),
            (gate_proj, False), (up_proj, False), (shared_proj, False),
            (expert_gate_w, True), (expert_up_w, True), (expert_down_w, True),
            (shared_in_w, True), (shared_down_w, True),
        ],
        [
            array(slot_count, width), array(slot_count, unit_count), array(slot_count, unit_count),
            array(seq_len, columns),
            jax.ShapeDtypeStruct((groups, tok_rows, width + 128), LOW),
        ],
        [pltpu.VMEM((slot_count // steps, width + 128), LOW)],
        routed_flops * 3 // 2,
    )

    if layers == 2:
        down_sent, down_kept = grad_out(inner_low, made_grad)
        gate_sent, gate_kept = grad_in(expert_in, gate_grad)
        up_sent, up_kept = grad_in(expert_in, up_grad)
        part_grad = after(part_grad, down_sent, gate_sent, up_sent)
    else:
        down_kept, down_sent = spread_start(t_dot(inner_low, made_grad))
        gate_kept, gate_sent = spread_start(t_dot(expert_in, gate_grad))
        up_kept, up_sent = spread_start(t_dot(expert_in, up_grad))
    grad_expert_down = spread_end(down_kept, down_sent)
    grad_expert_gate = spread_end(gate_kept, gate_sent)
    grad_expert_up = spread_end(up_kept, up_sent)
    grad_shared_in = spread_grad(t_dot(two_low, shared_grads))
    grad_shared_down = spread_grad(t_dot(shared_low, grad_low)[:units])

    own_probs = lax.dynamic_slice_in_dim(probs, place * tok_rows, tok_rows, 0)

    def make_attn(total, part, extras, outs):
        probs = extras[0][part]
        score = total[:, width:]
        score = score + jnp.concatenate([score[:, experts:], score[:, :experts]], axis=1)
        logit = probs * (score - jnp.sum(probs * score, axis=-1, keepdims=True))
        high, rest = two_parts(logit)
        grad = total[:, :width] + dot_t(high, extras[4][...]) + dot_t(rest, extras[4][...])
        gain = extras[1][...]
        _, normed, factor = norm_forward(extras[2][part], gain)
        inner = grad * gain
        back = factor * (inner - normed * jnp.mean(inner * normed, axis=-1, keepdims=True))
        back = extras[3][part].astype(F32) + back
        outs[0][part] = back
        outs[1][part] = grad * normed
        rest = rest.astype(F32)
        rest = jnp.concatenate([rest[:, 128 - experts :], rest[:, : 128 - experts]], axis=1)
        return jnp.concatenate([back, high.astype(F32) + rest], axis=1).astype(LOW)

    residual_grad, gain_parts, attn_grad = ring_reduce(
        part_grad,
        [own_probs, gain_ffn, residual, cotangent[0], router_w],
        [own_shape, own_shape],
        make_attn,
        groups,
        3,
        width + 128,
    )
    grad_gain_ffn = jnp.sum(gain_parts, axis=0)
    attn_grad = attn_grad.reshape(seq_len, width + 128)

    own_width = width // groups
    two_slice = lax.dynamic_slice_in_dim(two_low, place * own_width, own_width, 1)
    grad_router = t_dot(two_slice, attn_grad[:, width:])
    grad_router = grad_router[:, :experts] + grad_router[:, experts : 2 * experts]

    grad_output = spread_grad(t_dot(head_out, attn_grad)[:, :width])
    head_g = dot_t(attn_grad, jnp.pad(output_w, ((0, 0), (0, 128)))).astype(LOW)
    query_grad, key_grad, value_grad = attend_backward(
        head_q, head_k, head_v, doc_ids, logs, head_g
    )
    part_rows, grad_query_head, grad_expand_head = project_back(
        (query_grad, key_grad, value_grad),
        table, one_low, latent_low, query_w, expand_w, tok_rows,
    )
    grad_query_head = grad_query_head.reshape(groups, layers, own_rows, query_width)
    grad_expand_head = grad_expand_head.reshape(groups, layers, own_rows, fold)
    head_grads = jnp.concatenate([grad_query_head, grad_expand_head], axis=3).transpose(1, 0, 2, 3)
    head_grads = spread_grad(head_grads)[0].astype(LOW)
    head_grads = lax.all_to_all(head_grads, "seq", split_axis=0, concat_axis=0, tiled=True)
    grad_query = (
        head_grads[..., :query_width].transpose(1, 0, 2).reshape(own_rows, H * query_width)
    ).astype(F32)
    grad_expand = (
        head_grads[..., query_width:]
        .reshape(H, lat_rows, NOPE + VD)
        .transpose(1, 0, 2)
        .reshape(lat_rows, H * (NOPE + VD))
    ).astype(F32)

    own_latent = lax.dynamic_slice_in_dim(latent_proj, place * tok_rows, tok_rows, 0)
    own_table = lax.dynamic_slice_in_dim(table, place * tok_rows, tok_rows, 0)

    def make_latent(total, part, extras, outs):
        gain = extras[1][...]
        grad = total[:, width : width + LAT]
        _, normed, factor = norm_forward(extras[0][part], gain)
        inner = grad * gain
        back = factor * (inner - normed * jnp.mean(inner * normed, axis=-1, keepdims=True))
        turned = total[:, width + LAT : width + LAT + ROPE]
        turned = turned * extras[2][part, :ROPE] - swapped(turned) * extras[2][part, ROPE:]
        outs[0][part] = total[:, :width]
        outs[1][part] = grad * normed
        return jnp.concatenate([back, turned, jnp.zeros_like(turned)], axis=1).astype(LOW)

    one_grad, latent_gains, latent_grad = ring_reduce(
        part_rows,
        [own_latent, gain_latent, own_table],
        [own_shape, jax.ShapeDtypeStruct((tok_rows, LAT), F32)],
        make_latent,
        groups,
        4,
        LAT + 2 * ROPE,
    )
    own_latent_grad = lax.dynamic_index_in_dim(latent_grad, place, 0, keepdims=False)
    one_grad = one_grad + dot_t(own_latent_grad[:, : LAT + ROPE], small[:, : LAT + ROPE])
    _, normed_one, factor_one = norm_forward(hidden_own, gain_attn)
    input_part, grad_gain_attn = norm_backward(one_grad, normed_one, factor_one, gain_attn)
    input_grad = (residual_grad + input_part).astype(LOW)

    one_slice = lax.dynamic_slice_in_dim(one_low, place * own_width, own_width, 1)
    grad_latent = t_dot(one_slice, latent_grad.reshape(seq_len, LAT + 2 * ROPE))
    gain_sums = jnp.concatenate(
        [
            grad_gain_attn.reshape(groups, own_width),
            grad_gain_ffn.reshape(groups, own_width),
            jnp.pad(
                jnp.sum(latent_gains, axis=0).reshape(groups, layers, lat_rows),
                ((0, 0), (0, 0), (0, own_rows - lat_rows)),
            ).reshape(groups, own_width),
        ],
        axis=1,
    )
    gain_sums = lax.all_to_all(gain_sums, "seq", split_axis=0, concat_axis=0, tiled=True)
    gain_columns = jnp.sum(gain_sums, axis=0).reshape(3, own_width).T
    packed = jnp.concatenate([grad_latent[:, :at], grad_router, gain_columns], axis=1)
    packed = jnp.pad(packed, ((0, 0), (0, -packed.shape[1] % 128)))
    packed = spread_grad(packed, F32)
    return (
        output[None],
        input_grad[None],
        packed[:, last],
        grad_query,
        packed[:, :at],
        packed[:lat_rows, last + 2],
        grad_expand,
        grad_output,
        packed[:, last + 1],
        packed[:, at:last],
        grad_shared_in[:, :units],
        grad_shared_in[:, units + padding : 2 * units + padding],
        grad_shared_down,
        grad_expert_gate[None],
        grad_expert_up[None],
        grad_expert_down[None],
    )


def solution(mesh):
    flat = P(("seq", "fsdp"))
    rows = P(("seq", "fsdp"), None)
    tokens = P("fsdp", "seq", None)
    expert = P("seq", "fsdp", None)
    weights = (
        flat,
        rows,
        rows,
        flat,
        rows,
        rows,
        flat,
        rows,
        P("fsdp", "seq"),
        P("fsdp", "seq"),
        rows,
        expert,
        expert,
        expert,
    )
    return jax.shard_map(
        body,
        mesh=mesh,
        in_specs=(tokens, tokens, P("fsdp", None), tokens) + weights,
        out_specs=(tokens, tokens) + weights,
        check_vma=False,
    )
```

```python
import functools
import math

import jax
import jax.numpy as jnp
import numpy as np
from jax import lax
from jax.experimental import pallas as pl
from jax.experimental.pallas import tpu as pltpu
from jax.sharding import PartitionSpec as P

H = 16
NOPE = 128
ROPE = 64
VD = 128
LAT = 512
TOP = 6
EPSILON = 1e-06
HIGHEST = lax.Precision.HIGHEST
LOW = jnp.bfloat16
F32 = jnp.float32
MESH = pl.DeviceIdType.MESH


def rotary_table(count):
    powers = np.arange(ROPE // 2, dtype=np.float32) * np.float32(2.0 / ROPE)
    inverse = np.exp(powers * np.float32(-math.log(10000.0)))
    angles = np.arange(count, dtype=np.float32)[:, None] * inverse[None, :]
    cosine, sine = np.cos(angles), np.sin(angles)
    return np.concatenate([cosine, cosine, -sine, sine], axis=1)


def dot(left, right):
    return jnp.dot(left, right, preferred_element_type=F32)


def dot_t(left, right):
    return lax.dot_general(left, right, (((1,), (1,)), ((), ())), preferred_element_type=F32)


def t_dot(left, right):
    return lax.dot_general(left, right, (((0,), (0,)), ((), ())), preferred_element_type=F32)


def exact_t_dot(left, right):
    return lax.dot_general(
        left, right, (((0,), (0,)), ((), ())), precision=HIGHEST, preferred_element_type=F32
    )


def exact_dot_t(left, right):
    return lax.dot_general(
        left, right, (((1,), (1,)), ((), ())), precision=HIGHEST, preferred_element_type=F32
    )


def norm_forward(values, gain):
    factor = lax.rsqrt(jnp.mean(values * values, axis=-1, keepdims=True) + EPSILON)
    normed = values * factor
    return normed * gain, normed, factor


def norm_backward(grad_in, normed, factor, gain):
    inner = grad_in * gain
    gain_grad = jnp.sum(grad_in * normed, axis=0)
    back = factor * (inner - normed * jnp.mean(inner * normed, axis=-1, keepdims=True))
    return back, gain_grad


def swish_slope(value, sigmoid):
    return sigmoid * (1.0 + value * (1.0 - sigmoid))


def after(value, *others):
    return lax.optimization_barrier((value,) + others)[0]


def narrow(array):
    return jnp.concatenate([array[:, i : i + 512] for i in range(0, array.shape[1], 512)])


def widen(array, width):
    rows = array.shape[0] * 512 // width
    return jnp.concatenate([array[i * rows : (i + 1) * rows] for i in range(width // 512)], axis=1)


def swap_layers(own):
    return lax.ppermute(own, "fsdp", ((0, 1), (1, 0)))


def layers_in_order(own, other, axis=0):
    first = lax.axis_index("fsdp") == 0
    return jnp.concatenate([jnp.where(first, own, other), jnp.where(first, other, own)], axis=axis)


def whole_over_layers(own):
    if lax.axis_size("fsdp") != 2:
        return lax.all_gather(own, "fsdp", axis=0, tiled=True)
    return layers_in_order(own, swap_layers(own))


def halves_over_layers(own):
    if lax.axis_size("fsdp") == 2:
        return own, swap_layers(own)
    whole = lax.all_gather(own, "fsdp", axis=0, tiled=True)
    half = whole.shape[0] // 2
    return whole[:half], whole[half:]


def half_columns(pair, count):
    first = lax.axis_index("fsdp") if pair else 0
    size = count // 2
    return [pl.ds(pl.multiple_of(place * size, 64), size) for place in (first, 1 - first)]


def spread_start(grad, kind=LOW):
    layers = lax.axis_size("fsdp")
    if layers != 2:
        return grad.astype(kind), None
    layer, half = lax.axis_index("fsdp"), grad.shape[0] // 2
    sent = lax.dynamic_slice_in_dim(grad, (1 - layer) * half, half, 0).astype(kind)
    return lax.dynamic_slice_in_dim(grad, layer * half, half, 0), sent


def spread_end(kept, sent):
    if sent is None:
        return lax.psum_scatter(kept, "fsdp", scatter_dimension=0, tiled=True).astype(F32)
    return kept + swap_layers(sent).astype(F32)


def spread_grad(grad, kind=LOW):
    return spread_end(*spread_start(grad, kind))


def gather_rows(block):
    return lax.all_gather(block, "seq", axis=0, tiled=True)


def scatter_rows(partial):
    return lax.psum_scatter(partial, "seq", scatter_dimension=0, tiled=True)


def ring_places(groups):
    ring = groups // 2
    me = lax.axis_index("seq")
    chip, core = me // 2, lax.rem(me, 2)
    odd = lax.rem(chip, 2)
    spot = (1 - odd) * (chip // 2) + odd * (ring - 1 - chip // 2)

    def chip_at(place):
        place = lax.rem(place + 2 * ring, ring)
        late = place // (ring // 2)
        return (1 - late) * (2 * place) + late * (2 * ring - 1 - 2 * place)

    def index_at(place, which):
        return 2 * chip_at(place) + which

    return spot, core, index_at


def enter(neighbours):
    barrier = pltpu.get_barrier_semaphore()
    for index in neighbours:
        pl.semaphore_signal(barrier, inc=1, device_id={"seq": index}, device_id_type=MESH)
    pl.semaphore_wait(barrier, len(neighbours))


class Gather:
    def __init__(self, groups, chunks, rows, source, out_ref, sems):
        self.groups, self.chunks, self.size = groups, chunks, rows // chunks
        self.source, self.out = source, out_ref
        self.send, self.recv, self.side_send, self.side_recv = sems
        self.spot, self.core, self.at = ring_places(groups)
        self.ring = groups // 2
        self.steps = groups // 4
        self.started = []

    def block(self, way, step):
        return self.at(self.spot - step if way == 0 else self.spot + step, self.core)

    def slice(self, ref, chunk):
        return ref.at[pl.ds(chunk * self.size, self.size)]

    def forward(self, step, chunk, way):
        index = self.block(way, step)
        own = self.slice(self.source if step == 0 else self.out.at[index], chunk)
        copy = pltpu.make_async_remote_copy(
            src_ref=own,
            dst_ref=self.slice(self.out.at[index], chunk),
            send_sem=self.send.at[way, step, chunk],
            recv_sem=self.recv.at[way, step, chunk],
            device_id={"seq": self.at(self.spot + (1 if way == 0 else -1), self.core)},
            device_id_type=MESH,
        )
        copy.start()
        self.started.append(copy)

    def arrived(self, step, chunk, way):
        index = self.block(way, step + 1)
        here = self.slice(self.out.at[index], chunk)
        pltpu.make_async_remote_copy(
            src_ref=here,
            dst_ref=here,
            send_sem=self.send.at[way, step, chunk],
            recv_sem=self.recv.at[way, step, chunk],
            device_id={"seq": self.at(self.spot, 1 - self.core)},
            device_id_type=MESH,
        ).wait_recv()

    def aside(self, distance, chunk):
        index = self.at(self.spot - distance, self.core)
        own = self.slice(self.source if distance == 0 else self.out.at[index], chunk)
        copy = pltpu.make_async_remote_copy(
            src_ref=own,
            dst_ref=self.slice(self.out.at[index], chunk),
            send_sem=self.side_send.at[distance, chunk],
            recv_sem=self.side_recv.at[distance, chunk],
            device_id={"seq": self.at(self.spot, 1 - self.core)},
            device_id_type=MESH,
        )
        copy.start()
        self.started.append(copy)

    def begin(self, chunk):
        for way in range(2):
            if self.steps > 1 or (chunk < self.chunks // 2) == (way == 0):
                self.forward(0, chunk, way)
        self.aside(0, chunk)

    def turn(self, step):
        last = self.steps - 1
        for chunk in range(self.chunks):
            for way in range(2):
                half = (chunk < self.chunks // 2) == (way == 0)
                if step == last and not half:
                    continue
                self.arrived(step, chunk, way)
                if step < last and (step + 1 < last or half):
                    self.forward(step + 1, chunk, way)
                self.aside(step + 1 if way == 0 else self.ring - 1 - step, chunk)

    def run(self):
        for step in range(self.steps):
            self.turn(step)

    def finish(self):
        for distance in range(self.ring):
            for chunk in range(self.chunks):
                here = self.slice(self.out.at[self.at(self.spot - distance, 1 - self.core)], chunk)
                pltpu.make_async_remote_copy(
                    src_ref=here,
                    dst_ref=here,
                    send_sem=self.side_send.at[distance, chunk],
                    recv_sem=self.side_recv.at[distance, chunk],
                    device_id={"seq": self.at(self.spot, 1 - self.core)},
                    device_id_type=MESH,
                ).wait_recv()
        for copy in self.started:
            copy.wait_send()


def gather_sems(groups, chunks):
    steps, ring = groups // 4, groups // 2
    return [
        pltpu.SemaphoreType.DMA((2, steps, chunks)),
        pltpu.SemaphoreType.DMA((2, steps, chunks)),
        pltpu.SemaphoreType.DMA((ring, chunks)),
        pltpu.SemaphoreType.DMA((ring, chunks)),
    ]


class Exchange:
    def __init__(self, groups, source, place_of, sems):
        self.groups, self.source, self.place_of = groups, source, place_of
        self.send, self.recv = sems
        self.me = lax.axis_index("seq")

    def copy(self, turn):
        other = lax.rem(self.me + turn, self.groups)
        return pltpu.make_async_remote_copy(
            src_ref=self.source.at[other],
            dst_ref=self.place_of(self.me),
            send_sem=self.send.at[turn],
            recv_sem=self.recv.at[turn],
            device_id={"seq": other},
            device_id_type=MESH,
        )

    def begin(self):
        for turn in range(1, self.groups):
            self.copy(turn).start()

    def arrived(self, turn):
        origin = lax.rem(self.me - turn + self.groups, self.groups)
        pltpu.make_async_remote_copy(
            src_ref=self.place_of(origin),
            dst_ref=self.place_of(origin),
            send_sem=self.send.at[turn],
            recv_sem=self.recv.at[turn],
            device_id={"seq": lax.rem(self.me + turn, self.groups)},
            device_id_type=MESH,
        ).wait_recv()
        return origin

    def finish(self):
        for turn in range(1, self.groups):
            self.copy(turn).wait_send()


def enter_all(groups, pair):
    barrier = pltpu.get_barrier_semaphore()
    me = lax.axis_index("seq")
    for turn in range(1, groups):
        pl.semaphore_signal(
            barrier, inc=1, device_id={"seq": lax.rem(me + turn, groups)}, device_id_type=MESH
        )
    if pair:
        other = {"fsdp": 1 - lax.axis_index("fsdp")}
        pl.semaphore_signal(barrier, inc=1, device_id=other, device_id_type=MESH)
    pl.semaphore_wait(barrier, groups if pair else groups - 1)


def across(source, target, send, recv):
    return pltpu.make_async_remote_copy(
        src_ref=source,
        dst_ref=target,
        send_sem=send,
        recv_sem=recv,
        device_id={"fsdp": 1 - lax.axis_index("fsdp")},
        device_id_type=MESH,
    )


def start_kernel(
    groups, chunks, pair, rows_ref, small_ref, heads_ref, *rest,
):
    if pair:
        bulk_ref, rows_out, small_out, heads_out, bulk_out, *rest = rest
    else:
        rows_out, small_out, heads_out, *rest = rest
    local_sems, small_y, head_sems, head_recv, head_y, head_y_recv, *sems = rest
    me, layer = lax.axis_index("seq"), lax.axis_index("fsdp")
    mine = layer if pair else 0
    rows = Gather(groups, chunks, rows_ref.shape[0], rows_ref, rows_out, sems[:4])
    spare = small_ref.shape[0]
    block = small_out.at[me]
    part = block.at[pl.ds(pl.multiple_of(mine * spare, spare), spare)]
    small = Gather(groups, chunks, small_out.shape[1], block, small_out, sems[4:])
    heads = Exchange(
        groups, heads_ref, lambda index: heads_out.at[index, mine], (head_sems, head_recv)
    )
    enter_all(groups, pair)
    locals_ = [
        pltpu.make_async_copy(small_ref, part, local_sems.at[0]),
        pltpu.make_async_copy(rows_ref, rows_out.at[me], local_sems.at[1]),
        pltpu.make_async_copy(heads_ref.at[me], heads_out.at[me, mine], local_sems.at[2]),
    ]
    for copy in locals_:
        copy.start()
    if pair:
        across(small_ref, part, small_y.at[0], small_y.at[1]).start()
    for chunk in range(chunks):
        rows.begin(chunk)
    heads.begin()
    if pair:
        across(heads_ref.at[me], heads_out.at[me, mine], head_y.at[0], head_y_recv.at[0]).start()
        theirs = block.at[pl.ds(pl.multiple_of((1 - mine) * spare, spare), spare)]
        across(theirs, theirs, small_y.at[0], small_y.at[1]).wait_recv()
        across(bulk_ref, bulk_out, small_y.at[2], small_y.at[3]).start()
    locals_[0].wait()
    for chunk in range(chunks):
        small.begin(chunk)
    for step in range(rows.steps):
        small.turn(step)
        rows.turn(step)
        if step == 0:
            for turn in range(1, groups):
                origin = heads.arrived(turn)
                if pair:
                    own = heads_out.at[origin, mine]
                    across(own, own, head_y.at[turn], head_y_recv.at[turn]).start()
    small.finish()
    rows.finish()
    heads.finish()
    for copy in locals_[1:]:
        copy.wait()
    if pair:
        across(small_ref, part, small_y.at[0], small_y.at[1]).wait_send()
        for turn in range(groups):
            origin = lax.rem(me - turn + groups, groups)
            theirs = heads_out.at[origin, 1 - mine]
            copy = across(theirs, theirs, head_y.at[turn], head_y_recv.at[turn])
            copy.wait_send()
            copy.wait_recv()
        copy = across(bulk_ref, bulk_out, small_y.at[2], small_y.at[3])
        copy.wait_send()
        copy.wait_recv()


def gather_start(rows, small, heads, bulk, groups, layers, collective_id, chunks=4):
    pair = layers == 2
    if not pair:
        small = lax.all_gather(small, "fsdp", axis=0, tiled=True)
    height = small.shape[0] * (2 if pair else 1)
    dma = pltpu.SemaphoreType.DMA
    any_spec = pl.BlockSpec(memory_space=pl.ANY)
    bulks = [bulk] if pair else []
    rows_out, small_out, heads_out, *bulk_out = pl.pallas_call(
        functools.partial(start_kernel, groups, chunks, pair),
        out_shape=[
            jax.ShapeDtypeStruct((groups,) + rows.shape, LOW),
            jax.ShapeDtypeStruct((groups, height, small.shape[1]), LOW),
            jax.ShapeDtypeStruct((groups, 2 if pair else 1) + heads.shape[1:], LOW),
        ]
        + [jax.ShapeDtypeStruct(array.shape, LOW) for array in bulks],
        in_specs=[any_spec] * (3 + len(bulks)),
        out_specs=[any_spec] * (3 + len(bulks)),
        scratch_shapes=[dma((3,)), dma((4,))]
        + [dma((groups,))] * 4
        + gather_sems(groups, chunks)
        + gather_sems(groups, chunks),
        compiler_params=pltpu.CompilerParams(collective_id=collective_id, has_side_effects=True),
        cost_estimate=pl.CostEstimate(flops=0, bytes_accessed=4 << 20, transcendentals=0),
    )(rows, small, heads, *bulks)
    if not pair:
        heads_out = lax.all_gather(heads_out, "fsdp", axis=1, tiled=True)
    return (
        rows_out.reshape(groups * rows.shape[0], rows.shape[1]),
        small_out.reshape(groups * height, small.shape[1]),
        heads_out,
        (bulk, bulk_out[0]) if pair else halves_over_layers(bulk),
    )


class HeadGrads:
    def __init__(self, groups, pair, grads_ref, out_ref, came, total, y_sems, send, recv, own_sem):
        self.pair, self.grads, self.out = pair, grads_ref, out_ref
        self.came, self.total, self.y_sems, self.own_sem = came, total, y_sems, own_sem
        self.mine = lax.axis_index("fsdp") if pair else 0
        self.groups = groups
        self.me = lax.axis_index("seq")
        self.spread = Exchange(groups, total, lambda index: out_ref.at[index], (send, recv))

    def cross(self):
        return across(self.grads.at[1 - self.mine], self.came, self.y_sems.at[0], self.y_sems.at[1])

    def begin(self):
        if self.pair:
            self.cross().start()

    def middle(self):
        if self.pair:
            self.cross().wait_recv()
            total = self.grads[self.mine].astype(F32) + self.came[...].astype(F32)
            self.total[...] = total.astype(LOW)
        else:
            self.total[...] = self.grads[0]
        self.spread.begin()
        self.local = pltpu.make_async_copy(
            self.total.at[self.me], self.out.at[self.me], self.own_sem
        )
        self.local.start()

    def finish(self):
        for turn in range(1, self.groups):
            self.spread.arrived(turn)
        self.spread.finish()
        self.local.wait()
        if self.pair:
            self.cross().wait_send()


def reduce_kernel(groups, chunks, extras, outs, rowfn, gathers, heads, *refs):
    parts_ref = refs[0]
    extra_refs = refs[1 : 1 + extras]
    if heads is not None:
        heads_ref, refs = refs[1 + extras], refs[: 1 + extras] + refs[2 + extras :]
    out_refs = refs[1 + extras : 1 + extras + outs]
    rest = list(refs[1 + extras + outs :])
    if heads is not None:
        head_out = rest.pop(0)
    gather_ref = rest.pop(0) if gathers else None
    own, side, came, sent = rest[:4]
    own_sem, side_send, side_recv, send_sem, recv_sem = rest[4:9]
    ready = rest[9] if gathers else None
    rows = own.shape[1]
    size = rows // chunks
    ring, steps = groups // 2, groups // 4
    spot, core, at = ring_places(groups)
    sibling = {"seq": at(spot, 1 - core)}
    if heads is None:
        enter((at(spot - 1, core), at(spot + 1, core), at(spot, 1 - core)))
    else:
        head_grads = HeadGrads(groups, heads, heads_ref, head_out, *rest[-6:])
        enter_all(groups, heads)
        head_grads.begin()

    order = []
    for step in range(steps):
        order.append(steps - step)
        if step:
            order.append(ring - steps + step)
    order.append(0)
    started = []
    loads = {}
    for far in order:
        copy = pltpu.make_async_remote_copy(
            src_ref=parts_ref.at[at(spot + far, 1 - core)],
            dst_ref=side.at[far],
            send_sem=side_send.at[far],
            recv_sem=side_recv.at[far],
            device_id=sibling,
            device_id_type=MESH,
        )
        copy.start()
        started.append(copy)
        load = pltpu.make_async_copy(
            parts_ref.at[at(spot + far, core)], own.at[far], own_sem.at[far]
        )
        load.start()
        loads[far] = (load, copy)

    here = set()

    def both(far, chunk):
        if far not in here:
            here.add(far)
            loads[far][0].wait()
            loads[far][1].wait_recv()
        part = pl.ds(chunk * size, size)
        return own[far, part].astype(F32) + side[far, part].astype(F32)

    def neighbour_copy(way, step, chunk):
        part = pl.ds(chunk * size, size)
        return pltpu.make_async_remote_copy(
            src_ref=sent.at[way, step, part],
            dst_ref=came.at[way, step, part],
            send_sem=send_sem.at[way, step, chunk],
            recv_sem=recv_sem.at[way, step, chunk],
            device_id={"seq": at(spot + (1 if way == 0 else -1), core)},
            device_id_type=MESH,
        )

    def half(way, chunk):
        return (chunk < chunks // 2) == (way == 0)

    for step in range(steps):
        for chunk in range(chunks):
            for way in range(2):
                if step == 0 and not half(way, chunk):
                    continue
                far = steps - step if way == 0 else ring - (steps - step)
                part = pl.ds(chunk * size, size)
                total = both(far, chunk)
                if step > 1 or (step == 1 and half(way, chunk)):
                    neighbour_copy(way, step - 1, chunk).wait_recv()
                    total = total + came[way, step - 1, part].astype(F32)
                sent[way, step, part] = total.astype(sent.dtype)
                copy = neighbour_copy(way, step, chunk)
                copy.start()
                started.append(copy)
    if heads is not None:
        head_grads.middle()
    gather = Gather(groups, chunks, rows, ready, gather_ref, rest[10:14]) if gathers else None
    for chunk in range(chunks):
        part = pl.ds(chunk * size, size)
        total = both(0, chunk)
        for way in range(2):
            if steps > 1 or half(way, chunk):
                neighbour_copy(way, steps - 1, chunk).wait_recv()
                total = total + came[way, steps - 1, part].astype(F32)
        made = rowfn(total, part, extra_refs, out_refs)
        if gathers:
            ready[part] = made
            gather.begin(chunk)
    if gathers:
        local = pltpu.make_async_copy(ready, gather_ref.at[at(spot, core)], rest[14])
        local.start()
        gather.run()
        gather.finish()
        local.wait()
    if heads is not None:
        head_grads.finish()
    for copy in started:
        copy.wait_send()


def ring_reduce(
    parts, extras, outs, rowfn, groups, collective_id, gathers=None, heads=None, chunks=4
):
    _, rows, columns = parts.shape
    ring, steps = groups // 2, groups // 4
    scratch = [
        pltpu.VMEM((ring, rows, columns), LOW),
        pltpu.VMEM((ring, rows, columns), LOW),
        pltpu.VMEM((2, steps, rows, columns), LOW),
        pltpu.VMEM((2, steps, rows, columns), LOW),
        pltpu.SemaphoreType.DMA((ring,)),
        pltpu.SemaphoreType.DMA((ring,)),
        pltpu.SemaphoreType.DMA((ring,)),
        pltpu.SemaphoreType.DMA((2, steps, chunks)),
        pltpu.SemaphoreType.DMA((2, steps, chunks)),
    ]
    shapes = list(outs)
    specs = [pl.BlockSpec(memory_space=pltpu.VMEM)] * len(outs)
    extras = list(extras)
    count = len(extras)
    pair = None
    if heads is not None:
        pair = heads.shape[0] == 2
        extras.append(heads)
        shapes.append(jax.ShapeDtypeStruct(heads.shape[1:], LOW))
        specs.append(pl.BlockSpec(memory_space=pltpu.VMEM))
    if gathers is not None:
        shapes.append(jax.ShapeDtypeStruct((groups, rows, gathers), LOW))
        specs.append(pl.BlockSpec(memory_space=pl.ANY))
        scratch.append(pltpu.VMEM((rows, gathers), LOW))
        scratch += gather_sems(groups, chunks)
        scratch.append(pltpu.SemaphoreType.DMA)
    if heads is not None:
        scratch += [pltpu.VMEM(heads.shape[1:], LOW)] * 2
        scratch += [pltpu.SemaphoreType.DMA((2,))]
        scratch += [pltpu.SemaphoreType.DMA((groups,))] * 2
        scratch += [pltpu.SemaphoreType.DMA]
    return pl.pallas_call(
        functools.partial(
            reduce_kernel, groups, chunks, count, len(outs), rowfn, gathers is not None, pair
        ),
        out_shape=shapes,
        in_specs=[pl.BlockSpec(memory_space=pl.ANY)]
        + [pl.BlockSpec(memory_space=pltpu.VMEM)] * len(extras),
        out_specs=specs,
        scratch_shapes=scratch,
        compiler_params=pltpu.CompilerParams(
            collective_id=collective_id, has_side_effects=True, vmem_limit_bytes=50 << 20
        ),
        cost_estimate=pl.CostEstimate(
            flops=0, bytes_accessed=4 << 20, transcendentals=0
        ),
    )(parts, *extras)


def attend_kernel(blocks, q_ref, k_ref, v_ref, col_ref, row_ref, out_ref, log_ref):
    size = q_ref.shape[0] // blocks
    scale = (NOPE + ROPE) ** (-0.5)
    for index in range(blocks):
        part = pl.ds(index * size, size)
        reach = (index + 1) * size
        scores = dot_t(q_ref[part], k_ref[:reach]) * scale
        rows = index * size + lax.broadcasted_iota(jnp.int32, (size, reach), 0)
        columns = lax.broadcasted_iota(jnp.int32, (size, reach), 1)
        allowed = (col_ref[part] == row_ref[:, :reach]) & (rows >= columns)
        scores = jnp.where(allowed, scores, -1e30)
        peak = jnp.max(scores, axis=-1, keepdims=True)
        raised = jnp.exp(scores - peak)
        total = jnp.sum(raised, axis=-1, keepdims=True)
        weights = (raised * (1.0 / total)).astype(LOW)
        out_ref[part] = dot(weights, v_ref[:reach]).astype(LOW)
        log_ref[part] = peak + jnp.log(total)


def attend_forward(head_q, head_k, head_v, doc_ids):
    seq_len = head_q.shape[0]
    return pl.pallas_call(
        functools.partial(attend_kernel, seq_len // 256),
        out_shape=[
            jax.ShapeDtypeStruct((seq_len, VD), LOW),
            jax.ShapeDtypeStruct((seq_len, 1), F32),
        ],
        compiler_params=pltpu.CompilerParams(vmem_limit_bytes=50 << 20),
        cost_estimate=pl.CostEstimate(
            flops=seq_len * seq_len * 400, bytes_accessed=4 << 20, transcendentals=seq_len * seq_len // 2
        ),
    )(head_q, head_k, head_v, doc_ids[:, None], doc_ids[None, :])


def attend_back_kernel(
    blocks, q_ref, k_ref, v_ref, g_ref, col_ref, row_ref, log_ref, dq_ref, dk_ref, dv_ref, ksum, vsum
):
    size = q_ref.shape[0] // blocks
    scale = (NOPE + ROPE) ** (-0.5)
    ksum[...] = jnp.zeros_like(ksum)
    vsum[...] = jnp.zeros_like(vsum)
    for index in range(blocks):
        part = pl.ds(index * size, size)
        reach = (index + 1) * size
        query, grad = q_ref[part], g_ref[part]
        scores = dot_t(k_ref[:reach], query) * scale
        keys = lax.broadcasted_iota(jnp.int32, (reach, size), 0)
        rows = index * size + lax.broadcasted_iota(jnp.int32, (reach, size), 1)
        allowed = (col_ref[:reach] == row_ref[:, part]) & (rows >= keys)
        weights = jnp.exp(jnp.where(allowed, scores, -1e30) - log_ref[:, part])
        vsum[:reach] += dot(weights.astype(LOW), grad)
        slopes = dot_t(v_ref[:reach], grad)
        inner = jnp.sum(weights * slopes, axis=0, keepdims=True)
        back = (weights * (slopes - inner)).astype(LOW)
        ksum[:reach] += dot(back, query)
        dq_ref[part] = (t_dot(back, k_ref[:reach]) * scale).astype(LOW)
    dk_ref[...] = (ksum[...] * scale).astype(LOW)
    dv_ref[...] = vsum[...].astype(LOW)


def attend_backward(head_q, head_k, head_v, doc_ids, logs, head_g):
    seq_len = head_q.shape[0]
    return pl.pallas_call(
        functools.partial(attend_back_kernel, seq_len // 256),
        out_shape=[
            jax.ShapeDtypeStruct((seq_len, NOPE + ROPE), LOW),
            jax.ShapeDtypeStruct((seq_len, NOPE + ROPE), LOW),
            jax.ShapeDtypeStruct((seq_len, VD), LOW),
        ],
        scratch_shapes=[
            pltpu.VMEM((seq_len, NOPE + ROPE), F32),
            pltpu.VMEM((seq_len, VD), F32),
        ],
        compiler_params=pltpu.CompilerParams(vmem_limit_bytes=56 << 20),
        cost_estimate=pl.CostEstimate(
            flops=seq_len * seq_len * 1000, bytes_accessed=6 << 20, transcendentals=seq_len * seq_len // 2
        ),
    )(head_q, head_k, head_v, head_g, doc_ids[:, None], doc_ids[None, :], logs.reshape(1, seq_len))


def swapped(values):
    half = values.shape[-1] // 2
    return jnp.concatenate([values[:, half:], values[:, :half]], axis=-1)


def project_kernel(
    x_ref, gain_ref, wq_ref, wl_ref, gain_lat_ref, we_ref, table_ref,
    one_ref, q_ref, k_ref, v_ref, m_ref, c_ref,
):
    one = norm_forward(x_ref[...].astype(F32), gain_ref[...])[0].astype(LOW)
    one_ref[...] = one
    cosine, sine = table_ref[:, :ROPE], table_ref[:, ROPE:]
    query = dot(one, wq_ref[...])
    turned = query[:, NOPE:]
    q_ref[:, :NOPE] = query[:, :NOPE].astype(LOW)
    q_ref[:, NOPE:] = (turned * cosine + swapped(turned) * sine).astype(LOW)
    latent = dot(one, wl_ref[...])
    turned = latent[:, LAT : LAT + ROPE]
    k_ref[:, NOPE:] = (turned * cosine + swapped(turned) * sine).astype(LOW)
    c_ref[...] = latent[:, :LAT]
    scaled = norm_forward(latent[:, :LAT], gain_lat_ref[...])[0].astype(LOW)
    m_ref[...] = scaled
    expanded = dot(scaled, we_ref[...])
    k_ref[:, :NOPE] = expanded[:, :NOPE].astype(LOW)
    v_ref[...] = expanded[:, NOPE:].astype(LOW)


def project(rows, gain, query_w, small, gain_latent, expand_w, table, tile=256):
    seq_len, width = rows.shape

    def cut(columns):
        return pl.BlockSpec((tile, columns), lambda i: (i, 0))

    def whole(array):
        return pl.BlockSpec(array.shape, lambda i: (0, 0))

    outs = [(width, LOW), (NOPE + ROPE, LOW), (NOPE + ROPE, LOW), (VD, LOW), (LAT, LOW), (LAT, F32)]
    return pl.pallas_call(
        project_kernel,
        grid=(seq_len // tile,),
        out_shape=[jax.ShapeDtypeStruct((seq_len, c), t) for c, t in outs],
        in_specs=[
            cut(width), whole(gain), whole(query_w), whole(small), whole(gain_latent),
            whole(expand_w), cut(2 * ROPE),
        ],
        out_specs=[cut(c) for c, _ in outs],
        compiler_params=pltpu.CompilerParams(vmem_limit_bytes=50 << 20),
        cost_estimate=pl.CostEstimate(
            flops=seq_len * width * 1800, bytes_accessed=28 << 20, transcendentals=0
        ),
    )(rows, gain, query_w, small, gain_latent, expand_w, table)


def project_back_kernel(
    dq_ref, dk_ref, dv_ref, table_ref, one_ref, m_ref, wq_ref, we_ref,
    parts_ref, gq_ref, ge_ref, dq_low, de_low,
):
    cosine, sine = table_ref[:, :ROPE], table_ref[:, ROPE:]
    turned = dq_ref[:, NOPE:].astype(F32)
    dq_low[:, :NOPE] = dq_ref[:, :NOPE]
    dq_low[:, NOPE:] = (turned * cosine - swapped(turned) * sine).astype(LOW)
    de_low[:, :NOPE] = dk_ref[:, :NOPE]
    de_low[:, NOPE:] = dv_ref[...]
    blocks, rows, wide = parts_ref.shape
    width, last = one_ref.shape[1], LAT + ROPE
    parts_ref[:, :, :width] = dot_t(dq_low[...], wq_ref[...]).astype(LOW).reshape(blocks, rows, width)
    parts_ref[:, :, width : width + LAT] = (
        dot_t(de_low[...], we_ref[...]).astype(LOW).reshape(blocks, rows, LAT)
    )
    parts_ref[:, :, width + LAT : width + last] = dk_ref[:, NOPE:].reshape(blocks, rows, ROPE)
    parts_ref[:, :, width + last :] = jnp.zeros((blocks, rows, wide - width - last), LOW)

    @pl.when(pl.program_id(0) == 0)
    def _():
        gq_ref[...] = jnp.zeros_like(gq_ref)
        ge_ref[...] = jnp.zeros_like(ge_ref)

    gq_ref[...] += t_dot(one_ref[...], dq_low[...])
    ge_ref[...] += t_dot(m_ref[...], de_low[...])


def project_back(grads, table, one_low, latent_low, query_w, expand_w, tok_rows, tile=256):
    seq_len, width = one_low.shape
    wide = width + LAT + 2 * ROPE

    def cut(columns):
        return pl.BlockSpec((tile, columns), lambda i: (i, 0))

    def whole(shape):
        return pl.BlockSpec(shape, lambda i: (0, 0))

    return pl.pallas_call(
        project_back_kernel,
        grid=(seq_len // tile,),
        out_shape=[
            jax.ShapeDtypeStruct((seq_len // tok_rows, tok_rows, wide), LOW),
            jax.ShapeDtypeStruct(query_w.shape, F32),
            jax.ShapeDtypeStruct(expand_w.shape, F32),
        ],
        in_specs=[
            cut(NOPE + ROPE), cut(NOPE + ROPE), cut(VD), cut(2 * ROPE), cut(width), cut(LAT),
            whole(query_w.shape), whole(expand_w.shape),
        ],
        out_specs=[
            pl.BlockSpec((tile // tok_rows, tok_rows, wide), lambda i: (i, 0, 0)),
            whole(query_w.shape),
            whole(expand_w.shape),
        ],
        scratch_shapes=[pltpu.VMEM((tile, NOPE + ROPE), LOW), pltpu.VMEM((tile, NOPE + VD), LOW)],
        compiler_params=pltpu.CompilerParams(vmem_limit_bytes=50 << 20),
        cost_estimate=pl.CostEstimate(
            flops=seq_len * width * 1300, bytes_accessed=28 << 20, transcendentals=0
        ),
    )(*grads, table, one_low, latent_low, query_w, expand_w)


def blocks_of(ref, count):
    size = ref.shape[0] // count
    return [pl.ds(block * size, size) for block in range(count)]


def two_parts(values):
    high = values.astype(LOW)
    return high, (values - high.astype(F32)).astype(LOW)


def join_halves(pair, own_ref, other_ref, whole_ref):
    @pl.when(pl.program_id(0) == 0)
    def _():
        own, other = half_columns(pair, whole_ref.shape[0])
        whole_ref[own] = own_ref[...]
        whole_ref[other] = other_ref[...]


def ffn_kernel(
    pair, rows_ref, chosen_ref, mine_ref, router_ref, wg_own, wg_other, wu_own, wu_other,
    wd_own, wd_other, wi_ref, wo_ref,
    probs_ref, slot_gate_ref, in_ref, gate_ref, up_ref, inner_ref, made_ref, proj_ref, hs_ref, out_ref,
    spread, wd_ref,
):
    count = 4
    width = rows_ref.shape[1]
    join_halves(pair, wd_own, wd_other, wd_ref)
    tokens, slots = blocks_of(rows_ref, count), blocks_of(chosen_ref, count)
    lanes = lax.broadcasted_iota(jnp.int32, mine_ref.shape, 1)
    logits = jnp.where(mine_ref[1:2] > 0, dot(rows_ref[...], router_ref[...]), -1e30)
    raised = jnp.exp(logits - jnp.max(logits, axis=-1, keepdims=True))
    probs = raised / jnp.sum(raised, axis=-1, keepdims=True)
    probs_ref[...] = probs
    high, rest = two_parts(jnp.sum(probs * mine_ref[0:1], axis=-1, keepdims=True))
    high, rest = high.astype(F32), rest.astype(F32)
    columns = jnp.where(lanes[0:1] == 0, high, jnp.where(lanes[0:1] == 1, rest, 0.0)).astype(LOW)
    for token, slot in zip(tokens, slots):
        size = token.size
        picked = columns[token.start : token.start + size]
        chosen = chosen_ref[slot]
        slot_gate_ref[slot] = jnp.sum(dot(chosen, picked), axis=-1, keepdims=True)
        in_ref[slot] = dot(chosen, rows_ref[token]).astype(LOW)
    own, other = half_columns(pair, width)
    gate = dot(in_ref[:, own], wg_own[...]) + dot(in_ref[:, other], wg_other[...])
    up = dot(in_ref[:, own], wu_own[...]) + dot(in_ref[:, other], wu_other[...])
    gate_ref[...] = gate
    up_ref[...] = up
    inner_ref[...] = (gate * jax.nn.sigmoid(gate) * up).astype(LOW)
    made = dot(inner_ref[...], wd_ref[...]).astype(LOW)
    made_ref[...] = made
    spread[...] = (slot_gate_ref[...] * made.astype(F32)).astype(LOW)
    proj = dot(rows_ref[...], wi_ref[...])
    proj_ref[...] = proj
    half = proj.shape[1] // 2
    gate, up = proj[:, :half], proj[:, half:]
    hs_ref[...] = (gate * jax.nn.sigmoid(gate) * up).astype(LOW)
    for token, slot in zip(tokens, slots):
        total = t_dot(chosen_ref[slot], spread[slot]) + dot(hs_ref[token], wo_ref[...])
        out_ref[token] = total.astype(LOW)


def ffn_back_kernel(
    pair, grads_ref, chosen_ref, mine_ref, slot_gate_ref, made_ref, gate_ref, up_ref, proj_ref,
    wg_own, wg_other, wu_own, wu_other, wd_own, wd_other, wi_ref, wo_ref,
    dy_ref, dgate_ref, dup_ref, dproj_ref, parts_ref, spread, wd_ref,
):
    count = 4
    width = grads_ref.shape[1]
    join_halves(pair, wd_own, wd_other, wd_ref)
    tokens, slots = blocks_of(grads_ref, count), blocks_of(chosen_ref, count)
    mine, shifted = mine_ref[0:1], mine_ref[2:3]
    for token, slot in zip(tokens, slots):
        picked = dot(chosen_ref[slot], grads_ref[token])
        dy_ref[slot] = (slot_gate_ref[slot] * picked).astype(LOW)
        score = jnp.sum(picked * made_ref[slot].astype(F32), axis=-1, keepdims=True)
        high, rest = two_parts(score)
        spread[slot, width:] = (high.astype(F32) * mine + rest.astype(F32) * shifted).astype(LOW)
    inner = dot_t(dy_ref[...], wd_ref[...])
    gate = gate_ref[...]
    sigmoid = jax.nn.sigmoid(gate)
    dgate_ref[...] = (inner * up_ref[...] * swish_slope(gate, sigmoid)).astype(LOW)
    dup_ref[...] = (inner * gate * sigmoid).astype(LOW)
    own, other = half_columns(pair, width)
    back = dot_t(dgate_ref[...], wg_own[...]) + dot_t(dup_ref[...], wu_own[...])
    spread[:, own] = back.astype(LOW)
    back = dot_t(dgate_ref[...], wg_other[...]) + dot_t(dup_ref[...], wu_other[...])
    spread[:, other] = back.astype(LOW)
    half = proj_ref.shape[1] // 2
    gate, up = proj_ref[:, :half], proj_ref[:, half:]
    sigmoid = jax.nn.sigmoid(gate)
    inner = dot_t(grads_ref[...], wo_ref[...])
    dproj_ref[:, :half] = (inner * up * swish_slope(gate, sigmoid)).astype(LOW)
    dproj_ref[:, half:] = (inner * gate * sigmoid).astype(LOW)
    for block, (token, slot) in enumerate(zip(tokens, slots)):
        total = t_dot(chosen_ref[slot], spread[slot])
        parts_ref[block, :, :width] = (
            total[:, :width] + dot_t(dproj_ref[token], wi_ref[...])
        ).astype(LOW)
        parts_ref[block, :, width:] = total[:, width:].astype(LOW)


def row_grid(kernel, steps, cuts, outs, scratch, flops):
    def cut(shape):
        rest = (0,) * (len(shape) - 1)
        return pl.BlockSpec((shape[0] // steps,) + tuple(shape[1:]), lambda i: (i,) + rest)

    def whole(shape):
        rest = (0,) * len(shape)
        return pl.BlockSpec(tuple(shape), lambda i: rest, pipeline_mode=pl.Buffered(1))

    operands = [array for array, _ in cuts]
    return pl.pallas_call(
        kernel,
        grid=(steps,),
        out_shape=outs,
        in_specs=[whole(a.shape) if fixed else cut(a.shape) for a, fixed in cuts],
        out_specs=[cut(o.shape) for o in outs],
        scratch_shapes=scratch,
        compiler_params=pltpu.CompilerParams(vmem_limit_bytes=60 << 20),
        cost_estimate=pl.CostEstimate(flops=flops, bytes_accessed=60 << 20, transcendentals=0),
    )(*operands)


def grad_in_kernel(layer_ref, rows_ref, grads_ref, sent_ref, kept_ref):
    made = t_dot(rows_ref[...], grads_ref[...])
    step, half = pl.program_id(0), pl.num_programs(0) // 2

    @pl.when(step < half)
    def _():
        sent_ref[...] = made.astype(LOW)

    @pl.when(step >= half)
    def _():
        kept_ref[...] = made


def grad_in(rows, grads, tile=512):
    count, width = rows.shape
    columns = grads.shape[1]
    half = width // 2 // tile
    layer = lax.axis_index("fsdp").reshape(1)

    def source(i, layer_ref):
        return (0, lax.rem(i + (1 - layer_ref[0]) * half, 2 * half))

    return pl.pallas_call(
        grad_in_kernel,
        grid_spec=pltpu.PrefetchScalarGridSpec(
            num_scalar_prefetch=1,
            grid=(2 * half,),
            in_specs=[
                pl.BlockSpec((count, tile), source),
                pl.BlockSpec((count, columns), lambda i, _: (0, 0)),
            ],
            out_specs=[
                pl.BlockSpec((tile, columns), lambda i, _: (jnp.minimum(i, half - 1), 0)),
                pl.BlockSpec((tile, columns), lambda i, _: (jnp.maximum(i - half, 0), 0)),
            ],
        ),
        out_shape=[
            jax.ShapeDtypeStruct((width // 2, columns), LOW),
            jax.ShapeDtypeStruct((width // 2, columns), F32),
        ],
        compiler_params=pltpu.CompilerParams(vmem_limit_bytes=50 << 20),
        cost_estimate=pl.CostEstimate(
            flops=2 * count * width * columns, bytes_accessed=16 << 20, transcendentals=0
        ),
    )(layer, rows, grads)


def grad_out_kernel(layer_ref, inner_ref, grads_ref, sent_ref, kept_ref, made):
    half = sent_ref.shape[0]
    layer = layer_ref[0]
    made[...] = t_dot(inner_ref[...], grads_ref[...])
    sent_ref[...] = made[pl.ds(pl.multiple_of((1 - layer) * half, 8), half)].astype(LOW)
    kept_ref[...] = made[pl.ds(pl.multiple_of(layer * half, 8), half)]


def grad_out(inner, grads, tile=512):
    count, units = inner.shape
    width = grads.shape[1]
    layer = lax.axis_index("fsdp").reshape(1)
    return pl.pallas_call(
        grad_out_kernel,
        grid_spec=pltpu.PrefetchScalarGridSpec(
            num_scalar_prefetch=1,
            grid=(width // tile,),
            in_specs=[
                pl.BlockSpec((count, units), lambda i, _: (0, 0)),
                pl.BlockSpec((count, tile), lambda i, _: (0, i)),
            ],
            out_specs=[
                pl.BlockSpec((units // 2, tile), lambda i, _: (0, i)),
                pl.BlockSpec((units // 2, tile), lambda i, _: (0, i)),
            ],
            scratch_shapes=[pltpu.VMEM((units, tile), F32)],
        ),
        out_shape=[
            jax.ShapeDtypeStruct((units // 2, width), LOW),
            jax.ShapeDtypeStruct((units // 2, width), F32),
        ],
        compiler_params=pltpu.CompilerParams(vmem_limit_bytes=50 << 20),
        cost_estimate=pl.CostEstimate(
            flops=2 * count * width * units, bytes_accessed=16 << 20, transcendentals=0
        ),
    )(layer, inner, grads)


def body(
    tokens,
    cotangent,
    segments,
    routes,
    norm_attn,
    w_query,
    w_latent,
    norm_latent,
    w_expand,
    w_output,
    norm_ffn,
    w_router,
    w_shared_gate,
    w_shared_up,
    w_shared_down,
    w_expert_gate,
    w_expert_up,
    w_expert_down,
):
    groups = lax.axis_size("seq")
    layers = lax.axis_size("fsdp")
    both = ("seq", "fsdp")
    place = lax.axis_index("seq")
    tok_rows, width = tokens.shape[1], tokens.shape[2]
    seq_len = segments.shape[1]
    own_rows = w_query.shape[0]
    lat_rows = w_expand.shape[0]
    experts = w_router.shape[1]
    capacity = tok_rows // 2
    query_width = NOPE + ROPE
    hidden_own = tokens[0].astype(F32)
    grad_own = cotangent[0].astype(F32)
    doc_ids = segments[0]

    lat_column = jnp.pad(norm_latent[:, None], ((0, own_rows - lat_rows), (0, 0)))
    at = LAT + ROPE
    route_columns = routes.reshape(own_rows, tok_rows * TOP // own_rows).astype(F32)
    packed = [w_latent, w_router, norm_attn[:, None], norm_ffn[:, None], lat_column, route_columns]
    packed = jnp.concatenate(packed, axis=1).astype(LOW)
    used = packed.shape[1]
    last = at + experts
    packed = jnp.pad(packed, ((0, 0), (0, -used % 128)))

    fold = lat_rows * (NOPE + VD) // own_rows
    query_parts = w_query.astype(LOW).reshape(own_rows, H, query_width).transpose(1, 0, 2)
    expand_parts = (
        w_expand.astype(LOW)
        .reshape(lat_rows, H, NOPE + VD)
        .transpose(1, 0, 2)
        .reshape(H, own_rows, fold)
    )
    head_parts = jnp.concatenate([query_parts, expand_parts], axis=2)
    hidden_low, small, head_parts, expert_gate_w = gather_start(
        tokens[0], packed, head_parts, w_expert_gate[0].astype(LOW), groups, layers, 1
    )
    query_w = head_parts[..., :query_width].reshape(width, query_width)
    expand_w = head_parts[..., query_width:].reshape(LAT, NOPE + VD)
    router_w = jnp.pad(small[:, at:last], ((0, 0), (0, 128 - experts)))
    all_routes = small[:, last + 3 : used].reshape(groups, layers, -1)
    all_routes = lax.dynamic_index_in_dim(all_routes, lax.axis_index("fsdp"), 1, keepdims=False)
    all_routes = all_routes.reshape(groups, tok_rows, TOP)
    gains = small[:, last : last + 3].astype(F32).T
    gain_attn, gain_ffn = gains[0:1], gains[1:2]
    gain_latent = gains[2].reshape(groups * layers, own_rows)[:, :lat_rows].reshape(1, LAT)

    units = w_shared_gate.shape[1]
    padding = -units % 128
    spare = ((0, 0), (0, padding))
    shared_in = jnp.concatenate([jnp.pad(w_shared_gate, spare), jnp.pad(w_shared_up, spare)], axis=1)
    shared_in = shared_in.astype(LOW)
    shared_in = after(shared_in, hidden_low)
    down_low, output_low = w_shared_down.astype(LOW), w_output.astype(LOW)
    if layers == 2:
        lone = jnp.concatenate([shared_in, narrow(down_low), narrow(output_low)])
        pair_of = swap_layers(lone)
        cut = shared_in.shape[0]
        end = cut + narrow(down_low).shape[0]
        shared_in_w = layers_in_order(shared_in, pair_of[:cut])
        shared_down_w = layers_in_order(down_low, widen(pair_of[cut:end], width))
        output_w = layers_in_order(output_low, widen(pair_of[end:], width))
    else:
        shared_in_w = whole_over_layers(shared_in)
        shared_down_w = whole_over_layers(down_low)
        output_w = whole_over_layers(output_low)
    shared_down_w = jnp.pad(shared_down_w, ((0, padding), (0, 0)))

    expert_up_w = halves_over_layers(after(w_expert_up[0].astype(LOW), hidden_low))
    expert_down_w = halves_over_layers(after(w_expert_down[0].astype(LOW), hidden_low))
    grad_low = gather_rows(after(cotangent[0], hidden_low))

    table = jnp.asarray(rotary_table(seq_len))
    one_low, head_q, head_k, head_v, latent_low, latent_proj = project(
        hidden_low, gain_attn, query_w, small, gain_latent, expand_w, table
    )
    head_out, logs = attend_forward(head_q, head_k, head_v, doc_ids)
    part_residual = dot(head_out, output_w).astype(LOW).reshape(groups, tok_rows, width)

    def make_two(total, part, extras, outs):
        row_sum = extras[0][part].astype(F32) + total
        outs[0][part] = row_sum
        return norm_forward(row_sum, extras[1][...])[0].astype(LOW)

    own_shape = jax.ShapeDtypeStruct((tok_rows, width), F32)
    residual, two_low = ring_reduce(
        part_residual, [tokens[0], gain_ffn], [own_shape], make_two, groups, 2, width
    )
    two_low = after(two_low, grad_low).reshape(seq_len, width)

    named = jnp.any(all_routes == place.astype(LOW), axis=-1)
    rank = jnp.cumsum(named.astype(jnp.int32), axis=1) - 1
    slots = jnp.arange(capacity, dtype=jnp.int32)
    chosen = named[:, None, :] & (rank[:, None, :] == slots[None, :, None])
    chosen = chosen.astype(LOW).reshape(groups * capacity, tok_rows)
    lanes = jnp.arange(128, dtype=jnp.int32)
    mine = jnp.stack(
        [(lanes == place), (lanes < experts), (lanes == place + experts)] + [lanes < 0] * 5
    ).astype(F32)
    slot_count, unit_count = groups * capacity, w_expert_gate.shape[2]
    expert_w = [(half, True) for half in expert_gate_w + expert_up_w + expert_down_w]
    columns = shared_in_w.shape[1]

    def array(rows, columns, kind=LOW):
        return jax.ShapeDtypeStruct((rows, columns), kind)

    steps = groups // 4
    routed_flops = 6 * slot_count * width * unit_count
    probs, slot_gate, expert_in, gate_proj, up_proj, inner_low, made, shared_proj, shared_low, part_out = row_grid(
        functools.partial(ffn_kernel, layers == 2),
        steps,
        [
            (two_low, False), (chosen, False), (mine, True), (router_w, True),
            *expert_w, (shared_in_w, True), (shared_down_w, True),
        ],
        [
            array(seq_len, 128, F32), array(slot_count, 1, F32), array(slot_count, width),
            array(slot_count, unit_count, F32), array(slot_count, unit_count, F32),
            array(slot_count, unit_count), array(slot_count, width), array(seq_len, columns, F32),
            array(seq_len, columns // 2), array(seq_len, width),
        ],
        [pltpu.VMEM((slot_count // steps, width), LOW), pltpu.VMEM((unit_count, width), LOW)],
        routed_flops * 3 // 2,
    )
    ffn_out = scatter_rows(part_out).astype(F32)
    output = (residual + ffn_out).astype(LOW)

    made_grad, gate_grad, up_grad, shared_grads, part_grad = row_grid(
        functools.partial(ffn_back_kernel, layers == 2),
        steps,
        [
            (grad_low, False), (chosen, False), (mine, True), (slot_gate, False), (made, False),
            (gate_proj, False), (up_proj, False), (shared_proj, False),
            *expert_w, (shared_in_w, True), (shared_down_w, True),
        ],
        [
            array(slot_count, width), array(slot_count, unit_count), array(slot_count, unit_count),
            array(seq_len, columns),
            jax.ShapeDtypeStruct((groups, tok_rows, width + 128), LOW),
        ],
        [pltpu.VMEM((slot_count // steps, width + 128), LOW), pltpu.VMEM((unit_count, width), LOW)],
        routed_flops * 3 // 2,
    )

    if layers == 2:
        down_sent, down_kept = grad_out(inner_low, made_grad)
        gate_sent, gate_kept = grad_in(expert_in, gate_grad)
        up_sent, up_kept = grad_in(expert_in, up_grad)
        part_grad = after(part_grad, down_sent, gate_sent, up_sent)
    else:
        down_kept, down_sent = spread_start(t_dot(inner_low, made_grad))
        gate_kept, gate_sent = spread_start(t_dot(expert_in, gate_grad))
        up_kept, up_sent = spread_start(t_dot(expert_in, up_grad))
    grad_expert_down = spread_end(down_kept, down_sent)
    grad_expert_gate = spread_end(gate_kept, gate_sent)
    grad_expert_up = spread_end(up_kept, up_sent)
    shared_in_kept, shared_in_sent = spread_start(t_dot(two_low, shared_grads))
    shared_down_kept, shared_down_sent = spread_start(t_dot(shared_low, grad_low)[:units])

    own_probs = lax.dynamic_slice_in_dim(probs, place * tok_rows, tok_rows, 0)

    def make_attn(total, part, extras, outs):
        probs = extras[0][part]
        score = total[:, width:]
        score = score + jnp.concatenate([score[:, experts:], score[:, :experts]], axis=1)
        logit = probs * (score - jnp.sum(probs * score, axis=-1, keepdims=True))
        high, rest = two_parts(logit)
        grad = total[:, :width] + dot_t(high, extras[4][...]) + dot_t(rest, extras[4][...])
        gain = extras[1][...]
        _, normed, factor = norm_forward(extras[2][part], gain)
        inner = grad * gain
        back = factor * (inner - normed * jnp.mean(inner * normed, axis=-1, keepdims=True))
        back = extras[3][part].astype(F32) + back
        outs[0][part] = back
        outs[1][part] = grad * normed
        rest = rest.astype(F32)
        rest = jnp.concatenate([rest[:, 128 - experts :], rest[:, : 128 - experts]], axis=1)
        return jnp.concatenate([back, high.astype(F32) + rest], axis=1).astype(LOW)

    residual_grad, gain_parts, attn_grad = ring_reduce(
        part_grad,
        [own_probs, gain_ffn, residual, cotangent[0], router_w],
        [own_shape, own_shape],
        make_attn,
        groups,
        3,
        width + 128,
    )
    grad_gain_ffn = jnp.sum(gain_parts, axis=0)
    attn_grad = attn_grad.reshape(seq_len, width + 128)

    own_width = width // groups
    two_slice = lax.dynamic_slice_in_dim(two_low, place * own_width, own_width, 1)
    grad_router = t_dot(two_slice, attn_grad[:, width:])
    grad_router = grad_router[:, :experts] + grad_router[:, experts : 2 * experts]

    output_kept, output_sent = spread_start(t_dot(head_out, attn_grad)[:, :width])
    if layers == 2:
        lone = jnp.concatenate([shared_in_sent, narrow(shared_down_sent), narrow(output_sent)])
        pair_of = swap_layers(lone)
        cut = shared_in_sent.shape[0]
        end = cut + narrow(shared_down_sent).shape[0]
        grad_shared_in = shared_in_kept + pair_of[:cut].astype(F32)
        grad_shared_down = shared_down_kept + widen(pair_of[cut:end], width).astype(F32)
        grad_output = output_kept + widen(pair_of[end:], width).astype(F32)
    else:
        grad_shared_in = spread_end(shared_in_kept, shared_in_sent)
        grad_shared_down = spread_end(shared_down_kept, shared_down_sent)
        grad_output = spread_end(output_kept, output_sent)
    head_g = dot_t(attn_grad, jnp.pad(output_w, ((0, 0), (0, 128)))).astype(LOW)
    query_grad, key_grad, value_grad = attend_backward(
        head_q, head_k, head_v, doc_ids, logs, head_g
    )
    part_rows, grad_query_head, grad_expand_head = project_back(
        (query_grad, key_grad, value_grad),
        table, one_low, latent_low, query_w, expand_w, tok_rows,
    )
    grad_query_head = grad_query_head.reshape(groups, layers, own_rows, query_width)
    grad_expand_head = grad_expand_head.reshape(groups, layers, own_rows, fold)
    head_grads = jnp.concatenate([grad_query_head, grad_expand_head], axis=3).transpose(1, 0, 2, 3)
    head_grads = head_grads.astype(LOW)
    if layers != 2:
        head_grads = lax.psum_scatter(head_grads, "fsdp", scatter_dimension=0, tiled=True)
    own_latent = lax.dynamic_slice_in_dim(latent_proj, place * tok_rows, tok_rows, 0)
    own_table = lax.dynamic_slice_in_dim(table, place * tok_rows, tok_rows, 0)

    def make_latent(total, part, extras, outs):
        gain = extras[1][...]
        grad = total[:, width : width + LAT]
        _, normed, factor = norm_forward(extras[0][part], gain)
        inner = grad * gain
        back = factor * (inner - normed * jnp.mean(inner * normed, axis=-1, keepdims=True))
        turned = total[:, width + LAT : width + LAT + ROPE]
        turned = turned * extras[2][part, :ROPE] - swapped(turned) * extras[2][part, ROPE:]
        outs[0][part] = total[:, :width]
        outs[1][part] = grad * normed
        return jnp.concatenate([back, turned, jnp.zeros_like(turned)], axis=1).astype(LOW)

    one_grad, latent_gains, head_grads, latent_grad = ring_reduce(
        part_rows,
        [own_latent, gain_latent, own_table],
        [own_shape, jax.ShapeDtypeStruct((tok_rows, LAT), F32)],
        make_latent,
        groups,
        4,
        LAT + 2 * ROPE,
        head_grads,
    )
    grad_query = (
        head_grads[..., :query_width].transpose(1, 0, 2).reshape(own_rows, H * query_width)
    ).astype(F32)
    grad_expand = (
        head_grads[..., query_width:]
        .reshape(H, lat_rows, NOPE + VD)
        .transpose(1, 0, 2)
        .reshape(lat_rows, H * (NOPE + VD))
    ).astype(F32)

    own_latent_grad = lax.dynamic_index_in_dim(latent_grad, place, 0, keepdims=False)
    one_grad = one_grad + dot_t(own_latent_grad[:, : LAT + ROPE], small[:, : LAT + ROPE])
    _, normed_one, factor_one = norm_forward(hidden_own, gain_attn)
    input_part, grad_gain_attn = norm_backward(one_grad, normed_one, factor_one, gain_attn)
    input_grad = (residual_grad + input_part).astype(LOW)

    one_slice = lax.dynamic_slice_in_dim(one_low, place * own_width, own_width, 1)
    grad_latent = t_dot(one_slice, latent_grad.reshape(seq_len, LAT + 2 * ROPE))
    gain_sums = jnp.concatenate(
        [
            grad_gain_attn.reshape(groups, own_width),
            grad_gain_ffn.reshape(groups, own_width),
            jnp.pad(
                jnp.sum(latent_gains, axis=0).reshape(groups, layers, lat_rows),
                ((0, 0), (0, 0), (0, own_rows - lat_rows)),
            ).reshape(groups, own_width),
        ],
        axis=1,
    )
    gain_sums = lax.all_to_all(gain_sums, "seq", split_axis=0, concat_axis=0, tiled=True)
    gain_columns = jnp.sum(gain_sums, axis=0).reshape(3, own_width).T
    packed = jnp.concatenate([grad_latent[:, :at], grad_router, gain_columns], axis=1)
    packed = jnp.pad(packed, ((0, 0), (0, -packed.shape[1] % 128)))
    packed = spread_grad(packed, F32)
    return (
        output[None],
        input_grad[None],
        packed[:, last],
        grad_query,
        packed[:, :at],
        packed[:lat_rows, last + 2],
        grad_expand,
        grad_output,
        packed[:, last + 1],
        packed[:, at:last],
        grad_shared_in[:, :units],
        grad_shared_in[:, units + padding : 2 * units + padding],
        grad_shared_down,
        grad_expert_gate[None],
        grad_expert_up[None],
        grad_expert_down[None],
    )


def solution(mesh):
    flat = P(("seq", "fsdp"))
    rows = P(("seq", "fsdp"), None)
    tokens = P("fsdp", "seq", None)
    expert = P("seq", "fsdp", None)
    weights = (
        flat,
        rows,
        rows,
        flat,
        rows,
        rows,
        flat,
        rows,
        P("fsdp", "seq"),
        P("fsdp", "seq"),
        rows,
        expert,
        expert,
        expert,
    )
    return jax.shard_map(
        body,
        mesh=mesh,
        in_specs=(tokens, tokens, P("fsdp", None), tokens) + weights,
        out_specs=(tokens, tokens) + weights,
        check_vma=False,
    )
```

```python
import functools
import math

import jax
import jax.numpy as jnp
import numpy as np
from jax import lax
from jax.experimental import pallas as pl
from jax.experimental.pallas import tpu as pltpu
from jax.sharding import PartitionSpec as P

H = 16
NOPE = 128
ROPE = 64
VD = 128
LAT = 512
TOP = 6
EPSILON = 1e-06
HIGHEST = lax.Precision.HIGHEST
LOW = jnp.bfloat16
F32 = jnp.float32
MESH = pl.DeviceIdType.MESH


def rotary_table(count):
    powers = np.arange(ROPE // 2, dtype=np.float32) * np.float32(2.0 / ROPE)
    inverse = np.exp(powers * np.float32(-math.log(10000.0)))
    angles = np.arange(count, dtype=np.float32)[:, None] * inverse[None, :]
    cosine, sine = np.cos(angles), np.sin(angles)
    return np.concatenate([cosine, cosine, -sine, sine], axis=1)


def dot(left, right):
    return jnp.dot(left, right, preferred_element_type=F32)


def dot_t(left, right):
    return lax.dot_general(left, right, (((1,), (1,)), ((), ())), preferred_element_type=F32)


def t_dot(left, right):
    return lax.dot_general(left, right, (((0,), (0,)), ((), ())), preferred_element_type=F32)


def exact_t_dot(left, right):
    return lax.dot_general(
        left, right, (((0,), (0,)), ((), ())), precision=HIGHEST, preferred_element_type=F32
    )


def exact_dot_t(left, right):
    return lax.dot_general(
        left, right, (((1,), (1,)), ((), ())), precision=HIGHEST, preferred_element_type=F32
    )


def norm_forward(values, gain):
    factor = lax.rsqrt(jnp.mean(values * values, axis=-1, keepdims=True) + EPSILON)
    normed = values * factor
    return normed * gain, normed, factor


def norm_backward(grad_in, normed, factor, gain):
    inner = grad_in * gain
    gain_grad = jnp.sum(grad_in * normed, axis=0)
    back = factor * (inner - normed * jnp.mean(inner * normed, axis=-1, keepdims=True))
    return back, gain_grad


def swish_slope(value, sigmoid):
    return sigmoid * (1.0 + value * (1.0 - sigmoid))


def after(value, *others):
    return lax.optimization_barrier((value,) + others)[0]


def narrow(array):
    return jnp.concatenate([array[:, i : i + 512] for i in range(0, array.shape[1], 512)])


def widen(array, width):
    rows = array.shape[0] * 512 // width
    return jnp.concatenate([array[i * rows : (i + 1) * rows] for i in range(width // 512)], axis=1)


def swap_layers(own):
    return lax.ppermute(own, "fsdp", ((0, 1), (1, 0)))


def layers_in_order(own, other, axis=0):
    first = lax.axis_index("fsdp") == 0
    return jnp.concatenate([jnp.where(first, own, other), jnp.where(first, other, own)], axis=axis)


def whole_over_layers(own):
    if lax.axis_size("fsdp") != 2:
        return lax.all_gather(own, "fsdp", axis=0, tiled=True)
    return layers_in_order(own, swap_layers(own))


def halves_over_layers(own):
    if lax.axis_size("fsdp") == 2:
        return own, swap_layers(own)
    whole = lax.all_gather(own, "fsdp", axis=0, tiled=True)
    half = whole.shape[0] // 2
    return whole[:half], whole[half:]


def spread_start(grad, kind=LOW):
    layers = lax.axis_size("fsdp")
    if layers != 2:
        return grad.astype(kind), None
    layer, half = lax.axis_index("fsdp"), grad.shape[0] // 2
    sent = lax.dynamic_slice_in_dim(grad, (1 - layer) * half, half, 0).astype(kind)
    return lax.dynamic_slice_in_dim(grad, layer * half, half, 0), sent


def spread_end(kept, sent):
    if sent is None:
        return lax.psum_scatter(kept, "fsdp", scatter_dimension=0, tiled=True).astype(F32)
    return kept + swap_layers(sent).astype(F32)


def spread_grad(grad, kind=LOW):
    return spread_end(*spread_start(grad, kind))


def gather_rows(block):
    return lax.all_gather(block, "seq", axis=0, tiled=True)


def scatter_rows(partial):
    return lax.psum_scatter(partial, "seq", scatter_dimension=0, tiled=True)


def ring_places(groups):
    ring = groups // 2
    me = lax.axis_index("seq")
    chip, core = me // 2, lax.rem(me, 2)
    odd = lax.rem(chip, 2)
    spot = (1 - odd) * (chip // 2) + odd * (ring - 1 - chip // 2)

    def chip_at(place):
        place = lax.rem(place + 2 * ring, ring)
        late = place // (ring // 2)
        return (1 - late) * (2 * place) + late * (2 * ring - 1 - 2 * place)

    def index_at(place, which):
        return 2 * chip_at(place) + which

    return spot, core, index_at


def enter(neighbours):
    barrier = pltpu.get_barrier_semaphore()
    for index in neighbours:
        pl.semaphore_signal(barrier, inc=1, device_id={"seq": index}, device_id_type=MESH)
    pl.semaphore_wait(barrier, len(neighbours))


class Gather:
    def __init__(self, groups, chunks, rows, source, out_ref, sems):
        self.groups, self.chunks, self.size = groups, chunks, rows // chunks
        self.source, self.out = source, out_ref
        self.send, self.recv, self.side_send, self.side_recv = sems
        self.spot, self.core, self.at = ring_places(groups)
        self.ring = groups // 2
        self.steps = groups // 4
        self.started = []

    def block(self, way, step):
        return self.at(self.spot - step if way == 0 else self.spot + step, self.core)

    def slice(self, ref, chunk):
        return ref.at[pl.ds(chunk * self.size, self.size)]

    def forward(self, step, chunk, way):
        index = self.block(way, step)
        own = self.slice(self.source if step == 0 else self.out.at[index], chunk)
        copy = pltpu.make_async_remote_copy(
            src_ref=own,
            dst_ref=self.slice(self.out.at[index], chunk),
            send_sem=self.send.at[way, step, chunk],
            recv_sem=self.recv.at[way, step, chunk],
            device_id={"seq": self.at(self.spot + (1 if way == 0 else -1), self.core)},
            device_id_type=MESH,
        )
        copy.start()
        self.started.append(copy)

    def arrived(self, step, chunk, way):
        index = self.block(way, step + 1)
        here = self.slice(self.out.at[index], chunk)
        pltpu.make_async_remote_copy(
            src_ref=here,
            dst_ref=here,
            send_sem=self.send.at[way, step, chunk],
            recv_sem=self.recv.at[way, step, chunk],
            device_id={"seq": self.at(self.spot, 1 - self.core)},
            device_id_type=MESH,
        ).wait_recv()

    def aside(self, distance, chunk):
        index = self.at(self.spot - distance, self.core)
        own = self.slice(self.source if distance == 0 else self.out.at[index], chunk)
        copy = pltpu.make_async_remote_copy(
            src_ref=own,
            dst_ref=self.slice(self.out.at[index], chunk),
            send_sem=self.side_send.at[distance, chunk],
            recv_sem=self.side_recv.at[distance, chunk],
            device_id={"seq": self.at(self.spot, 1 - self.core)},
            device_id_type=MESH,
        )
        copy.start()
        self.started.append(copy)

    def begin(self, chunk):
        for way in range(2):
            if self.steps > 1 or (chunk < self.chunks // 2) == (way == 0):
                self.forward(0, chunk, way)
        self.aside(0, chunk)

    def turn(self, step, beside=None):
        last = self.steps - 1
        for chunk in range(self.chunks):
            for way in range(2):
                half = (chunk < self.chunks // 2) == (way == 0)
                if step == last and not half:
                    continue
                self.arrived(step, chunk, way)
                if step < last and (step + 1 < last or half):
                    self.forward(step + 1, chunk, way)
                self.aside(step + 1 if way == 0 else self.ring - 1 - step, chunk)
                if beside is not None:
                    beside.step()

    def run(self, beside=None):
        for step in range(self.steps):
            self.turn(step, beside)

    def finish(self):
        for distance in range(self.ring):
            for chunk in range(self.chunks):
                here = self.slice(self.out.at[self.at(self.spot - distance, 1 - self.core)], chunk)
                pltpu.make_async_remote_copy(
                    src_ref=here,
                    dst_ref=here,
                    send_sem=self.side_send.at[distance, chunk],
                    recv_sem=self.side_recv.at[distance, chunk],
                    device_id={"seq": self.at(self.spot, 1 - self.core)},
                    device_id_type=MESH,
                ).wait_recv()
        for copy in self.started:
            copy.wait_send()


def gather_sems(groups, chunks):
    steps, ring = groups // 4, groups // 2
    return [
        pltpu.SemaphoreType.DMA((2, steps, chunks)),
        pltpu.SemaphoreType.DMA((2, steps, chunks)),
        pltpu.SemaphoreType.DMA((ring, chunks)),
        pltpu.SemaphoreType.DMA((ring, chunks)),
    ]


class Exchange:
    def __init__(self, groups, source, place_of, sems):
        self.groups, self.source, self.place_of = groups, source, place_of
        self.send, self.recv = sems
        self.me = lax.axis_index("seq")

    def copy(self, turn):
        other = lax.rem(self.me + turn, self.groups)
        return pltpu.make_async_remote_copy(
            src_ref=self.source.at[other],
            dst_ref=self.place_of(self.me),
            send_sem=self.send.at[turn],
            recv_sem=self.recv.at[turn],
            device_id={"seq": other},
            device_id_type=MESH,
        )

    def begin(self):
        for turn in range(1, self.groups):
            self.copy(turn).start()

    def arrived(self, turn):
        origin = lax.rem(self.me - turn + self.groups, self.groups)
        pltpu.make_async_remote_copy(
            src_ref=self.place_of(origin),
            dst_ref=self.place_of(origin),
            send_sem=self.send.at[turn],
            recv_sem=self.recv.at[turn],
            device_id={"seq": lax.rem(self.me + turn, self.groups)},
            device_id_type=MESH,
        ).wait_recv()
        return origin

    def finish(self):
        for turn in range(1, self.groups):
            self.copy(turn).wait_send()


def enter_all(groups, pair):
    barrier = pltpu.get_barrier_semaphore()
    me = lax.axis_index("seq")
    for turn in range(1, groups):
        pl.semaphore_signal(
            barrier, inc=1, device_id={"seq": lax.rem(me + turn, groups)}, device_id_type=MESH
        )
    if pair:
        other = {"fsdp": 1 - lax.axis_index("fsdp")}
        pl.semaphore_signal(barrier, inc=1, device_id=other, device_id_type=MESH)
    pl.semaphore_wait(barrier, groups if pair else groups - 1)


def across(source, target, send, recv):
    return pltpu.make_async_remote_copy(
        src_ref=source,
        dst_ref=target,
        send_sem=send,
        recv_sem=recv,
        device_id={"fsdp": 1 - lax.axis_index("fsdp")},
        device_id_type=MESH,
    )


def cast_cuts(rows):
    return 4 if rows % 64 == 0 else 1


class Cast:
    def __init__(self, source, target, wide, low, loads, stores):
        self.source, self.target, self.wide, self.low = source, target, wide, low
        self.loads, self.stores = loads, stores
        self.count = cast_cuts(source.shape[0])
        self.size = source.shape[0] // self.count

    def part(self, piece):
        return pl.ds(piece * self.size, self.size)

    def load(self, piece):
        return pltpu.make_async_copy(
            self.source.at[self.part(piece)], self.wide.at[piece % 2], self.loads.at[piece]
        )

    def store(self, piece):
        return pltpu.make_async_copy(
            self.low.at[piece], self.target.at[self.part(piece)], self.stores.at[piece]
        )

    def begin(self):
        for piece in range(min(2, self.count)):
            self.load(piece).start()

    def step(self, piece):
        if piece >= self.count:
            return
        self.load(piece).wait()
        self.low[piece] = self.wide[piece % 2].astype(LOW)
        self.store(piece).start()
        if piece + 2 < self.count:
            self.load(piece + 2).start()

    def finish(self):
        for piece in range(self.count):
            self.store(piece).wait()


def cast_scratch(array):
    rows, columns = array.shape
    count = cast_cuts(rows)
    return [
        pltpu.VMEM((2, rows // count, columns), F32),
        pltpu.VMEM((count, rows // count, columns), LOW),
        pltpu.SemaphoreType.DMA((count,)),
        pltpu.SemaphoreType.DMA((count,)),
    ]


def start_kernel(groups, chunks, pair, rows_ref, small_ref, heads_ref, *rest):
    sources, rest = rest[:3], rest[3:]
    rows_out, small_out, heads_out, *rest = rest
    targets, rest = rest[:3], rest[3:]
    if pair:
        bulk_out, *rest = rest
    casts = [
        Cast(source, target, *rest[4 * i : 4 * i + 4])
        for i, (source, target) in enumerate(zip(sources, targets))
    ]
    rest = rest[12:]
    local_sems, small_y, bulk_y, head_sems, head_recv, head_y, head_y_recv, *sems = rest
    me, layer = lax.axis_index("seq"), lax.axis_index("fsdp")
    mine = layer if pair else 0
    rows = Gather(groups, chunks, rows_ref.shape[0], rows_ref, rows_out, sems[:4])
    spare = small_ref.shape[0]
    block = small_out.at[me]
    part = block.at[pl.ds(pl.multiple_of(mine * spare, spare), spare)]
    small = Gather(groups, chunks, small_out.shape[1], block, small_out, sems[4:])
    heads = Exchange(
        groups, heads_ref, lambda index: heads_out.at[index, mine], (head_sems, head_recv)
    )
    for cast in casts:
        cast.begin()
    locals_ = [
        pltpu.make_async_copy(small_ref, part, local_sems.at[0]),
        pltpu.make_async_copy(rows_ref, rows_out.at[me], local_sems.at[1]),
        pltpu.make_async_copy(heads_ref.at[me], heads_out.at[me, mine], local_sems.at[2]),
    ]
    for copy in locals_:
        copy.start()

    def bulk(piece):
        start = piece * casts[0].size
        size = min(casts[0].size, bulk_out.shape[0] - start)
        return across(
            casts[0].low.at[piece, pl.ds(0, size)],
            bulk_out.at[pl.ds(start, size)],
            bulk_y.at[0, piece],
            bulk_y.at[1, piece],
        )

    enter_all(groups, pair)
    if pair:
        across(small_ref, part, small_y.at[0], small_y.at[1]).start()
    for chunk in range(chunks):
        rows.begin(chunk)
    heads.begin()
    if pair:
        across(heads_ref.at[me], heads_out.at[me, mine], head_y.at[0], head_y_recv.at[0]).start()
        theirs = block.at[pl.ds(pl.multiple_of((1 - mine) * spare, spare), spare)]
        across(theirs, theirs, small_y.at[0], small_y.at[1]).wait_recv()
    locals_[0].wait()
    for chunk in range(chunks):
        small.begin(chunk)
    for piece in range(casts[0].count):
        casts[0].step(piece)
        if pair:
            bulk(piece).start()
    for step in range(rows.steps):
        casts[1].step(step)
        casts[2].step(step)
        small.turn(step)
        rows.turn(step)
        if step == 0:
            for turn in range(1, groups):
                origin = heads.arrived(turn)
                if pair:
                    own = heads_out.at[origin, mine]
                    across(own, own, head_y.at[turn], head_y_recv.at[turn]).start()
    small.finish()
    rows.finish()
    heads.finish()
    for copy in locals_[1:]:
        copy.wait()
    if pair:
        across(small_ref, part, small_y.at[0], small_y.at[1]).wait_send()
        for turn in range(groups):
            origin = lax.rem(me - turn + groups, groups)
            theirs = heads_out.at[origin, 1 - mine]
            copy = across(theirs, theirs, head_y.at[turn], head_y_recv.at[turn])
            copy.wait_send()
            copy.wait_recv()
        for piece in range(casts[0].count):
            bulk(piece).wait_send()
            bulk(piece).wait_recv()
    for cast in casts:
        cast.finish()


def gather_start(rows, small, heads, weights, groups, layers, collective_id, chunks=4):
    pair = layers == 2
    if not pair:
        small = lax.all_gather(small, "fsdp", axis=0, tiled=True)
    height = small.shape[0] * (2 if pair else 1)
    dma = pltpu.SemaphoreType.DMA
    any_spec = pl.BlockSpec(memory_space=pl.ANY)
    share = weights[0].shape[0] * 7 // 8
    outs = [
        jax.ShapeDtypeStruct((groups,) + rows.shape, LOW),
        jax.ShapeDtypeStruct((groups, height, small.shape[1]), LOW),
        jax.ShapeDtypeStruct((groups, 2 if pair else 1) + heads.shape[1:], LOW),
    ] + [jax.ShapeDtypeStruct(array.shape, LOW) for array in weights]
    if pair:
        outs.append(jax.ShapeDtypeStruct((share, weights[0].shape[1]), LOW))
    rows_out, small_out, heads_out, *lows = pl.pallas_call(
        functools.partial(start_kernel, groups, chunks, pair),
        out_shape=outs,
        in_specs=[any_spec] * 6,
        out_specs=[any_spec] * len(outs),
        scratch_shapes=[item for array in weights for item in cast_scratch(array)]
        + [dma((3,)), dma((2,)), dma((2, cast_cuts(weights[0].shape[0])))]
        + [dma((groups,))] * 4
        + gather_sems(groups, chunks)
        + gather_sems(groups, chunks),
        compiler_params=pltpu.CompilerParams(
            collective_id=collective_id, has_side_effects=True, vmem_limit_bytes=50 << 20
        ),
        cost_estimate=pl.CostEstimate(flops=0, bytes_accessed=4 << 20, transcendentals=0),
    )(rows, small, heads, *weights)
    if pair:
        gate = (lows[0], lows[3], swap_layers(lows[0][share:]))
    else:
        heads_out = lax.all_gather(heads_out, "fsdp", axis=1, tiled=True)
        gate = halves_over_layers(lows[0])
    return (
        rows_out.reshape(groups * rows.shape[0], rows.shape[1]),
        small_out.reshape(groups * height, small.shape[1]),
        heads_out,
        (gate, halves_over_layers(lows[1]), halves_over_layers(lows[2])),
    )


class Piece:
    def __init__(self, source, buffer, load_sem, products):
        self.load = pltpu.make_async_copy(source, buffer, load_sem)
        self.products = products


class Products:
    def __init__(self, held, pieces):
        self.held, self.pieces = held, pieces
        self.jobs = [(piece, which) for piece in pieces for which in range(len(piece.products))]
        self.at, self.busy = 0, {}

    def begin(self):
        for copy in self.held:
            copy.start()
        for piece in self.pieces[:2]:
            piece.load.start()

    def step(self):
        if self.at >= len(self.jobs):
            return
        piece, which = self.jobs[self.at]
        if self.at == 0:
            for copy in self.held:
                copy.wait()
        if which == 0:
            piece.load.wait()
        compute, key, stage, store = piece.products[which]
        if key in self.busy:
            self.busy[key].wait()
        stage[...] = compute()
        store.start()
        self.busy[key] = store
        self.at += 1
        if which == len(piece.products) - 1:
            later = self.pieces.index(piece) + 2
            if later < len(self.pieces):
                self.pieces[later].load.start()

    def finish(self):
        while self.at < len(self.jobs):
            self.step()
        for store in self.busy.values():
            store.wait()


class GradProducts:
    tile = 256

    def __init__(self, pair, shapes):
        self.pair = pair
        self.rows, self.width = shapes[0]
        self.units, self.tokens, self.columns = shapes[1][1], shapes[3][0], shapes[4][1]

    def outs(self):
        shared = [(self.width, self.columns), (self.columns // 2, self.width)]
        experts = [(self.width // 2, self.units)] * 2 if self.pair else []
        return [jax.ShapeDtypeStruct(shape, F32) for shape in experts + shared]

    def counts(self):
        experts = self.width // 2 // self.tile if self.pair else 0
        return experts, self.width // self.tile

    def scratch(self):
        experts, shared = self.counts()
        dma, tile = pltpu.SemaphoreType.DMA, self.tile
        scratch = [
            pltpu.VMEM((self.tokens, self.columns), LOW),
            pltpu.VMEM((self.tokens, self.columns // 2), LOW),
            pltpu.VMEM((2, self.tokens, tile), LOW),
            pltpu.VMEM((2, tile, self.columns), F32),
            pltpu.VMEM((2, self.columns // 2, tile), F32),
            dma((4,)),
            dma((experts + 2 * shared,)),
            dma((2 * experts + 2 * shared,)),
        ]
        if self.pair:
            scratch += [
                pltpu.VMEM((self.rows, self.units), LOW),
                pltpu.VMEM((self.rows, self.units), LOW),
                pltpu.VMEM((2, self.rows, tile), LOW),
                pltpu.VMEM((2, tile, self.units), F32),
            ]
        return scratch

    def build(self, ins, outs, scratch):
        rows_ref, gate_ref, up_ref, two_ref, dproj_ref, hs_ref, grads_ref = ins
        dproj, hs, pieces_buf, in_stage, out_stage, held_sems, load_sems, store_sems, *rest = scratch
        tile = self.tile
        held = [
            pltpu.make_async_copy(dproj_ref, dproj, held_sems.at[0]),
            pltpu.make_async_copy(hs_ref, hs, held_sems.at[1]),
        ]
        pieces, stored = [], 0
        experts, shared = self.counts()

        def columns(ref, index, base=0):
            return ref.at[:, pl.ds(pl.multiple_of(base + index * tile, tile), tile)]

        if self.pair:
            gate, up, slots, stage = rest
            held += [
                pltpu.make_async_copy(gate_ref, gate, held_sems.at[2]),
                pltpu.make_async_copy(up_ref, up, held_sems.at[3]),
            ]
            base = lax.axis_index("fsdp") * (self.width // 2)
            for index in range(experts):
                slot = slots.at[index % 2]
                products = []
                for number, right in enumerate((gate, up)):
                    target = outs[number].at[pl.ds(index * tile, tile)]
                    products.append(
                        (
                            functools.partial(lambda a, b: t_dot(a[...], b[...]), slot, right),
                            ("e", number),
                            stage.at[number],
                            pltpu.make_async_copy(stage.at[number], target, store_sems.at[stored]),
                        )
                    )
                    stored += 1
                pieces.append(
                    Piece(columns(rows_ref, index, base), slot, load_sems.at[len(pieces)], products)
                )
        for index in range(shared):
            slot, stage = pieces_buf.at[index % 2], in_stage.at[index % 2]
            target = outs[-2].at[pl.ds(index * tile, tile)]
            product = (
                functools.partial(lambda a, b: t_dot(a[...], b[...]), slot, dproj),
                ("i", index % 2),
                stage,
                pltpu.make_async_copy(stage, target, store_sems.at[stored]),
            )
            stored += 1
            pieces.append(Piece(columns(two_ref, index), slot, load_sems.at[len(pieces)], [product]))
        for index in range(shared):
            slot, stage = pieces_buf.at[index % 2], out_stage.at[index % 2]
            product = (
                functools.partial(lambda a, b: t_dot(b[...], a[...]), slot, hs),
                ("o", index % 2),
                stage,
                pltpu.make_async_copy(stage, columns(outs[-1], index), store_sems.at[stored]),
            )
            stored += 1
            pieces.append(Piece(columns(grads_ref, index), slot, load_sems.at[len(pieces)], [product]))
        return Products(held, pieces)


class HeadGrads:
    def __init__(self, groups, pair, grads_ref, out_ref, came, total, y_sems, send, recv, own_sem):
        self.pair, self.grads, self.out = pair, grads_ref, out_ref
        self.came, self.total, self.y_sems, self.own_sem = came, total, y_sems, own_sem
        self.mine = lax.axis_index("fsdp") if pair else 0
        self.groups = groups
        self.me = lax.axis_index("seq")
        self.spread = Exchange(groups, total, lambda index: out_ref.at[index], (send, recv))

    def cross(self):
        return across(self.grads.at[1 - self.mine], self.came, self.y_sems.at[0], self.y_sems.at[1])

    def begin(self):
        if self.pair:
            self.cross().start()

    def middle(self):
        if self.pair:
            self.cross().wait_recv()
            total = self.grads[self.mine].astype(F32) + self.came[...].astype(F32)
            self.total[...] = total.astype(LOW)
        else:
            self.total[...] = self.grads[0]
        self.spread.begin()
        self.local = pltpu.make_async_copy(
            self.total.at[self.me], self.out.at[self.me], self.own_sem
        )
        self.local.start()

    def finish(self):
        for turn in range(1, self.groups):
            self.spread.arrived(turn)
        self.spread.finish()
        self.local.wait()
        if self.pair:
            self.cross().wait_send()


def reduce_kernel(groups, chunks, extras, outs, rowfn, gathers, heads, grads, *refs):
    parts_ref = refs[0]
    extra_refs = refs[1 : 1 + extras]
    if heads is not None:
        heads_ref, refs = refs[1 + extras], refs[: 1 + extras] + refs[2 + extras :]
    beside = None
    if grads is not None:
        beside_ins, refs = refs[1 + extras : 8 + extras], refs[: 1 + extras] + refs[8 + extras :]
    out_refs = refs[1 + extras : 1 + extras + outs]
    rest = list(refs[1 + extras + outs :])
    if heads is not None:
        head_out = rest.pop(0)
    if grads is not None:
        count = len(grads.outs())
        beside_outs, rest = rest[:count], rest[count:]
        count = len(grads.scratch())
        beside = grads.build(beside_ins, beside_outs, rest[-count:])
        rest = rest[:-count]
        beside.begin()
    gather_ref = rest.pop(0) if gathers else None
    own, side, came, sent = rest[:4]
    own_sem, side_send, side_recv, send_sem, recv_sem = rest[4:9]
    ready = rest[9] if gathers else None
    rows = own.shape[1]
    size = rows // chunks
    ring, steps = groups // 2, groups // 4
    spot, core, at = ring_places(groups)
    sibling = {"seq": at(spot, 1 - core)}
    if heads is None:
        enter((at(spot - 1, core), at(spot + 1, core), at(spot, 1 - core)))
    else:
        head_grads = HeadGrads(groups, heads, heads_ref, head_out, *rest[-6:])
        enter_all(groups, heads)
        head_grads.begin()

    order = []
    for step in range(steps):
        order.append(steps - step)
        if step:
            order.append(ring - steps + step)
    order.append(0)
    started = []
    loads = {}
    for far in order:
        copy = pltpu.make_async_remote_copy(
            src_ref=parts_ref.at[at(spot + far, 1 - core)],
            dst_ref=side.at[far],
            send_sem=side_send.at[far],
            recv_sem=side_recv.at[far],
            device_id=sibling,
            device_id_type=MESH,
        )
        copy.start()
        started.append(copy)
        load = pltpu.make_async_copy(
            parts_ref.at[at(spot + far, core)], own.at[far], own_sem.at[far]
        )
        load.start()
        loads[far] = (load, copy)

    here = set()

    def both(far, chunk):
        if far not in here:
            here.add(far)
            loads[far][0].wait()
            loads[far][1].wait_recv()
        part = pl.ds(chunk * size, size)
        return own[far, part].astype(F32) + side[far, part].astype(F32)

    def neighbour_copy(way, step, chunk):
        part = pl.ds(chunk * size, size)
        return pltpu.make_async_remote_copy(
            src_ref=sent.at[way, step, part],
            dst_ref=came.at[way, step, part],
            send_sem=send_sem.at[way, step, chunk],
            recv_sem=recv_sem.at[way, step, chunk],
            device_id={"seq": at(spot + (1 if way == 0 else -1), core)},
            device_id_type=MESH,
        )

    def half(way, chunk):
        return (chunk < chunks // 2) == (way == 0)

    for step in range(steps):
        for chunk in range(chunks):
            for way in range(2):
                if step == 0 and not half(way, chunk):
                    continue
                far = steps - step if way == 0 else ring - (steps - step)
                part = pl.ds(chunk * size, size)
                total = both(far, chunk)
                if step > 1 or (step == 1 and half(way, chunk)):
                    neighbour_copy(way, step - 1, chunk).wait_recv()
                    total = total + came[way, step - 1, part].astype(F32)
                sent[way, step, part] = total.astype(sent.dtype)
                copy = neighbour_copy(way, step, chunk)
                copy.start()
                started.append(copy)
                if beside is not None and step:
                    beside.step()
    if heads is not None:
        head_grads.middle()
    gather = Gather(groups, chunks, rows, ready, gather_ref, rest[10:14]) if gathers else None
    for chunk in range(chunks):
        part = pl.ds(chunk * size, size)
        total = both(0, chunk)
        for way in range(2):
            if steps > 1 or half(way, chunk):
                neighbour_copy(way, steps - 1, chunk).wait_recv()
                total = total + came[way, steps - 1, part].astype(F32)
        made = rowfn(total, part, extra_refs, out_refs)
        if gathers:
            ready[part] = made
            gather.begin(chunk)
    if gathers:
        local = pltpu.make_async_copy(ready, gather_ref.at[at(spot, core)], rest[14])
        local.start()
        gather.run(beside)
        gather.finish()
        local.wait()
    if beside is not None:
        beside.finish()
    if heads is not None:
        head_grads.finish()
    for copy in started:
        copy.wait_send()


def ring_reduce(
    parts, extras, outs, rowfn, groups, collective_id, gathers=None, heads=None, grads=None,
    grad_ins=(), chunks=4,
):
    _, rows, columns = parts.shape
    ring, steps = groups // 2, groups // 4
    scratch = [
        pltpu.VMEM((ring, rows, columns), LOW),
        pltpu.VMEM((ring, rows, columns), LOW),
        pltpu.VMEM((2, steps, rows, columns), LOW),
        pltpu.VMEM((2, steps, rows, columns), LOW),
        pltpu.SemaphoreType.DMA((ring,)),
        pltpu.SemaphoreType.DMA((ring,)),
        pltpu.SemaphoreType.DMA((ring,)),
        pltpu.SemaphoreType.DMA((2, steps, chunks)),
        pltpu.SemaphoreType.DMA((2, steps, chunks)),
    ]
    shapes = list(outs)
    specs = [pl.BlockSpec(memory_space=pltpu.VMEM)] * len(outs)
    extras = list(extras)
    count = len(extras)
    pair = None
    if heads is not None:
        pair = heads.shape[0] == 2
        extras.append(heads)
        shapes.append(jax.ShapeDtypeStruct(heads.shape[1:], LOW))
        specs.append(pl.BlockSpec(memory_space=pltpu.VMEM))
    any_spec = pl.BlockSpec(memory_space=pl.ANY)
    if grads is not None:
        shapes += grads.outs()
        specs += [any_spec] * len(grads.outs())
    if gathers is not None:
        shapes.append(jax.ShapeDtypeStruct((groups, rows, gathers), LOW))
        specs.append(pl.BlockSpec(memory_space=pl.ANY))
        scratch.append(pltpu.VMEM((rows, gathers), LOW))
        scratch += gather_sems(groups, chunks)
        scratch.append(pltpu.SemaphoreType.DMA)
    if heads is not None:
        scratch += [pltpu.VMEM(heads.shape[1:], LOW)] * 2
        scratch += [pltpu.SemaphoreType.DMA((2,))]
        scratch += [pltpu.SemaphoreType.DMA((groups,))] * 2
        scratch += [pltpu.SemaphoreType.DMA]
    if grads is not None:
        scratch += grads.scratch()
    return pl.pallas_call(
        functools.partial(
            reduce_kernel, groups, chunks, count, len(outs), rowfn, gathers is not None, pair, grads
        ),
        out_shape=shapes,
        in_specs=[pl.BlockSpec(memory_space=pl.ANY)]
        + [pl.BlockSpec(memory_space=pltpu.VMEM)] * len(extras)
        + [any_spec] * len(grad_ins),
        out_specs=specs,
        scratch_shapes=scratch,
        compiler_params=pltpu.CompilerParams(
            collective_id=collective_id, has_side_effects=True, vmem_limit_bytes=60 << 20
        ),
        cost_estimate=pl.CostEstimate(
            flops=0, bytes_accessed=4 << 20, transcendentals=0
        ),
    )(parts, *extras, *grad_ins)


def attend_kernel(blocks, q_ref, k_ref, v_ref, col_ref, row_ref, out_ref, log_ref):
    size = q_ref.shape[0] // blocks
    scale = (NOPE + ROPE) ** (-0.5)
    for index in range(blocks):
        part = pl.ds(index * size, size)
        reach = (index + 1) * size
        scores = dot_t(q_ref[part], k_ref[:reach]) * scale
        rows = index * size + lax.broadcasted_iota(jnp.int32, (size, reach), 0)
        columns = lax.broadcasted_iota(jnp.int32, (size, reach), 1)
        allowed = (col_ref[part] == row_ref[:, :reach]) & (rows >= columns)
        scores = jnp.where(allowed, scores, -1e30)
        peak = jnp.max(scores, axis=-1, keepdims=True)
        raised = jnp.exp(scores - peak)
        total = jnp.sum(raised, axis=-1, keepdims=True)
        weights = (raised * (1.0 / total)).astype(LOW)
        out_ref[part] = dot(weights, v_ref[:reach]).astype(LOW)
        log_ref[part] = peak + jnp.log(total)


def attend_forward(head_q, head_k, head_v, doc_ids):
    seq_len = head_q.shape[0]
    return pl.pallas_call(
        functools.partial(attend_kernel, seq_len // 256),
        out_shape=[
            jax.ShapeDtypeStruct((seq_len, VD), LOW),
            jax.ShapeDtypeStruct((seq_len, 1), F32),
        ],
        compiler_params=pltpu.CompilerParams(vmem_limit_bytes=50 << 20),
        cost_estimate=pl.CostEstimate(
            flops=seq_len * seq_len * 400, bytes_accessed=4 << 20, transcendentals=seq_len * seq_len // 2
        ),
    )(head_q, head_k, head_v, doc_ids[:, None], doc_ids[None, :])


def attend_back_kernel(
    blocks, q_ref, k_ref, v_ref, g_ref, col_ref, row_ref, log_ref, dq_ref, dk_ref, dv_ref, ksum, vsum
):
    size = q_ref.shape[0] // blocks
    scale = (NOPE + ROPE) ** (-0.5)
    ksum[...] = jnp.zeros_like(ksum)
    vsum[...] = jnp.zeros_like(vsum)
    for index in range(blocks):
        part = pl.ds(index * size, size)
        reach = (index + 1) * size
        query, grad = q_ref[part], g_ref[part]
        scores = dot_t(k_ref[:reach], query) * scale
        keys = lax.broadcasted_iota(jnp.int32, (reach, size), 0)
        rows = index * size + lax.broadcasted_iota(jnp.int32, (reach, size), 1)
        allowed = (col_ref[:reach] == row_ref[:, part]) & (rows >= keys)
        weights = jnp.exp(jnp.where(allowed, scores, -1e30) - log_ref[:, part])
        vsum[:reach] += dot(weights.astype(LOW), grad)
        slopes = dot_t(v_ref[:reach], grad)
        inner = jnp.sum(weights * slopes, axis=0, keepdims=True)
        back = (weights * (slopes - inner)).astype(LOW)
        ksum[:reach] += dot(back, query)
        dq_ref[part] = (t_dot(back, k_ref[:reach]) * scale).astype(LOW)
    dk_ref[...] = (ksum[...] * scale).astype(LOW)
    dv_ref[...] = vsum[...].astype(LOW)


def attend_backward(head_q, head_k, head_v, doc_ids, logs, head_g):
    seq_len = head_q.shape[0]
    return pl.pallas_call(
        functools.partial(attend_back_kernel, seq_len // 256),
        out_shape=[
            jax.ShapeDtypeStruct((seq_len, NOPE + ROPE), LOW),
            jax.ShapeDtypeStruct((seq_len, NOPE + ROPE), LOW),
            jax.ShapeDtypeStruct((seq_len, VD), LOW),
        ],
        scratch_shapes=[
            pltpu.VMEM((seq_len, NOPE + ROPE), F32),
            pltpu.VMEM((seq_len, VD), F32),
        ],
        compiler_params=pltpu.CompilerParams(vmem_limit_bytes=56 << 20),
        cost_estimate=pl.CostEstimate(
            flops=seq_len * seq_len * 1000, bytes_accessed=6 << 20, transcendentals=seq_len * seq_len // 2
        ),
    )(head_q, head_k, head_v, head_g, doc_ids[:, None], doc_ids[None, :], logs.reshape(1, seq_len))


def swapped(values):
    half = values.shape[-1] // 2
    return jnp.concatenate([values[:, half:], values[:, :half]], axis=-1)


def project_kernel(
    x_ref, gain_ref, wq_ref, wl_ref, gain_lat_ref, we_ref, table_ref,
    one_ref, q_ref, k_ref, v_ref, m_ref, c_ref,
):
    one = norm_forward(x_ref[...].astype(F32), gain_ref[...])[0].astype(LOW)
    one_ref[...] = one
    cosine, sine = table_ref[:, :ROPE], table_ref[:, ROPE:]
    query = dot(one, wq_ref[...])
    turned = query[:, NOPE:]
    q_ref[:, :NOPE] = query[:, :NOPE].astype(LOW)
    q_ref[:, NOPE:] = (turned * cosine + swapped(turned) * sine).astype(LOW)
    latent = dot(one, wl_ref[...])
    turned = latent[:, LAT : LAT + ROPE]
    k_ref[:, NOPE:] = (turned * cosine + swapped(turned) * sine).astype(LOW)
    c_ref[...] = latent[:, :LAT]
    scaled = norm_forward(latent[:, :LAT], gain_lat_ref[...])[0].astype(LOW)
    m_ref[...] = scaled
    expanded = dot(scaled, we_ref[...])
    k_ref[:, :NOPE] = expanded[:, :NOPE].astype(LOW)
    v_ref[...] = expanded[:, NOPE:].astype(LOW)


def project(rows, gain, query_w, small, gain_latent, expand_w, table, tile=256):
    seq_len, width = rows.shape

    def cut(columns):
        return pl.BlockSpec((tile, columns), lambda i: (i, 0))

    def whole(array):
        return pl.BlockSpec(array.shape, lambda i: (0, 0))

    outs = [(width, LOW), (NOPE + ROPE, LOW), (NOPE + ROPE, LOW), (VD, LOW), (LAT, LOW), (LAT, F32)]
    return pl.pallas_call(
        project_kernel,
        grid=(seq_len // tile,),
        out_shape=[jax.ShapeDtypeStruct((seq_len, c), t) for c, t in outs],
        in_specs=[
            cut(width), whole(gain), whole(query_w), whole(small), whole(gain_latent),
            whole(expand_w), cut(2 * ROPE),
        ],
        out_specs=[cut(c) for c, _ in outs],
        compiler_params=pltpu.CompilerParams(vmem_limit_bytes=50 << 20),
        cost_estimate=pl.CostEstimate(
            flops=seq_len * width * 1800, bytes_accessed=28 << 20, transcendentals=0
        ),
    )(rows, gain, query_w, small, gain_latent, expand_w, table)


def project_back_kernel(
    dq_ref, dk_ref, dv_ref, table_ref, one_ref, m_ref, wq_ref, we_ref,
    parts_ref, gq_ref, ge_ref, dq_low, de_low,
):
    cosine, sine = table_ref[:, :ROPE], table_ref[:, ROPE:]
    turned = dq_ref[:, NOPE:].astype(F32)
    dq_low[:, :NOPE] = dq_ref[:, :NOPE]
    dq_low[:, NOPE:] = (turned * cosine - swapped(turned) * sine).astype(LOW)
    de_low[:, :NOPE] = dk_ref[:, :NOPE]
    de_low[:, NOPE:] = dv_ref[...]
    blocks, rows, wide = parts_ref.shape
    width, last = one_ref.shape[1], LAT + ROPE
    parts_ref[:, :, :width] = dot_t(dq_low[...], wq_ref[...]).astype(LOW).reshape(blocks, rows, width)
    parts_ref[:, :, width : width + LAT] = (
        dot_t(de_low[...], we_ref[...]).astype(LOW).reshape(blocks, rows, LAT)
    )
    parts_ref[:, :, width + LAT : width + last] = dk_ref[:, NOPE:].reshape(blocks, rows, ROPE)
    parts_ref[:, :, width + last :] = jnp.zeros((blocks, rows, wide - width - last), LOW)

    @pl.when(pl.program_id(0) == 0)
    def _():
        gq_ref[...] = jnp.zeros_like(gq_ref)
        ge_ref[...] = jnp.zeros_like(ge_ref)

    gq_ref[...] += t_dot(one_ref[...], dq_low[...])
    ge_ref[...] += t_dot(m_ref[...], de_low[...])


def project_back(grads, table, one_low, latent_low, query_w, expand_w, tok_rows, tile=256):
    seq_len, width = one_low.shape
    wide = width + LAT + 2 * ROPE

    def cut(columns):
        return pl.BlockSpec((tile, columns), lambda i: (i, 0))

    def whole(shape):
        return pl.BlockSpec(shape, lambda i: (0, 0))

    return pl.pallas_call(
        project_back_kernel,
        grid=(seq_len // tile,),
        out_shape=[
            jax.ShapeDtypeStruct((seq_len // tok_rows, tok_rows, wide), LOW),
            jax.ShapeDtypeStruct(query_w.shape, F32),
            jax.ShapeDtypeStruct(expand_w.shape, F32),
        ],
        in_specs=[
            cut(NOPE + ROPE), cut(NOPE + ROPE), cut(VD), cut(2 * ROPE), cut(width), cut(LAT),
            whole(query_w.shape), whole(expand_w.shape),
        ],
        out_specs=[
            pl.BlockSpec((tile // tok_rows, tok_rows, wide), lambda i: (i, 0, 0)),
            whole(query_w.shape),
            whole(expand_w.shape),
        ],
        scratch_shapes=[pltpu.VMEM((tile, NOPE + ROPE), LOW), pltpu.VMEM((tile, NOPE + VD), LOW)],
        compiler_params=pltpu.CompilerParams(vmem_limit_bytes=50 << 20),
        cost_estimate=pl.CostEstimate(
            flops=seq_len * width * 1300, bytes_accessed=28 << 20, transcendentals=0
        ),
    )(*grads, table, one_low, latent_low, query_w, expand_w)


def blocks_of(ref, count):
    size = ref.shape[0] // count
    return [pl.ds(block * size, size) for block in range(count)]


def two_parts(values):
    high = values.astype(LOW)
    return high, (values - high.astype(F32)).astype(LOW)


class Weights:
    def __init__(self, pair, counts, refs, wholes, sems):
        self.copies, at, number = [], 0, 0
        first = lax.axis_index("fsdp") if pair else 0
        for whole, pieces in zip(wholes, counts):
            half, own, copies = whole.shape[0] // 2, refs[at], []
            start = first * half
            for piece in [own] + list(refs[at + 1 : at + pieces]):
                size = piece.shape[0]
                place = pl.ds(pl.multiple_of(start, 64), size)
                copies.append(pltpu.make_async_copy(piece, whole.at[place], sems.at[number]))
                number += 1
                start = (1 - first) * half if piece is own else start + size
            self.copies.append(copies)
            at += pieces

    def on_first(self, act):
        @pl.when(pl.program_id(0) == 0)
        def _():
            act()

    def begin(self, order):
        self.on_first(lambda: [copy.start() for which in order for copy in self.copies[which]])

    def ready(self, which):
        self.on_first(lambda: [copy.wait() for copy in self.copies[which]])


def ffn_kernel(
    pair, counts, rows_ref, chosen_ref, mine_ref, router_ref, wi_ref, wo_ref, *refs,
):
    pieces = sum(counts)
    parts, refs = refs[:pieces], refs[pieces:]
    (
        probs_ref, slot_gate_ref, in_ref, gate_ref, up_ref, inner_ref, made_ref, proj_ref, hs_ref,
        out_ref, spread, wg_ref, wu_ref, wd_ref, sems,
    ) = refs
    count = 4
    weights = Weights(pair, counts, parts, (wg_ref, wu_ref, wd_ref), sems)
    weights.begin((0, 1, 2))
    tokens, slots = blocks_of(rows_ref, count), blocks_of(chosen_ref, count)
    lanes = lax.broadcasted_iota(jnp.int32, mine_ref.shape, 1)
    logits = jnp.where(mine_ref[1:2] > 0, dot(rows_ref[...], router_ref[...]), -1e30)
    raised = jnp.exp(logits - jnp.max(logits, axis=-1, keepdims=True))
    probs = raised / jnp.sum(raised, axis=-1, keepdims=True)
    probs_ref[...] = probs
    high, rest = two_parts(jnp.sum(probs * mine_ref[0:1], axis=-1, keepdims=True))
    high, rest = high.astype(F32), rest.astype(F32)
    columns = jnp.where(lanes[0:1] == 0, high, jnp.where(lanes[0:1] == 1, rest, 0.0)).astype(LOW)
    for token, slot in zip(tokens, slots):
        size = token.size
        picked = columns[token.start : token.start + size]
        chosen = chosen_ref[slot]
        slot_gate_ref[slot] = jnp.sum(dot(chosen, picked), axis=-1, keepdims=True)
        in_ref[slot] = dot(chosen, rows_ref[token]).astype(LOW)
    weights.ready(0)
    gate = dot(in_ref[...], wg_ref[...])
    weights.ready(1)
    up = dot(in_ref[...], wu_ref[...])
    gate_ref[...] = gate
    up_ref[...] = up
    inner_ref[...] = (gate * jax.nn.sigmoid(gate) * up).astype(LOW)
    weights.ready(2)
    made = dot(inner_ref[...], wd_ref[...]).astype(LOW)
    made_ref[...] = made
    spread[...] = (slot_gate_ref[...] * made.astype(F32)).astype(LOW)
    proj = dot(rows_ref[...], wi_ref[...])
    proj_ref[...] = proj
    half = proj.shape[1] // 2
    gate, up = proj[:, :half], proj[:, half:]
    hs_ref[...] = (gate * jax.nn.sigmoid(gate) * up).astype(LOW)
    for token, slot in zip(tokens, slots):
        total = t_dot(chosen_ref[slot], spread[slot]) + dot(hs_ref[token], wo_ref[...])
        out_ref[token] = total.astype(LOW)


def ffn_back_kernel(
    pair, counts, grads_ref, chosen_ref, mine_ref, slot_gate_ref, made_ref, gate_ref, up_ref,
    proj_ref, wi_ref, wo_ref, *refs,
):
    pieces = sum(counts)
    parts, refs = refs[:pieces], refs[pieces:]
    dy_ref, dgate_ref, dup_ref, dproj_ref, parts_ref, spread, wg_ref, wu_ref, wd_ref, sems = refs
    count = 4
    width = grads_ref.shape[1]
    weights = Weights(pair, counts, parts, (wg_ref, wu_ref, wd_ref), sems)
    weights.begin((2, 0, 1))
    tokens, slots = blocks_of(grads_ref, count), blocks_of(chosen_ref, count)
    mine, shifted = mine_ref[0:1], mine_ref[2:3]
    for token, slot in zip(tokens, slots):
        picked = dot(chosen_ref[slot], grads_ref[token])
        dy_ref[slot] = (slot_gate_ref[slot] * picked).astype(LOW)
        score = jnp.sum(picked * made_ref[slot].astype(F32), axis=-1, keepdims=True)
        high, rest = two_parts(score)
        spread[slot, width:] = (high.astype(F32) * mine + rest.astype(F32) * shifted).astype(LOW)
    weights.ready(2)
    inner = dot_t(dy_ref[...], wd_ref[...])
    gate = gate_ref[...]
    sigmoid = jax.nn.sigmoid(gate)
    dgate_ref[...] = (inner * up_ref[...] * swish_slope(gate, sigmoid)).astype(LOW)
    dup_ref[...] = (inner * gate * sigmoid).astype(LOW)
    weights.ready(0)
    weights.ready(1)
    back = dot_t(dgate_ref[...], wg_ref[...]) + dot_t(dup_ref[...], wu_ref[...])
    spread[:, :width] = back.astype(LOW)
    half = proj_ref.shape[1] // 2
    gate, up = proj_ref[:, :half], proj_ref[:, half:]
    sigmoid = jax.nn.sigmoid(gate)
    inner = dot_t(grads_ref[...], wo_ref[...])
    dproj_ref[:, :half] = (inner * up * swish_slope(gate, sigmoid)).astype(LOW)
    dproj_ref[:, half:] = (inner * gate * sigmoid).astype(LOW)
    for block, (token, slot) in enumerate(zip(tokens, slots)):
        total = t_dot(chosen_ref[slot], spread[slot])
        parts_ref[block, :, :width] = (
            total[:, :width] + dot_t(dproj_ref[token], wi_ref[...])
        ).astype(LOW)
        parts_ref[block, :, width:] = total[:, width:].astype(LOW)


def row_grid(kernel, steps, cuts, outs, scratch, flops):
    def cut(shape):
        rest = (0,) * (len(shape) - 1)
        return pl.BlockSpec((shape[0] // steps,) + tuple(shape[1:]), lambda i: (i,) + rest)

    def whole(shape):
        rest = (0,) * len(shape)
        return pl.BlockSpec(tuple(shape), lambda i: rest, pipeline_mode=pl.Buffered(1))

    operands = [array for array, _ in cuts]
    return pl.pallas_call(
        kernel,
        grid=(steps,),
        out_shape=outs,
        in_specs=[
            pl.BlockSpec(memory_space=pl.ANY)
            if fixed is None
            else whole(a.shape) if fixed else cut(a.shape)
            for a, fixed in cuts
        ],
        out_specs=[cut(o.shape) for o in outs],
        scratch_shapes=scratch,
        compiler_params=pltpu.CompilerParams(vmem_limit_bytes=60 << 20),
        cost_estimate=pl.CostEstimate(flops=flops, bytes_accessed=60 << 20, transcendentals=0),
    )(*operands)


def grad_in_kernel(layer_ref, rows_ref, grads_ref, sent_ref):
    sent_ref[...] = t_dot(rows_ref[...], grads_ref[...]).astype(LOW)


def grad_in(rows, grads, tile=512):
    count, width = rows.shape
    columns = grads.shape[1]
    half = width // 2 // tile
    layer = lax.axis_index("fsdp").reshape(1)
    return pl.pallas_call(
        grad_in_kernel,
        grid_spec=pltpu.PrefetchScalarGridSpec(
            num_scalar_prefetch=1,
            grid=(half,),
            in_specs=[
                pl.BlockSpec((count, tile), lambda i, layer: (0, i + (1 - layer[0]) * half)),
                pl.BlockSpec((count, columns), lambda i, _: (0, 0)),
            ],
            out_specs=pl.BlockSpec((tile, columns), lambda i, _: (i, 0)),
        ),
        out_shape=jax.ShapeDtypeStruct((width // 2, columns), LOW),
        compiler_params=pltpu.CompilerParams(vmem_limit_bytes=50 << 20),
        cost_estimate=pl.CostEstimate(
            flops=count * width * columns, bytes_accessed=10 << 20, transcendentals=0
        ),
    )(layer, rows, grads)


def grad_out_kernel(layer_ref, inner_ref, grads_ref, sent_ref, kept_ref, made):
    half = sent_ref.shape[0]
    layer = layer_ref[0]
    made[...] = t_dot(inner_ref[...], grads_ref[...])
    sent_ref[...] = made[pl.ds(pl.multiple_of((1 - layer) * half, 8), half)].astype(LOW)
    kept_ref[...] = made[pl.ds(pl.multiple_of(layer * half, 8), half)]


def grad_out(inner, grads, tile=512):
    count, units = inner.shape
    width = grads.shape[1]
    layer = lax.axis_index("fsdp").reshape(1)
    return pl.pallas_call(
        grad_out_kernel,
        grid_spec=pltpu.PrefetchScalarGridSpec(
            num_scalar_prefetch=1,
            grid=(width // tile,),
            in_specs=[
                pl.BlockSpec((count, units), lambda i, _: (0, 0)),
                pl.BlockSpec((count, tile), lambda i, _: (0, i)),
            ],
            out_specs=[
                pl.BlockSpec((units // 2, tile), lambda i, _: (0, i)),
                pl.BlockSpec((units // 2, tile), lambda i, _: (0, i)),
            ],
            scratch_shapes=[pltpu.VMEM((units, tile), F32)],
        ),
        out_shape=[
            jax.ShapeDtypeStruct((units // 2, width), LOW),
            jax.ShapeDtypeStruct((units // 2, width), F32),
        ],
        compiler_params=pltpu.CompilerParams(vmem_limit_bytes=50 << 20),
        cost_estimate=pl.CostEstimate(
            flops=2 * count * width * units, bytes_accessed=16 << 20, transcendentals=0
        ),
    )(layer, inner, grads)


def body(
    tokens,
    cotangent,
    segments,
    routes,
    norm_attn,
    w_query,
    w_latent,
    norm_latent,
    w_expand,
    w_output,
    norm_ffn,
    w_router,
    w_shared_gate,
    w_shared_up,
    w_shared_down,
    w_expert_gate,
    w_expert_up,
    w_expert_down,
):
    groups = lax.axis_size("seq")
    layers = lax.axis_size("fsdp")
    both = ("seq", "fsdp")
    place = lax.axis_index("seq")
    tok_rows, width = tokens.shape[1], tokens.shape[2]
    seq_len = segments.shape[1]
    own_rows = w_query.shape[0]
    lat_rows = w_expand.shape[0]
    experts = w_router.shape[1]
    capacity = tok_rows // 2
    query_width = NOPE + ROPE
    hidden_own = tokens[0].astype(F32)
    grad_own = cotangent[0].astype(F32)
    doc_ids = segments[0]

    lat_column = jnp.pad(norm_latent[:, None], ((0, own_rows - lat_rows), (0, 0)))
    at = LAT + ROPE
    route_columns = routes.reshape(own_rows, tok_rows * TOP // own_rows).astype(F32)
    packed = [w_latent, w_router, norm_attn[:, None], norm_ffn[:, None], lat_column, route_columns]
    packed = jnp.concatenate(packed, axis=1).astype(LOW)
    used = packed.shape[1]
    last = at + experts
    packed = jnp.pad(packed, ((0, 0), (0, -used % 128)))

    fold = lat_rows * (NOPE + VD) // own_rows
    query_parts = w_query.astype(LOW).reshape(own_rows, H, query_width).transpose(1, 0, 2)
    expand_parts = (
        w_expand.astype(LOW)
        .reshape(lat_rows, H, NOPE + VD)
        .transpose(1, 0, 2)
        .reshape(H, own_rows, fold)
    )
    head_parts = jnp.concatenate([query_parts, expand_parts], axis=2)
    hidden_low, small, head_parts, expert_sets = gather_start(
        tokens[0],
        packed,
        head_parts,
        (w_expert_gate[0], w_expert_up[0], w_expert_down[0]),
        groups,
        layers,
        1,
    )
    query_w = head_parts[..., :query_width].reshape(width, query_width)
    expand_w = head_parts[..., query_width:].reshape(LAT, NOPE + VD)
    router_w = jnp.pad(small[:, at:last], ((0, 0), (0, 128 - experts)))
    all_routes = small[:, last + 3 : used].reshape(groups, layers, -1)
    all_routes = lax.dynamic_index_in_dim(all_routes, lax.axis_index("fsdp"), 1, keepdims=False)
    all_routes = all_routes.reshape(groups, tok_rows, TOP)
    gains = small[:, last : last + 3].astype(F32).T
    gain_attn, gain_ffn = gains[0:1], gains[1:2]
    gain_latent = gains[2].reshape(groups * layers, own_rows)[:, :lat_rows].reshape(1, LAT)

    units = w_shared_gate.shape[1]
    padding = -units % 128
    spare = ((0, 0), (0, padding))
    shared_in = jnp.concatenate([jnp.pad(w_shared_gate, spare), jnp.pad(w_shared_up, spare)], axis=1)
    shared_in = shared_in.astype(LOW)
    shared_in = after(shared_in, hidden_low)
    down_low, output_low = w_shared_down.astype(LOW), w_output.astype(LOW)
    if layers == 2:
        lone = jnp.concatenate([shared_in, narrow(down_low), narrow(output_low)])
        pair_of = swap_layers(lone)
        cut = shared_in.shape[0]
        end = cut + narrow(down_low).shape[0]
        shared_in_w = layers_in_order(shared_in, pair_of[:cut])
        shared_down_w = layers_in_order(down_low, widen(pair_of[cut:end], width))
        output_w = layers_in_order(output_low, widen(pair_of[end:], width))
    else:
        shared_in_w = whole_over_layers(shared_in)
        shared_down_w = whole_over_layers(down_low)
        output_w = whole_over_layers(output_low)
    shared_down_w = jnp.pad(shared_down_w, ((0, padding), (0, 0)))

    grad_low = gather_rows(after(cotangent[0], hidden_low))

    table = jnp.asarray(rotary_table(seq_len))
    one_low, head_q, head_k, head_v, latent_low, latent_proj = project(
        hidden_low, gain_attn, query_w, small, gain_latent, expand_w, table
    )
    head_out, logs = attend_forward(head_q, head_k, head_v, doc_ids)
    part_residual = dot(head_out, output_w).astype(LOW).reshape(groups, tok_rows, width)

    def make_two(total, part, extras, outs):
        row_sum = extras[0][part].astype(F32) + total
        outs[0][part] = row_sum
        return norm_forward(row_sum, extras[1][...])[0].astype(LOW)

    own_shape = jax.ShapeDtypeStruct((tok_rows, width), F32)
    residual, two_low = ring_reduce(
        part_residual, [tokens[0], gain_ffn], [own_shape], make_two, groups, 2, width
    )
    two_low = after(two_low, grad_low).reshape(seq_len, width)

    named = jnp.any(all_routes == place.astype(LOW), axis=-1)
    rank = jnp.cumsum(named.astype(jnp.int32), axis=1) - 1
    slots = jnp.arange(capacity, dtype=jnp.int32)
    chosen = named[:, None, :] & (rank[:, None, :] == slots[None, :, None])
    chosen = chosen.astype(LOW).reshape(groups * capacity, tok_rows)
    lanes = jnp.arange(128, dtype=jnp.int32)
    mine = jnp.stack(
        [(lanes == place), (lanes < experts), (lanes == place + experts)] + [lanes < 0] * 5
    ).astype(F32)
    slot_count, unit_count = groups * capacity, w_expert_gate.shape[2]
    expert_w = [(piece, None) for pieces in expert_sets for piece in pieces]
    counts = tuple(len(pieces) for pieces in expert_sets)
    expert_scratch = [
        pltpu.VMEM((width, unit_count), LOW),
        pltpu.VMEM((width, unit_count), LOW),
        pltpu.VMEM((unit_count, width), LOW),
        pltpu.SemaphoreType.DMA((len(expert_w),)),
    ]
    columns = shared_in_w.shape[1]

    def array(rows, columns, kind=LOW):
        return jax.ShapeDtypeStruct((rows, columns), kind)

    steps = groups // 4
    routed_flops = 6 * slot_count * width * unit_count
    probs, slot_gate, expert_in, gate_proj, up_proj, inner_low, made, shared_proj, shared_low, part_out = row_grid(
        functools.partial(ffn_kernel, layers == 2, counts),
        steps,
        [
            (two_low, False), (chosen, False), (mine, True), (router_w, True),
            (shared_in_w, True), (shared_down_w, True), *expert_w,
        ],
        [
            array(seq_len, 128, F32), array(slot_count, 1, F32), array(slot_count, width),
            array(slot_count, unit_count, F32), array(slot_count, unit_count, F32),
            array(slot_count, unit_count), array(slot_count, width), array(seq_len, columns, F32),
            array(seq_len, columns // 2), array(seq_len, width),
        ],
        [pltpu.VMEM((slot_count // steps, width), LOW)] + expert_scratch,
        routed_flops * 3 // 2,
    )
    ffn_out = scatter_rows(part_out).astype(F32)
    output = (residual + ffn_out).astype(LOW)

    made_grad, gate_grad, up_grad, shared_grads, part_grad = row_grid(
        functools.partial(ffn_back_kernel, layers == 2, counts),
        steps,
        [
            (grad_low, False), (chosen, False), (mine, True), (slot_gate, False), (made, False),
            (gate_proj, False), (up_proj, False), (shared_proj, False),
            (shared_in_w, True), (shared_down_w, True), *expert_w,
        ],
        [
            array(slot_count, width), array(slot_count, unit_count), array(slot_count, unit_count),
            array(seq_len, columns),
            jax.ShapeDtypeStruct((groups, tok_rows, width + 128), LOW),
        ],
        [pltpu.VMEM((slot_count // steps, width + 128), LOW)] + expert_scratch,
        routed_flops * 3 // 2,
    )

    if layers == 2:
        down_sent, down_kept = grad_out(inner_low, made_grad)
        gate_sent = grad_in(expert_in, gate_grad)
        up_sent = grad_in(expert_in, up_grad)
        part_grad = after(part_grad, down_sent, gate_sent, up_sent)
    else:
        down_kept, down_sent = spread_start(t_dot(inner_low, made_grad))
        gate_kept, gate_sent = spread_start(t_dot(expert_in, gate_grad))
        up_kept, up_sent = spread_start(t_dot(expert_in, up_grad))
    own_probs = lax.dynamic_slice_in_dim(probs, place * tok_rows, tok_rows, 0)

    def make_attn(total, part, extras, outs):
        probs = extras[0][part]
        score = total[:, width:]
        score = score + jnp.concatenate([score[:, experts:], score[:, :experts]], axis=1)
        logit = probs * (score - jnp.sum(probs * score, axis=-1, keepdims=True))
        high, rest = two_parts(logit)
        grad = total[:, :width] + dot_t(high, extras[4][...]) + dot_t(rest, extras[4][...])
        gain = extras[1][...]
        _, normed, factor = norm_forward(extras[2][part], gain)
        inner = grad * gain
        back = factor * (inner - normed * jnp.mean(inner * normed, axis=-1, keepdims=True))
        back = extras[3][part].astype(F32) + back
        outs[0][part] = back
        outs[1][part] = grad * normed
        rest = rest.astype(F32)
        rest = jnp.concatenate([rest[:, 128 - experts :], rest[:, : 128 - experts]], axis=1)
        return jnp.concatenate([back, high.astype(F32) + rest], axis=1).astype(LOW)

    grad_ins = (expert_in, gate_grad, up_grad, two_low, shared_grads, shared_low, grad_low)
    grads = GradProducts(layers == 2, [array.shape for array in grad_ins])
    residual_grad, gain_parts, *made_grads, attn_grad = ring_reduce(
        part_grad,
        [own_probs, gain_ffn, residual, cotangent[0], router_w],
        [own_shape, own_shape],
        make_attn,
        groups,
        3,
        width + 128,
        None,
        grads,
        grad_ins,
    )
    shared_in_kept, shared_in_sent = spread_start(made_grads[-2])
    shared_down_kept, shared_down_sent = spread_start(made_grads[-1][:units])
    if layers == 2:
        gate_kept, up_kept = made_grads[:2]
    grad_expert_down = spread_end(down_kept, down_sent)
    grad_expert_gate = spread_end(gate_kept, gate_sent)
    grad_expert_up = spread_end(up_kept, up_sent)
    grad_gain_ffn = jnp.sum(gain_parts, axis=0)
    attn_grad = attn_grad.reshape(seq_len, width + 128)

    own_width = width // groups
    two_slice = lax.dynamic_slice_in_dim(two_low, place * own_width, own_width, 1)
    grad_router = t_dot(two_slice, attn_grad[:, width:])
    grad_router = grad_router[:, :experts] + grad_router[:, experts : 2 * experts]

    output_kept, output_sent = spread_start(t_dot(head_out, attn_grad)[:, :width])
    if layers == 2:
        lone = jnp.concatenate([shared_in_sent, narrow(shared_down_sent), narrow(output_sent)])
        pair_of = swap_layers(lone)
        cut = shared_in_sent.shape[0]
        end = cut + narrow(shared_down_sent).shape[0]
        grad_shared_in = shared_in_kept + pair_of[:cut].astype(F32)
        grad_shared_down = shared_down_kept + widen(pair_of[cut:end], width).astype(F32)
        grad_output = output_kept + widen(pair_of[end:], width).astype(F32)
    else:
        grad_shared_in = spread_end(shared_in_kept, shared_in_sent)
        grad_shared_down = spread_end(shared_down_kept, shared_down_sent)
        grad_output = spread_end(output_kept, output_sent)
    head_g = dot_t(attn_grad, jnp.pad(output_w, ((0, 0), (0, 128)))).astype(LOW)
    query_grad, key_grad, value_grad = attend_backward(
        head_q, head_k, head_v, doc_ids, logs, head_g
    )
    part_rows, grad_query_head, grad_expand_head = project_back(
        (query_grad, key_grad, value_grad),
        table, one_low, latent_low, query_w, expand_w, tok_rows,
    )
    grad_query_head = grad_query_head.reshape(groups, layers, own_rows, query_width)
    grad_expand_head = grad_expand_head.reshape(groups, layers, own_rows, fold)
    head_grads = jnp.concatenate([grad_query_head, grad_expand_head], axis=3).transpose(1, 0, 2, 3)
    head_grads = head_grads.astype(LOW)
    if layers != 2:
        head_grads = lax.psum_scatter(head_grads, "fsdp", scatter_dimension=0, tiled=True)
    own_latent = lax.dynamic_slice_in_dim(latent_proj, place * tok_rows, tok_rows, 0)
    own_table = lax.dynamic_slice_in_dim(table, place * tok_rows, tok_rows, 0)

    def make_latent(total, part, extras, outs):
        gain = extras[1][...]
        grad = total[:, width : width + LAT]
        _, normed, factor = norm_forward(extras[0][part], gain)
        inner = grad * gain
        back = factor * (inner - normed * jnp.mean(inner * normed, axis=-1, keepdims=True))
        turned = total[:, width + LAT : width + LAT + ROPE]
        turned = turned * extras[2][part, :ROPE] - swapped(turned) * extras[2][part, ROPE:]
        outs[0][part] = total[:, :width]
        outs[1][part] = grad * normed
        return jnp.concatenate([back, turned, jnp.zeros_like(turned)], axis=1).astype(LOW)

    one_grad, latent_gains, head_grads, latent_grad = ring_reduce(
        part_rows,
        [own_latent, gain_latent, own_table],
        [own_shape, jax.ShapeDtypeStruct((tok_rows, LAT), F32)],
        make_latent,
        groups,
        4,
        LAT + 2 * ROPE,
        head_grads,
    )
    grad_query = (
        head_grads[..., :query_width].transpose(1, 0, 2).reshape(own_rows, H * query_width)
    ).astype(F32)
    grad_expand = (
        head_grads[..., query_width:]
        .reshape(H, lat_rows, NOPE + VD)
        .transpose(1, 0, 2)
        .reshape(lat_rows, H * (NOPE + VD))
    ).astype(F32)

    own_latent_grad = lax.dynamic_index_in_dim(latent_grad, place, 0, keepdims=False)
    one_grad = one_grad + dot_t(own_latent_grad[:, : LAT + ROPE], small[:, : LAT + ROPE])
    _, normed_one, factor_one = norm_forward(hidden_own, gain_attn)
    input_part, grad_gain_attn = norm_backward(one_grad, normed_one, factor_one, gain_attn)
    input_grad = (residual_grad + input_part).astype(LOW)

    one_slice = lax.dynamic_slice_in_dim(one_low, place * own_width, own_width, 1)
    grad_latent = t_dot(one_slice, latent_grad.reshape(seq_len, LAT + 2 * ROPE))
    gain_sums = jnp.concatenate(
        [
            grad_gain_attn.reshape(groups, own_width),
            grad_gain_ffn.reshape(groups, own_width),
            jnp.pad(
                jnp.sum(latent_gains, axis=0).reshape(groups, layers, lat_rows),
                ((0, 0), (0, 0), (0, own_rows - lat_rows)),
            ).reshape(groups, own_width),
        ],
        axis=1,
    )
    gain_sums = lax.all_to_all(gain_sums, "seq", split_axis=0, concat_axis=0, tiled=True)
    gain_columns = jnp.sum(gain_sums, axis=0).reshape(3, own_width).T
    packed = jnp.concatenate([grad_latent[:, :at], grad_router, gain_columns], axis=1)
    packed = jnp.pad(packed, ((0, 0), (0, -packed.shape[1] % 128)))
    packed_kept, packed_sent = spread_start(packed, F32)
    if layers == 2:
        came = after(
            swap_layers(packed_sent), grad_expert_down, grad_expert_gate, grad_expert_up
        )
        packed = packed_kept + came
    else:
        packed = spread_end(packed_kept, packed_sent)
    return (
        output[None],
        input_grad[None],
        packed[:, last],
        grad_query,
        packed[:, :at],
        packed[:lat_rows, last + 2],
        grad_expand,
        grad_output,
        packed[:, last + 1],
        packed[:, at:last],
        grad_shared_in[:, :units],
        grad_shared_in[:, units + padding : 2 * units + padding],
        grad_shared_down,
        grad_expert_gate[None],
        grad_expert_up[None],
        grad_expert_down[None],
    )


def solution(mesh):
    flat = P(("seq", "fsdp"))
    rows = P(("seq", "fsdp"), None)
    tokens = P("fsdp", "seq", None)
    expert = P("seq", "fsdp", None)
    weights = (
        flat,
        rows,
        rows,
        flat,
        rows,
        rows,
        flat,
        rows,
        P("fsdp", "seq"),
        P("fsdp", "seq"),
        rows,
        expert,
        expert,
        expert,
    )
    return jax.shard_map(
        body,
        mesh=mesh,
        in_specs=(tokens, tokens, P("fsdp", None), tokens) + weights,
        out_specs=(tokens, tokens) + weights,
        check_vma=False,
    )
```

```python
import functools
import math

import jax
import jax.numpy as jnp
import numpy as np
from jax import lax
from jax.experimental import pallas as pl
from jax.experimental.pallas import tpu as pltpu
from jax.sharding import PartitionSpec as P

H = 16
NOPE = 128
ROPE = 64
VD = 128
LAT = 512
TOP = 6
EPSILON = 1e-06
HIGHEST = lax.Precision.HIGHEST
LOW = jnp.bfloat16
F32 = jnp.float32
MESH = pl.DeviceIdType.MESH


def rotary_table(count):
    powers = np.arange(ROPE // 2, dtype=np.float32) * np.float32(2.0 / ROPE)
    inverse = np.exp(powers * np.float32(-math.log(10000.0)))
    angles = np.arange(count, dtype=np.float32)[:, None] * inverse[None, :]
    cosine, sine = np.cos(angles), np.sin(angles)
    return np.concatenate([cosine, cosine, -sine, sine], axis=1)


def dot(left, right):
    return jnp.dot(left, right, preferred_element_type=F32)


def dot_t(left, right):
    return lax.dot_general(left, right, (((1,), (1,)), ((), ())), preferred_element_type=F32)


def t_dot(left, right):
    return lax.dot_general(left, right, (((0,), (0,)), ((), ())), preferred_element_type=F32)


def exact_t_dot(left, right):
    return lax.dot_general(
        left, right, (((0,), (0,)), ((), ())), precision=HIGHEST, preferred_element_type=F32
    )


def exact_dot_t(left, right):
    return lax.dot_general(
        left, right, (((1,), (1,)), ((), ())), precision=HIGHEST, preferred_element_type=F32
    )


def norm_forward(values, gain):
    factor = lax.rsqrt(jnp.mean(values * values, axis=-1, keepdims=True) + EPSILON)
    normed = values * factor
    return normed * gain, normed, factor


def norm_backward(grad_in, normed, factor, gain):
    inner = grad_in * gain
    gain_grad = jnp.sum(grad_in * normed, axis=0)
    back = factor * (inner - normed * jnp.mean(inner * normed, axis=-1, keepdims=True))
    return back, gain_grad


def swish_slope(value, sigmoid):
    return sigmoid * (1.0 + value * (1.0 - sigmoid))


def after(value, *others):
    return lax.optimization_barrier((value,) + others)[0]


def swap_layers(own):
    return lax.ppermute(own, "fsdp", ((0, 1), (1, 0)))


def layers_in_order(own, other, axis=0):
    first = lax.axis_index("fsdp") == 0
    return jnp.concatenate([jnp.where(first, own, other), jnp.where(first, other, own)], axis=axis)


def whole_over_layers(own):
    if lax.axis_size("fsdp") != 2:
        return lax.all_gather(own, "fsdp", axis=0, tiled=True)
    return layers_in_order(own, swap_layers(own))


def halves_over_layers(own):
    if lax.axis_size("fsdp") == 2:
        return own, swap_layers(own)
    whole = lax.all_gather(own, "fsdp", axis=0, tiled=True)
    half = whole.shape[0] // 2
    return whole[:half], whole[half:]


def spread_start(grad, kind=LOW):
    layers = lax.axis_size("fsdp")
    if layers != 2:
        return grad.astype(kind), None
    layer, half = lax.axis_index("fsdp"), grad.shape[0] // 2
    sent = lax.dynamic_slice_in_dim(grad, (1 - layer) * half, half, 0).astype(kind)
    return lax.dynamic_slice_in_dim(grad, layer * half, half, 0), sent


def spread_end(kept, sent):
    if sent is None:
        return lax.psum_scatter(kept, "fsdp", scatter_dimension=0, tiled=True).astype(F32)
    return kept + swap_layers(sent).astype(F32)


def spread_grad(grad, kind=LOW):
    return spread_end(*spread_start(grad, kind))


def gather_rows(block):
    return lax.all_gather(block, "seq", axis=0, tiled=True)


def scatter_rows(partial):
    return lax.psum_scatter(partial, "seq", scatter_dimension=0, tiled=True)


def ring_places(groups):
    ring = groups // 2
    me = lax.axis_index("seq")
    chip, core = me // 2, lax.rem(me, 2)
    odd = lax.rem(chip, 2)
    spot = (1 - odd) * (chip // 2) + odd * (ring - 1 - chip // 2)

    def chip_at(place):
        place = lax.rem(place + 2 * ring, ring)
        late = place // (ring // 2)
        return (1 - late) * (2 * place) + late * (2 * ring - 1 - 2 * place)

    def index_at(place, which):
        return 2 * chip_at(place) + which

    return spot, core, index_at


def enter(neighbours):
    barrier = pltpu.get_barrier_semaphore()
    for index in neighbours:
        pl.semaphore_signal(barrier, inc=1, device_id={"seq": index}, device_id_type=MESH)
    pl.semaphore_wait(barrier, len(neighbours))


class Gather:
    def __init__(self, groups, chunks, rows, source, out_ref, sems):
        self.groups, self.chunks, self.size = groups, chunks, rows // chunks
        self.source, self.out = source, out_ref
        self.send, self.recv, self.side_send, self.side_recv = sems
        self.spot, self.core, self.at = ring_places(groups)
        self.ring = groups // 2
        self.steps = groups // 4
        self.started = []

    def block(self, way, step):
        return self.at(self.spot - step if way == 0 else self.spot + step, self.core)

    def slice(self, ref, chunk):
        return ref.at[pl.ds(chunk * self.size, self.size)]

    def forward(self, step, chunk, way):
        index = self.block(way, step)
        own = self.slice(self.source if step == 0 else self.out.at[index], chunk)
        copy = pltpu.make_async_remote_copy(
            src_ref=own,
            dst_ref=self.slice(self.out.at[index], chunk),
            send_sem=self.send.at[way, step, chunk],
            recv_sem=self.recv.at[way, step, chunk],
            device_id={"seq": self.at(self.spot + (1 if way == 0 else -1), self.core)},
            device_id_type=MESH,
        )
        copy.start()
        self.started.append(copy)

    def arrived(self, step, chunk, way):
        index = self.block(way, step + 1)
        here = self.slice(self.out.at[index], chunk)
        pltpu.make_async_remote_copy(
            src_ref=here,
            dst_ref=here,
            send_sem=self.send.at[way, step, chunk],
            recv_sem=self.recv.at[way, step, chunk],
            device_id={"seq": self.at(self.spot, 1 - self.core)},
            device_id_type=MESH,
        ).wait_recv()

    def aside(self, distance, chunk):
        index = self.at(self.spot - distance, self.core)
        own = self.slice(self.source if distance == 0 else self.out.at[index], chunk)
        copy = pltpu.make_async_remote_copy(
            src_ref=own,
            dst_ref=self.slice(self.out.at[index], chunk),
            send_sem=self.side_send.at[distance, chunk],
            recv_sem=self.side_recv.at[distance, chunk],
            device_id={"seq": self.at(self.spot, 1 - self.core)},
            device_id_type=MESH,
        )
        copy.start()
        self.started.append(copy)

    def begin(self, chunk):
        for way in range(2):
            if self.steps > 1 or (chunk < self.chunks // 2) == (way == 0):
                self.forward(0, chunk, way)
        self.aside(0, chunk)

    def turn(self, step, beside=None):
        last = self.steps - 1
        for chunk in range(self.chunks):
            for way in range(2):
                half = (chunk < self.chunks // 2) == (way == 0)
                if step == last and not half:
                    continue
                self.arrived(step, chunk, way)
                if step < last and (step + 1 < last or half):
                    self.forward(step + 1, chunk, way)
                self.aside(step + 1 if way == 0 else self.ring - 1 - step, chunk)
                if beside is not None:
                    beside.step()

    def run(self, beside=None):
        for step in range(self.steps):
            self.turn(step, beside)

    def finish(self):
        for distance in range(self.ring):
            for chunk in range(self.chunks):
                here = self.slice(self.out.at[self.at(self.spot - distance, 1 - self.core)], chunk)
                pltpu.make_async_remote_copy(
                    src_ref=here,
                    dst_ref=here,
                    send_sem=self.side_send.at[distance, chunk],
                    recv_sem=self.side_recv.at[distance, chunk],
                    device_id={"seq": self.at(self.spot, 1 - self.core)},
                    device_id_type=MESH,
                ).wait_recv()
        for copy in self.started:
            copy.wait_send()


def gather_sems(groups, chunks):
    steps, ring = groups // 4, groups // 2
    return [
        pltpu.SemaphoreType.DMA((2, steps, chunks)),
        pltpu.SemaphoreType.DMA((2, steps, chunks)),
        pltpu.SemaphoreType.DMA((ring, chunks)),
        pltpu.SemaphoreType.DMA((ring, chunks)),
    ]


class Exchange:
    def __init__(self, groups, source, place_of, sems):
        self.groups, self.source, self.place_of = groups, source, place_of
        self.send, self.recv = sems
        self.me = lax.axis_index("seq")

    def copy(self, turn):
        other = lax.rem(self.me + turn, self.groups)
        return pltpu.make_async_remote_copy(
            src_ref=self.source.at[other],
            dst_ref=self.place_of(self.me),
            send_sem=self.send.at[turn],
            recv_sem=self.recv.at[turn],
            device_id={"seq": other},
            device_id_type=MESH,
        )

    def begin(self):
        for turn in range(1, self.groups):
            self.copy(turn).start()

    def arrived(self, turn):
        origin = lax.rem(self.me - turn + self.groups, self.groups)
        pltpu.make_async_remote_copy(
            src_ref=self.place_of(origin),
            dst_ref=self.place_of(origin),
            send_sem=self.send.at[turn],
            recv_sem=self.recv.at[turn],
            device_id={"seq": lax.rem(self.me + turn, self.groups)},
            device_id_type=MESH,
        ).wait_recv()
        return origin

    def finish(self):
        for turn in range(1, self.groups):
            self.copy(turn).wait_send()


def enter_all(groups, pair):
    barrier = pltpu.get_barrier_semaphore()
    me = lax.axis_index("seq")
    for turn in range(1, groups):
        pl.semaphore_signal(
            barrier, inc=1, device_id={"seq": lax.rem(me + turn, groups)}, device_id_type=MESH
        )
    if pair:
        other = {"fsdp": 1 - lax.axis_index("fsdp")}
        pl.semaphore_signal(barrier, inc=1, device_id=other, device_id_type=MESH)
    pl.semaphore_wait(barrier, groups if pair else groups - 1)


def across(source, target, send, recv):
    return pltpu.make_async_remote_copy(
        src_ref=source,
        dst_ref=target,
        send_sem=send,
        recv_sem=recv,
        device_id={"fsdp": 1 - lax.axis_index("fsdp")},
        device_id_type=MESH,
    )


def cast_cuts(rows):
    return 4 if rows % 64 == 0 else 1


class Cast:
    def __init__(self, source, target, wide, low, loads, stores):
        self.source, self.target, self.wide, self.low = source, target, wide, low
        self.loads, self.stores = loads, stores
        self.count = cast_cuts(source.shape[0])
        self.size = source.shape[0] // self.count

    def part(self, piece):
        return pl.ds(piece * self.size, self.size)

    def load(self, piece):
        return pltpu.make_async_copy(
            self.source.at[self.part(piece)], self.wide.at[piece % 2], self.loads.at[piece]
        )

    def store(self, piece):
        if isinstance(self.target, tuple):
            first = self.target[0].shape[0] // self.size
            target = self.target[0 if piece < first else 1]
            place = pl.ds((piece if piece < first else piece - first) * self.size, self.size)
        else:
            target, place = self.target, self.part(piece)
        return pltpu.make_async_copy(self.low.at[piece], target.at[place], self.stores.at[piece])

    def begin(self):
        for piece in range(min(2, self.count)):
            self.load(piece).start()

    def step(self, piece):
        if piece >= self.count:
            return
        self.load(piece).wait()
        self.low[piece] = self.wide[piece % 2].astype(LOW)
        self.store(piece).start()
        if piece + 2 < self.count:
            self.load(piece + 2).start()

    def finish(self):
        for piece in range(self.count):
            self.store(piece).wait()


def cast_scratch(array):
    rows, columns = array.shape
    count = cast_cuts(rows)
    return [
        pltpu.VMEM((2, rows // count, columns), F32),
        pltpu.VMEM((count, rows // count, columns), LOW),
        pltpu.SemaphoreType.DMA((count,)),
        pltpu.SemaphoreType.DMA((count,)),
    ]


def start_kernel(groups, chunks, pair, count, rows_ref, small_ref, heads_ref, *rest):
    sources, rest = rest[:count], rest[count:]
    rows_out, small_out, heads_out, *rest = rest
    targets, rest = rest[:count], rest[count:]
    if pair:
        bulk_out, *rest = rest
        lone_outs, rest = rest[: count - 3], rest[count - 3 :]
        gate_rest, *rest = rest
        targets = ((targets[0], gate_rest),) + tuple(targets[1:])
    casts = [
        Cast(source, target, *rest[4 * i : 4 * i + 4])
        for i, (source, target) in enumerate(zip(sources, targets))
    ]
    rest = rest[4 * count :]
    local_sems, small_y, bulk_y, lone_y, head_sems, head_recv, head_y, head_y_recv, *sems = rest
    me, layer = lax.axis_index("seq"), lax.axis_index("fsdp")
    mine = layer if pair else 0
    rows = Gather(groups, chunks, rows_ref.shape[0], rows_ref, rows_out, sems[:4])
    spare = small_ref.shape[0]
    block = small_out.at[me]
    part = block.at[pl.ds(pl.multiple_of(mine * spare, spare), spare)]
    small = Gather(groups, chunks, small_out.shape[1], block, small_out, sems[4:])
    heads = Exchange(
        groups, heads_ref, lambda index: heads_out.at[index, mine], (head_sems, head_recv)
    )
    for cast in casts:
        cast.begin()
    locals_ = [
        pltpu.make_async_copy(small_ref, part, local_sems.at[0]),
        pltpu.make_async_copy(rows_ref, rows_out.at[me], local_sems.at[1]),
        pltpu.make_async_copy(heads_ref.at[me], heads_out.at[me, mine], local_sems.at[2]),
    ]
    for copy in locals_:
        copy.start()

    def bulk(piece):
        size = casts[0].size
        return across(
            casts[0].low.at[piece],
            bulk_out.at[pl.ds(piece * size, size)],
            bulk_y.at[0, piece],
            bulk_y.at[1, piece],
        )

    def lone(index):
        low = casts[3 + index].low
        return across(low, lone_outs[index], lone_y.at[0, index], lone_y.at[1, index])

    enter_all(groups, pair)
    if pair:
        across(small_ref, part, small_y.at[0], small_y.at[1]).start()
    for chunk in range(chunks):
        rows.begin(chunk)
    heads.begin()
    if pair:
        across(heads_ref.at[me], heads_out.at[me, mine], head_y.at[0], head_y_recv.at[0]).start()
        theirs = block.at[pl.ds(pl.multiple_of((1 - mine) * spare, spare), spare)]
        across(theirs, theirs, small_y.at[0], small_y.at[1]).wait_recv()
    locals_[0].wait()
    for chunk in range(chunks):
        small.begin(chunk)
    for index, cast in enumerate(casts[3:]):
        for piece in range(cast.count):
            cast.step(piece)
        if pair:
            lone(index).start()
    shared = range(bulk_out.shape[0] // casts[0].size) if pair else ()
    for piece in range(casts[0].count):
        casts[0].step(piece)
        if piece in shared:
            bulk(piece).start()
    for step in range(rows.steps):
        casts[1].step(step)
        casts[2].step(step)
        small.turn(step)
        rows.turn(step)
        if step == 0:
            for turn in range(1, groups):
                origin = heads.arrived(turn)
                if pair:
                    own = heads_out.at[origin, mine]
                    across(own, own, head_y.at[turn], head_y_recv.at[turn]).start()
    small.finish()
    rows.finish()
    heads.finish()
    for copy in locals_[1:]:
        copy.wait()
    if pair:
        across(small_ref, part, small_y.at[0], small_y.at[1]).wait_send()
        for turn in range(groups):
            origin = lax.rem(me - turn + groups, groups)
            theirs = heads_out.at[origin, 1 - mine]
            copy = across(theirs, theirs, head_y.at[turn], head_y_recv.at[turn])
            copy.wait_send()
            copy.wait_recv()
        for piece in shared:
            bulk(piece).wait_send()
            bulk(piece).wait_recv()
        for index in range(count - 3):
            lone(index).wait_send()
            lone(index).wait_recv()
    for cast in casts:
        cast.finish()


def gather_start(rows, small, heads, weights, groups, layers, collective_id, chunks=4):
    pair = layers == 2
    if not pair:
        small = lax.all_gather(small, "fsdp", axis=0, tiled=True)
    height = small.shape[0] * (2 if pair else 1)
    dma = pltpu.SemaphoreType.DMA
    any_spec = pl.BlockSpec(memory_space=pl.ANY)
    share = weights[0].shape[0] // 4
    count = len(weights)
    outs = [
        jax.ShapeDtypeStruct((groups,) + rows.shape, LOW),
        jax.ShapeDtypeStruct((groups, height, small.shape[1]), LOW),
        jax.ShapeDtypeStruct((groups, 2 if pair else 1) + heads.shape[1:], LOW),
    ] + [jax.ShapeDtypeStruct(array.shape, LOW) for array in weights]
    gate_shape = weights[0].shape
    if pair:
        outs[3] = jax.ShapeDtypeStruct((share, gate_shape[1]), LOW)
        outs.append(outs[3])
        for array in weights[3:]:
            cuts = cast_cuts(array.shape[0])
            outs.append(
                jax.ShapeDtypeStruct((cuts, array.shape[0] // cuts, array.shape[1]), LOW)
            )
        outs.append(jax.ShapeDtypeStruct((gate_shape[0] - share, gate_shape[1]), LOW))
    rows_out, small_out, heads_out, *lows = pl.pallas_call(
        functools.partial(start_kernel, groups, chunks, pair, count),
        out_shape=outs,
        in_specs=[any_spec] * (3 + count),
        out_specs=[any_spec] * len(outs),
        scratch_shapes=[item for array in weights for item in cast_scratch(array)]
        + [dma((3,)), dma((2,)), dma((2, cast_cuts(weights[0].shape[0]))), dma((2, count))]
        + [dma((groups,))] * 4
        + gather_sems(groups, chunks)
        + gather_sems(groups, chunks),
        compiler_params=pltpu.CompilerParams(
            collective_id=collective_id, has_side_effects=True, vmem_limit_bytes=50 << 20
        ),
        cost_estimate=pl.CostEstimate(flops=0, bytes_accessed=4 << 20, transcendentals=0),
    )(rows, small, heads, *weights)
    if pair:
        gate = (lows[0], lows[-1], lows[count], swap_layers(lows[-1]))
        lone = [
            layers_in_order(own, other.reshape(own.shape))
            for own, other in zip(lows[3:count], lows[count + 1 : -1])
        ]
    else:
        lone = [whole_over_layers(own) for own in lows[3:]]
        heads_out = lax.all_gather(heads_out, "fsdp", axis=1, tiled=True)
        gate = halves_over_layers(lows[0])
    return (
        rows_out.reshape(groups * rows.shape[0], rows.shape[1]),
        small_out.reshape(groups * height, small.shape[1]),
        heads_out,
        (gate, halves_over_layers(lows[1]), halves_over_layers(lows[2])),
        lone,
    )


class Piece:
    def __init__(self, source, buffer, load_sem, products):
        self.load = pltpu.make_async_copy(source, buffer, load_sem)
        self.products = products


class Products:
    def __init__(self, held, pieces):
        self.held, self.pieces = held, pieces
        self.jobs = [(piece, which) for piece in pieces for which in range(len(piece.products))]
        self.at, self.busy = 0, {}

    def begin(self):
        for copy in self.held:
            copy.start()
        for piece in self.pieces[:2]:
            piece.load.start()

    def step(self):
        if self.at >= len(self.jobs):
            return
        piece, which = self.jobs[self.at]
        if self.at == 0:
            for copy in self.held:
                copy.wait()
        if which == 0:
            piece.load.wait()
        compute, key, stage, store = piece.products[which]
        if key in self.busy:
            self.busy[key].wait()
        stage[...] = compute()
        store.start()
        self.busy[key] = store
        self.at += 1
        if which == len(piece.products) - 1:
            later = self.pieces.index(piece) + 2
            if later < len(self.pieces):
                self.pieces[later].load.start()

    def finish(self):
        while self.at < len(self.jobs):
            self.step()
        for store in self.busy.values():
            store.wait()


class GradProducts:
    tile = 256

    def __init__(self, pair, shapes):
        self.pair = pair
        self.rows, self.width = shapes[0]
        self.units, self.tokens, self.columns = shapes[1][1], shapes[3][0], shapes[4][1]

    def outs(self):
        shared = [(self.width, self.columns), (self.columns // 2, self.width)]
        experts = [(self.width // 2, self.units)] * 2 if self.pair else []
        return [jax.ShapeDtypeStruct(shape, F32) for shape in experts + shared]

    def counts(self):
        experts = self.width // 2 // self.tile if self.pair else 0
        return experts, self.width // self.tile

    def scratch(self):
        experts, shared = self.counts()
        dma, tile = pltpu.SemaphoreType.DMA, self.tile
        scratch = [
            pltpu.VMEM((self.tokens, self.columns), LOW),
            pltpu.VMEM((self.tokens, self.columns // 2), LOW),
            pltpu.VMEM((2, self.tokens, tile), LOW),
            pltpu.VMEM((2, tile, self.columns), F32),
            pltpu.VMEM((2, self.columns // 2, tile), F32),
            dma((4,)),
            dma((experts + 2 * shared,)),
            dma((2 * experts + 2 * shared,)),
        ]
        if self.pair:
            scratch += [
                pltpu.VMEM((self.rows, self.units), LOW),
                pltpu.VMEM((self.rows, self.units), LOW),
                pltpu.VMEM((2, self.rows, tile), LOW),
                pltpu.VMEM((2, tile, self.units), F32),
            ]
        return scratch

    def build(self, ins, outs, scratch):
        rows_ref, gate_ref, up_ref, two_ref, dproj_ref, hs_ref, grads_ref = ins
        dproj, hs, pieces_buf, in_stage, out_stage, held_sems, load_sems, store_sems, *rest = scratch
        tile = self.tile
        held = [
            pltpu.make_async_copy(dproj_ref, dproj, held_sems.at[0]),
            pltpu.make_async_copy(hs_ref, hs, held_sems.at[1]),
        ]
        pieces, stored = [], 0
        experts, shared = self.counts()

        def columns(ref, index, base=0):
            return ref.at[:, pl.ds(pl.multiple_of(base + index * tile, tile), tile)]

        if self.pair:
            gate, up, slots, stage = rest
            held += [
                pltpu.make_async_copy(gate_ref, gate, held_sems.at[2]),
                pltpu.make_async_copy(up_ref, up, held_sems.at[3]),
            ]
            base = lax.axis_index("fsdp") * (self.width // 2)
            for index in range(experts):
                slot = slots.at[index % 2]
                products = []
                for number, right in enumerate((gate, up)):
                    target = outs[number].at[pl.ds(index * tile, tile)]
                    products.append(
                        (
                            functools.partial(lambda a, b: t_dot(a[...], b[...]), slot, right),
                            ("e", number),
                            stage.at[number],
                            pltpu.make_async_copy(stage.at[number], target, store_sems.at[stored]),
                        )
                    )
                    stored += 1
                pieces.append(
                    Piece(columns(rows_ref, index, base), slot, load_sems.at[len(pieces)], products)
                )
        for index in range(shared):
            slot, stage = pieces_buf.at[index % 2], in_stage.at[index % 2]
            target = outs[-2].at[pl.ds(index * tile, tile)]
            product = (
                functools.partial(lambda a, b: t_dot(a[...], b[...]), slot, dproj),
                ("i", index % 2),
                stage,
                pltpu.make_async_copy(stage, target, store_sems.at[stored]),
            )
            stored += 1
            pieces.append(Piece(columns(two_ref, index), slot, load_sems.at[len(pieces)], [product]))
        for index in range(shared):
            slot, stage = pieces_buf.at[index % 2], out_stage.at[index % 2]
            product = (
                functools.partial(lambda a, b: t_dot(b[...], a[...]), slot, hs),
                ("o", index % 2),
                stage,
                pltpu.make_async_copy(stage, columns(outs[-1], index), store_sems.at[stored]),
            )
            stored += 1
            pieces.append(Piece(columns(grads_ref, index), slot, load_sems.at[len(pieces)], [product]))
        return Products(held, pieces)


class Later:
    def __init__(self, laterfn, chunks, size, extras, outs, ready):
        self.todo = [pl.ds(chunk * size, size) for chunk in range(chunks)]
        self.run = functools.partial(laterfn, extras=extras, outs=outs, ready=ready)

    def step(self):
        if self.todo:
            self.run(self.todo.pop(0))

    def finish(self):
        while self.todo:
            self.step()


class HeadGrads:
    def __init__(
        self, groups, pair, swaps, grads_ref, out_ref, came, total, y_sems, send, recv, own_sem, swap_sems
    ):
        self.swaps, self.swap_sems = swaps, swap_sems
        self.pair, self.grads, self.out = pair, grads_ref, out_ref
        self.came, self.total, self.y_sems, self.own_sem = came, total, y_sems, own_sem
        self.mine = lax.axis_index("fsdp") if pair else 0
        self.groups = groups
        self.me = lax.axis_index("seq")
        self.spread = Exchange(groups, total, lambda index: out_ref.at[index], (send, recv))

    def cross(self):
        return across(self.grads.at[1 - self.mine], self.came, self.y_sems.at[0], self.y_sems.at[1])

    def swap(self, index):
        source, target = self.swaps[index]
        return across(source, target, self.swap_sems.at[0, index], self.swap_sems.at[1, index])

    def begin(self):
        if self.pair:
            self.cross().start()
            for index in range(len(self.swaps)):
                self.swap(index).start()

    def middle(self):
        if self.pair:
            self.cross().wait_recv()
            total = self.grads[self.mine].astype(F32) + self.came[...].astype(F32)
            self.total[...] = total.astype(LOW)
        else:
            self.total[...] = self.grads[0]
        self.spread.begin()
        self.local = pltpu.make_async_copy(
            self.total.at[self.me], self.out.at[self.me], self.own_sem
        )
        self.local.start()

    def finish(self):
        for turn in range(1, self.groups):
            self.spread.arrived(turn)
        self.spread.finish()
        self.local.wait()
        if self.pair:
            self.cross().wait_send()
            for index in range(len(self.swaps)):
                self.swap(index).wait_send()
                self.swap(index).wait_recv()


def reduce_kernel(
    groups, chunks, extras, outs, rowfn, laterfn, gathers, heads, grads, swap_count, product, *refs
):
    parts_ref = refs[0]
    if product:
        right_ref, refs = refs[1], refs[:1] + refs[2:]
    extra_refs = refs[1 : 1 + extras]
    if heads is not None:
        heads_ref, refs = refs[1 + extras], refs[: 1 + extras] + refs[2 + extras :]
        swap_ins = refs[1 + extras : 1 + extras + swap_count]
        refs = refs[: 1 + extras] + refs[1 + extras + swap_count :]
    beside = None
    if grads is not None:
        beside_ins, refs = refs[1 + extras : 8 + extras], refs[: 1 + extras] + refs[8 + extras :]
    out_refs = refs[1 + extras : 1 + extras + outs]
    rest = list(refs[1 + extras + outs :])
    if heads is not None:
        head_out = rest.pop(0)
        swaps, rest = list(zip(swap_ins, rest[:swap_count])), rest[swap_count:]
    if product:
        side_made = rest.pop()
    if grads is not None:
        count = len(grads.outs())
        beside_outs, rest = rest[:count], rest[count:]
        count = len(grads.scratch())
        beside = grads.build(beside_ins, beside_outs, rest[-count:])
        rest = rest[:-count]
        beside.begin()
    gather_ref = rest.pop(0) if gathers else None
    own, side, came, sent = rest[:4]
    own_sem, side_send, side_recv, send_sem, recv_sem = rest[4:9]
    ready = rest[9] if gathers else None
    rows = own.shape[1]
    size = rows // chunks
    ring, steps = groups // 2, groups // 4
    spot, core, at = ring_places(groups)
    sibling = {"seq": at(spot, 1 - core)}
    if heads is None:
        enter((at(spot - 1, core), at(spot + 1, core), at(spot, 1 - core)))
    else:
        head_grads = HeadGrads(groups, heads, swaps, heads_ref, head_out, *rest[-7:])
        enter_all(groups, heads)
        head_grads.begin()

    order = []
    for step in range(steps):
        order.append(steps - step)
        if step:
            order.append(ring - steps + step)
    order.append(0)
    started = []
    loads = {}

    def prepare(far):
        if product:

            def block(index):
                part = pl.ds(pl.multiple_of(index * rows, rows), rows)
                return dot(parts_ref[part], right_ref[...]).astype(LOW)

            side_made[far] = block(at(spot + far, 1 - core))
            source = side_made.at[far]
        else:
            source = parts_ref.at[at(spot + far, 1 - core)]
        copy = pltpu.make_async_remote_copy(
            src_ref=source,
            dst_ref=side.at[far],
            send_sem=side_send.at[far],
            recv_sem=side_recv.at[far],
            device_id=sibling,
            device_id_type=MESH,
        )
        copy.start()
        started.append(copy)
        if product:
            own[far] = block(at(spot + far, core))
            loads[far] = (None, copy)
            return
        load = pltpu.make_async_copy(
            parts_ref.at[at(spot + far, core)], own.at[far], own_sem.at[far]
        )
        load.start()
        loads[far] = (load, copy)

    if not product:
        for far in order:
            prepare(far)
    here = set()

    def both(far, chunk):
        if far not in here:
            here.add(far)
            if loads[far][0] is not None:
                loads[far][0].wait()
            loads[far][1].wait_recv()
        part = pl.ds(chunk * size, size)
        return own[far, part].astype(F32) + side[far, part].astype(F32)

    def neighbour_copy(way, step, chunk):
        part = pl.ds(chunk * size, size)
        return pltpu.make_async_remote_copy(
            src_ref=sent.at[way, step, part],
            dst_ref=came.at[way, step, part],
            send_sem=send_sem.at[way, step, chunk],
            recv_sem=recv_sem.at[way, step, chunk],
            device_id={"seq": at(spot + (1 if way == 0 else -1), core)},
            device_id_type=MESH,
        )

    def half(way, chunk):
        return (chunk < chunks // 2) == (way == 0)

    if product:
        prepare(steps)
    for step in range(steps):
        if product and step:
            prepare(steps - step)
            prepare(ring - steps + step)
        for chunk in range(chunks):
            for way in range(2):
                if step == 0 and not half(way, chunk):
                    continue
                far = steps - step if way == 0 else ring - (steps - step)
                part = pl.ds(chunk * size, size)
                total = both(far, chunk)
                if step > 1 or (step == 1 and half(way, chunk)):
                    neighbour_copy(way, step - 1, chunk).wait_recv()
                    total = total + came[way, step - 1, part].astype(F32)
                sent[way, step, part] = total.astype(sent.dtype)
                copy = neighbour_copy(way, step, chunk)
                copy.start()
                started.append(copy)
                if beside is not None and step and chunk == chunks - 1:
                    beside.step()
    if product:
        prepare(0)
    if heads is not None:
        head_grads.middle()
    gather = Gather(groups, chunks, rows, ready, gather_ref, rest[10:14]) if gathers else None
    for chunk in range(chunks):
        part = pl.ds(chunk * size, size)
        total = both(0, chunk)
        for way in range(2):
            if steps > 1 or half(way, chunk):
                neighbour_copy(way, steps - 1, chunk).wait_recv()
                total = total + came[way, steps - 1, part].astype(F32)
        made = rowfn(total, part, extra_refs, out_refs)
        if gathers:
            ready[part] = made
            gather.begin(chunk)
    if gathers:
        local = pltpu.make_async_copy(ready, gather_ref.at[at(spot, core)], rest[14])
        local.start()
        if laterfn is not None:
            beside = Later(laterfn, chunks, size, extra_refs, out_refs, ready)
        gather.run(beside)
        gather.finish()
        local.wait()
    if beside is not None:
        beside.finish()
    if heads is not None:
        head_grads.finish()
    for copy in started:
        copy.wait_send()


def ring_reduce(
    parts, extras, outs, rowfn, groups, collective_id, gathers=None, heads=None, grads=None,
    grad_ins=(), swaps=(), right=None, laterfn=None, chunks=4,
):
    if right is None:
        _, rows, columns = parts.shape
    else:
        rows, columns = parts.shape[0] // groups, right.shape[1]
    ring, steps = groups // 2, groups // 4
    scratch = [
        pltpu.VMEM((ring, rows, columns), LOW),
        pltpu.VMEM((ring, rows, columns), LOW),
        pltpu.VMEM((2, steps, rows, columns), LOW),
        pltpu.VMEM((2, steps, rows, columns), LOW),
        pltpu.SemaphoreType.DMA((ring,)),
        pltpu.SemaphoreType.DMA((ring,)),
        pltpu.SemaphoreType.DMA((ring,)),
        pltpu.SemaphoreType.DMA((2, steps, chunks)),
        pltpu.SemaphoreType.DMA((2, steps, chunks)),
    ]
    shapes = list(outs)
    specs = [pl.BlockSpec(memory_space=pltpu.VMEM)] * len(outs)
    extras = list(extras)
    count = len(extras)
    pair = None
    if heads is not None:
        pair = heads.shape[0] == 2
        extras.append(heads)
        shapes.append(jax.ShapeDtypeStruct(heads.shape[1:], LOW))
        specs.append(pl.BlockSpec(memory_space=pltpu.VMEM))
    any_spec = pl.BlockSpec(memory_space=pl.ANY)
    for array in swaps:
        shapes.append(jax.ShapeDtypeStruct(array.shape, LOW))
        specs.append(any_spec)
    if grads is not None:
        shapes += grads.outs()
        specs += [any_spec] * len(grads.outs())
    if gathers is not None:
        shapes.append(jax.ShapeDtypeStruct((groups, rows, gathers), LOW))
        specs.append(pl.BlockSpec(memory_space=pl.ANY))
        scratch.append(pltpu.VMEM((rows, gathers), LOW))
        scratch += gather_sems(groups, chunks)
        scratch.append(pltpu.SemaphoreType.DMA)
    if heads is not None:
        scratch += [pltpu.VMEM(heads.shape[1:], LOW)] * 2
        scratch += [pltpu.SemaphoreType.DMA((2,))]
        scratch += [pltpu.SemaphoreType.DMA((groups,))] * 2
        scratch += [pltpu.SemaphoreType.DMA, pltpu.SemaphoreType.DMA((2, max(1, len(swaps))))]
    if grads is not None:
        scratch += grads.scratch()
    if right is not None:
        scratch.append(pltpu.VMEM((ring, rows, columns), LOW))
    return pl.pallas_call(
        functools.partial(
            reduce_kernel, groups, chunks, count, len(outs), rowfn, laterfn, gathers is not None, pair, grads,
            len(swaps), right is not None,
        ),
        out_shape=shapes,
        in_specs=(
            [any_spec] if right is None else [pl.BlockSpec(memory_space=pltpu.VMEM)] * 2
        )
        + [pl.BlockSpec(memory_space=pltpu.VMEM)] * len(extras)
        + [any_spec] * (len(swaps) + len(grad_ins)),
        out_specs=specs,
        scratch_shapes=scratch,
        compiler_params=pltpu.CompilerParams(
            collective_id=collective_id, has_side_effects=True, vmem_limit_bytes=50 << 20
        ),
        cost_estimate=pl.CostEstimate(
            flops=0, bytes_accessed=4 << 20, transcendentals=0
        ),
    )(parts, *([] if right is None else [right]), *extras, *swaps, *grad_ins)


def attend_kernel(blocks, q_ref, k_ref, v_ref, col_ref, row_ref, out_ref, log_ref):
    size = q_ref.shape[0] // blocks
    scale = (NOPE + ROPE) ** (-0.5)
    for index in range(blocks):
        part = pl.ds(index * size, size)
        reach = (index + 1) * size
        scores = dot_t(q_ref[part], k_ref[:reach]) * scale
        rows = index * size + lax.broadcasted_iota(jnp.int32, (size, reach), 0)
        columns = lax.broadcasted_iota(jnp.int32, (size, reach), 1)
        allowed = (col_ref[part] == row_ref[:, :reach]) & (rows >= columns)
        scores = jnp.where(allowed, scores, -1e30)
        peak = jnp.max(scores, axis=-1, keepdims=True)
        raised = jnp.exp(scores - peak)
        total = jnp.sum(raised, axis=-1, keepdims=True)
        weights = (raised * (1.0 / total)).astype(LOW)
        out_ref[part] = dot(weights, v_ref[:reach]).astype(LOW)
        log_ref[part] = peak + jnp.log(total)


def attend_forward(head_q, head_k, head_v, doc_ids):
    seq_len = head_q.shape[0]
    return pl.pallas_call(
        functools.partial(attend_kernel, seq_len // 256),
        out_shape=[
            jax.ShapeDtypeStruct((seq_len, VD), LOW),
            jax.ShapeDtypeStruct((seq_len, 1), F32),
        ],
        compiler_params=pltpu.CompilerParams(vmem_limit_bytes=50 << 20),
        cost_estimate=pl.CostEstimate(
            flops=seq_len * seq_len * 400, bytes_accessed=4 << 20, transcendentals=seq_len * seq_len // 2
        ),
    )(head_q, head_k, head_v, doc_ids[:, None], doc_ids[None, :])


def attend_back_kernel(
    blocks, q_ref, k_ref, v_ref, g_ref, col_ref, row_ref, log_ref, dq_ref, dk_ref, dv_ref, ksum, vsum
):
    size = q_ref.shape[0] // blocks
    scale = (NOPE + ROPE) ** (-0.5)
    ksum[...] = jnp.zeros_like(ksum)
    vsum[...] = jnp.zeros_like(vsum)
    for index in range(blocks):
        part = pl.ds(index * size, size)
        reach = (index + 1) * size
        query, grad = q_ref[part], g_ref[part]
        scores = dot_t(k_ref[:reach], query) * scale
        keys = lax.broadcasted_iota(jnp.int32, (reach, size), 0)
        rows = index * size + lax.broadcasted_iota(jnp.int32, (reach, size), 1)
        allowed = (col_ref[:reach] == row_ref[:, part]) & (rows >= keys)
        weights = jnp.exp(jnp.where(allowed, scores, -1e30) - log_ref[:, part])
        vsum[:reach] += dot(weights.astype(LOW), grad)
        slopes = dot_t(v_ref[:reach], grad)
        inner = jnp.sum(weights * slopes, axis=0, keepdims=True)
        back = (weights * (slopes - inner)).astype(LOW)
        ksum[:reach] += dot(back, query)
        dq_ref[part] = (t_dot(back, k_ref[:reach]) * scale).astype(LOW)
    dk_ref[...] = (ksum[...] * scale).astype(LOW)
    dv_ref[...] = vsum[...].astype(LOW)


def attend_backward(head_q, head_k, head_v, doc_ids, logs, head_g):
    seq_len = head_q.shape[0]
    return pl.pallas_call(
        functools.partial(attend_back_kernel, seq_len // 256),
        out_shape=[
            jax.ShapeDtypeStruct((seq_len, NOPE + ROPE), LOW),
            jax.ShapeDtypeStruct((seq_len, NOPE + ROPE), LOW),
            jax.ShapeDtypeStruct((seq_len, VD), LOW),
        ],
        scratch_shapes=[
            pltpu.VMEM((seq_len, NOPE + ROPE), F32),
            pltpu.VMEM((seq_len, VD), F32),
        ],
        compiler_params=pltpu.CompilerParams(vmem_limit_bytes=56 << 20),
        cost_estimate=pl.CostEstimate(
            flops=seq_len * seq_len * 1000, bytes_accessed=6 << 20, transcendentals=seq_len * seq_len // 2
        ),
    )(head_q, head_k, head_v, head_g, doc_ids[:, None], doc_ids[None, :], logs.reshape(1, seq_len))


def swapped(values):
    half = values.shape[-1] // 2
    return jnp.concatenate([values[:, half:], values[:, :half]], axis=-1)


def project_kernel(
    x_ref, gain_ref, wq_ref, wl_ref, gain_lat_ref, we_ref, table_ref,
    one_ref, q_ref, k_ref, v_ref, m_ref, c_ref,
):
    one = norm_forward(x_ref[...].astype(F32), gain_ref[...])[0].astype(LOW)
    one_ref[...] = one
    cosine, sine = table_ref[:, :ROPE], table_ref[:, ROPE:]
    query = dot(one, wq_ref[:, : NOPE + ROPE])
    turned = query[:, NOPE:]
    q_ref[:, :NOPE] = query[:, :NOPE].astype(LOW)
    q_ref[:, NOPE:] = (turned * cosine + swapped(turned) * sine).astype(LOW)
    latent = dot(one, wl_ref[...])
    turned = latent[:, LAT : LAT + ROPE]
    k_ref[:, NOPE:] = (turned * cosine + swapped(turned) * sine).astype(LOW)
    c_ref[...] = latent[:, :LAT]
    scaled = norm_forward(latent[:, :LAT], gain_lat_ref[...])[0].astype(LOW)
    m_ref[...] = scaled
    expanded = dot(scaled, we_ref[...])
    k_ref[:, :NOPE] = expanded[:, :NOPE].astype(LOW)
    v_ref[...] = expanded[:, NOPE:].astype(LOW)


def project(rows, gain, query_w, small, gain_latent, expand_w, table, tile=256):
    seq_len, width = rows.shape

    def cut(columns):
        return pl.BlockSpec((tile, columns), lambda i: (i, 0))

    def whole(array):
        return pl.BlockSpec(array.shape, lambda i: (0, 0))

    outs = [(width, LOW), (NOPE + ROPE, LOW), (NOPE + ROPE, LOW), (VD, LOW), (LAT, LOW), (LAT, F32)]
    return pl.pallas_call(
        project_kernel,
        grid=(seq_len // tile,),
        out_shape=[jax.ShapeDtypeStruct((seq_len, c), t) for c, t in outs],
        in_specs=[
            cut(width), whole(gain), whole(query_w), whole(small), whole(gain_latent),
            whole(expand_w), cut(2 * ROPE),
        ],
        out_specs=[cut(c) for c, _ in outs],
        compiler_params=pltpu.CompilerParams(vmem_limit_bytes=50 << 20),
        cost_estimate=pl.CostEstimate(
            flops=seq_len * width * 1800, bytes_accessed=28 << 20, transcendentals=0
        ),
    )(rows, gain, query_w, small, gain_latent, expand_w, table)


def project_back_kernel(
    dq_ref, dk_ref, dv_ref, table_ref, one_ref, m_ref, wq_ref, we_ref,
    parts_ref, gq_ref, ge_ref, dq_low, de_low,
):
    cosine, sine = table_ref[:, :ROPE], table_ref[:, ROPE:]
    turned = dq_ref[:, NOPE:].astype(F32)
    dq_low[:, :NOPE] = dq_ref[:, :NOPE]
    dq_low[:, NOPE:] = (turned * cosine - swapped(turned) * sine).astype(LOW)
    de_low[:, :NOPE] = dk_ref[:, :NOPE]
    de_low[:, NOPE:] = dv_ref[...]
    blocks, rows, wide = parts_ref.shape
    width, last = one_ref.shape[1], LAT + ROPE
    parts_ref[:, :, :width] = dot_t(dq_low[...], wq_ref[:, : NOPE + ROPE]).astype(LOW).reshape(blocks, rows, width)
    parts_ref[:, :, width : width + LAT] = (
        dot_t(de_low[...], we_ref[...]).astype(LOW).reshape(blocks, rows, LAT)
    )
    parts_ref[:, :, width + LAT : width + last] = dk_ref[:, NOPE:].reshape(blocks, rows, ROPE)
    parts_ref[:, :, width + last :] = jnp.zeros((blocks, rows, wide - width - last), LOW)

    @pl.when(pl.program_id(0) == 0)
    def _():
        gq_ref[...] = jnp.zeros_like(gq_ref)
        ge_ref[...] = jnp.zeros_like(ge_ref)

    gq_ref[...] += t_dot(one_ref[...], dq_low[...])
    ge_ref[...] += t_dot(m_ref[...], de_low[...])


def project_back(grads, table, one_low, latent_low, query_w, expand_w, tok_rows, tile=256):
    seq_len, width = one_low.shape
    wide = width + LAT + 2 * ROPE

    def cut(columns):
        return pl.BlockSpec((tile, columns), lambda i: (i, 0))

    def whole(shape):
        return pl.BlockSpec(shape, lambda i: (0, 0))

    return pl.pallas_call(
        project_back_kernel,
        grid=(seq_len // tile,),
        out_shape=[
            jax.ShapeDtypeStruct((seq_len // tok_rows, tok_rows, wide), LOW),
            jax.ShapeDtypeStruct((width, NOPE + ROPE), F32),
            jax.ShapeDtypeStruct(expand_w.shape, F32),
        ],
        in_specs=[
            cut(NOPE + ROPE), cut(NOPE + ROPE), cut(VD), cut(2 * ROPE), cut(width), cut(LAT),
            whole(query_w.shape), whole(expand_w.shape),
        ],
        out_specs=[
            pl.BlockSpec((tile // tok_rows, tok_rows, wide), lambda i: (i, 0, 0)),
            whole((width, NOPE + ROPE)),
            whole(expand_w.shape),
        ],
        scratch_shapes=[pltpu.VMEM((tile, NOPE + ROPE), LOW), pltpu.VMEM((tile, NOPE + VD), LOW)],
        compiler_params=pltpu.CompilerParams(vmem_limit_bytes=50 << 20),
        cost_estimate=pl.CostEstimate(
            flops=seq_len * width * 1300, bytes_accessed=28 << 20, transcendentals=0
        ),
    )(*grads, table, one_low, latent_low, query_w, expand_w)


def blocks_of(ref, count):
    size = ref.shape[0] // count
    return [pl.ds(block * size, size) for block in range(count)]


def two_parts(values):
    high = values.astype(LOW)
    return high, (values - high.astype(F32)).astype(LOW)


class Weights:
    def __init__(self, pair, counts, refs, wholes, sems):
        self.copies, at, number = [], 0, 0
        first = lax.axis_index("fsdp") if pair else 0
        for whole, pieces in zip(wholes, counts):
            half, done, copies = whole.shape[0] // 2, 0, []
            for piece in refs[at : at + pieces]:
                side, offset = done // half, done % half
                start = (first if side == 0 else 1 - first) * half + offset
                place = pl.ds(pl.multiple_of(start, 64), piece.shape[0])
                copies.append(pltpu.make_async_copy(piece, whole.at[place], sems.at[number]))
                number += 1
                done += piece.shape[0]
            self.copies.append(copies)
            at += pieces

    def on_first(self, act):
        @pl.when(pl.program_id(0) == 0)
        def _():
            act()

    def begin(self, order):
        self.on_first(lambda: [copy.start() for which in order for copy in self.copies[which]])

    def ready(self, which):
        self.on_first(lambda: [copy.wait() for copy in self.copies[which]])


def ffn_kernel(
    pair, counts, rows_ref, chosen_ref, mine_ref, router_ref, wi_ref, wo_ref, *refs,
):
    pieces = sum(counts)
    parts, refs = refs[:pieces], refs[pieces:]
    (
        probs_ref, slot_gate_ref, in_ref, gate_ref, up_ref, inner_ref, made_ref, proj_ref, hs_ref,
        out_ref, spread, wg_ref, wu_ref, wd_ref, sems,
    ) = refs
    count = 4
    weights = Weights(pair, counts, parts, (wg_ref, wu_ref, wd_ref), sems)
    weights.begin((0, 1, 2))
    tokens, slots = blocks_of(rows_ref, count), blocks_of(chosen_ref, count)
    lanes = lax.broadcasted_iota(jnp.int32, mine_ref.shape, 1)
    logits = jnp.where(mine_ref[1:2] > 0, dot(rows_ref[...], router_ref[...]), -1e30)
    raised = jnp.exp(logits - jnp.max(logits, axis=-1, keepdims=True))
    probs = raised / jnp.sum(raised, axis=-1, keepdims=True)
    probs_ref[...] = probs
    high, rest = two_parts(jnp.sum(probs * mine_ref[0:1], axis=-1, keepdims=True))
    high, rest = high.astype(F32), rest.astype(F32)
    columns = jnp.where(lanes[0:1] == 0, high, jnp.where(lanes[0:1] == 1, rest, 0.0)).astype(LOW)
    for token, slot in zip(tokens, slots):
        size = token.size
        picked = columns[token.start : token.start + size]
        chosen = chosen_ref[slot]
        slot_gate_ref[slot] = jnp.sum(dot(chosen, picked), axis=-1, keepdims=True)
        in_ref[slot] = dot(chosen, rows_ref[token]).astype(LOW)
    weights.ready(0)
    gate = dot(in_ref[...], wg_ref[...])
    weights.ready(1)
    up = dot(in_ref[...], wu_ref[...])
    gate_ref[...] = gate
    up_ref[...] = up
    inner_ref[...] = (gate * jax.nn.sigmoid(gate) * up).astype(LOW)
    weights.ready(2)
    made = dot(inner_ref[...], wd_ref[...]).astype(LOW)
    made_ref[...] = made
    spread[...] = (slot_gate_ref[...] * made.astype(F32)).astype(LOW)
    proj = dot(rows_ref[...], wi_ref[...])
    proj_ref[...] = proj
    half = proj.shape[1] // 2
    gate, up = proj[:, :half], proj[:, half:]
    hs_ref[...] = (gate * jax.nn.sigmoid(gate) * up).astype(LOW)
    for token, slot in zip(tokens, slots):
        total = t_dot(chosen_ref[slot], spread[slot]) + dot(hs_ref[token], wo_ref[...])
        out_ref[token] = total.astype(LOW)


def ffn_back_kernel(
    pair, counts, grads_ref, chosen_ref, mine_ref, slot_gate_ref, made_ref, gate_ref, up_ref,
    proj_ref, wi_ref, wo_ref, *refs,
):
    pieces = sum(counts)
    parts, refs = refs[:pieces], refs[pieces:]
    dy_ref, dgate_ref, dup_ref, dproj_ref, parts_ref, spread, wg_ref, wu_ref, wd_ref, sems = refs
    count = 4
    width = grads_ref.shape[1]
    weights = Weights(pair, counts, parts, (wg_ref, wu_ref, wd_ref), sems)
    weights.begin((2, 0, 1))
    tokens, slots = blocks_of(grads_ref, count), blocks_of(chosen_ref, count)
    mine, shifted = mine_ref[0:1], mine_ref[2:3]
    for token, slot in zip(tokens, slots):
        picked = dot(chosen_ref[slot], grads_ref[token])
        dy_ref[slot] = (slot_gate_ref[slot] * picked).astype(LOW)
        score = jnp.sum(picked * made_ref[slot].astype(F32), axis=-1, keepdims=True)
        high, rest = two_parts(score)
        spread[slot, width:] = (high.astype(F32) * mine + rest.astype(F32) * shifted).astype(LOW)
    weights.ready(2)
    inner = dot_t(dy_ref[...], wd_ref[...])
    gate = gate_ref[...]
    sigmoid = jax.nn.sigmoid(gate)
    dgate_ref[...] = (inner * up_ref[...] * swish_slope(gate, sigmoid)).astype(LOW)
    dup_ref[...] = (inner * gate * sigmoid).astype(LOW)
    weights.ready(0)
    weights.ready(1)
    back = dot_t(dgate_ref[...], wg_ref[...]) + dot_t(dup_ref[...], wu_ref[...])
    spread[:, :width] = back.astype(LOW)
    half = proj_ref.shape[1] // 2
    gate, up = proj_ref[:, :half], proj_ref[:, half:]
    sigmoid = jax.nn.sigmoid(gate)
    inner = dot_t(grads_ref[...], wo_ref[...])
    dproj_ref[:, :half] = (inner * up * swish_slope(gate, sigmoid)).astype(LOW)
    dproj_ref[:, half:] = (inner * gate * sigmoid).astype(LOW)
    for block, (token, slot) in enumerate(zip(tokens, slots)):
        total = t_dot(chosen_ref[slot], spread[slot])
        parts_ref[block, :, :width] = (
            total[:, :width] + dot_t(dproj_ref[token], wi_ref[...])
        ).astype(LOW)
        parts_ref[block, :, width:] = total[:, width:].astype(LOW)


def row_grid(kernel, steps, cuts, outs, scratch, flops):
    def cut(shape):
        rest = (0,) * (len(shape) - 1)
        return pl.BlockSpec((shape[0] // steps,) + tuple(shape[1:]), lambda i: (i,) + rest)

    def whole(shape):
        rest = (0,) * len(shape)
        return pl.BlockSpec(tuple(shape), lambda i: rest, pipeline_mode=pl.Buffered(1))

    operands = [array for array, _ in cuts]
    return pl.pallas_call(
        kernel,
        grid=(steps,),
        out_shape=outs,
        in_specs=[
            pl.BlockSpec(memory_space=pl.ANY)
            if fixed is None
            else whole(a.shape) if fixed else cut(a.shape)
            for a, fixed in cuts
        ],
        out_specs=[cut(o.shape) for o in outs],
        scratch_shapes=scratch,
        compiler_params=pltpu.CompilerParams(vmem_limit_bytes=60 << 20),
        cost_estimate=pl.CostEstimate(flops=flops, bytes_accessed=60 << 20, transcendentals=0),
    )(*operands)


def grad_in_kernel(layer_ref, rows_ref, grads_ref, sent_ref):
    sent_ref[...] = t_dot(rows_ref[...], grads_ref[...]).astype(LOW)


def grad_in(rows, grads, tile=512):
    count, width = rows.shape
    columns = grads.shape[1]
    half = width // 2 // tile
    layer = lax.axis_index("fsdp").reshape(1)
    return pl.pallas_call(
        grad_in_kernel,
        grid_spec=pltpu.PrefetchScalarGridSpec(
            num_scalar_prefetch=1,
            grid=(half,),
            in_specs=[
                pl.BlockSpec((count, tile), lambda i, layer: (0, i + (1 - layer[0]) * half)),
                pl.BlockSpec((count, columns), lambda i, _: (0, 0)),
            ],
            out_specs=pl.BlockSpec((tile, columns), lambda i, _: (i, 0)),
        ),
        out_shape=jax.ShapeDtypeStruct((width // 2, columns), LOW),
        compiler_params=pltpu.CompilerParams(vmem_limit_bytes=50 << 20),
        cost_estimate=pl.CostEstimate(
            flops=count * width * columns, bytes_accessed=10 << 20, transcendentals=0
        ),
    )(layer, rows, grads)


def grad_out_kernel(layer_ref, inner_ref, grads_ref, sent_ref, kept_ref, made):
    half = sent_ref.shape[0]
    layer = layer_ref[0]
    made[...] = t_dot(inner_ref[...], grads_ref[...])
    sent_ref[...] = made[pl.ds(pl.multiple_of((1 - layer) * half, 8), half)].astype(LOW)
    kept_ref[...] = made[pl.ds(pl.multiple_of(layer * half, 8), half)]


def grad_out(inner, grads, tile=512):
    count, units = inner.shape
    width = grads.shape[1]
    layer = lax.axis_index("fsdp").reshape(1)
    return pl.pallas_call(
        grad_out_kernel,
        grid_spec=pltpu.PrefetchScalarGridSpec(
            num_scalar_prefetch=1,
            grid=(width // tile,),
            in_specs=[
                pl.BlockSpec((count, units), lambda i, _: (0, 0)),
                pl.BlockSpec((count, tile), lambda i, _: (0, i)),
            ],
            out_specs=[
                pl.BlockSpec((units // 2, tile), lambda i, _: (0, i)),
                pl.BlockSpec((units // 2, tile), lambda i, _: (0, i)),
            ],
            scratch_shapes=[pltpu.VMEM((units, tile), F32)],
        ),
        out_shape=[
            jax.ShapeDtypeStruct((units // 2, width), LOW),
            jax.ShapeDtypeStruct((units // 2, width), F32),
        ],
        compiler_params=pltpu.CompilerParams(vmem_limit_bytes=50 << 20),
        cost_estimate=pl.CostEstimate(
            flops=2 * count * width * units, bytes_accessed=16 << 20, transcendentals=0
        ),
    )(layer, inner, grads)


def body(
    tokens,
    cotangent,
    segments,
    routes,
    norm_attn,
    w_query,
    w_latent,
    norm_latent,
    w_expand,
    w_output,
    norm_ffn,
    w_router,
    w_shared_gate,
    w_shared_up,
    w_shared_down,
    w_expert_gate,
    w_expert_up,
    w_expert_down,
):
    groups = lax.axis_size("seq")
    layers = lax.axis_size("fsdp")
    both = ("seq", "fsdp")
    place = lax.axis_index("seq")
    tok_rows, width = tokens.shape[1], tokens.shape[2]
    seq_len = segments.shape[1]
    own_rows = w_query.shape[0]
    lat_rows = w_expand.shape[0]
    experts = w_router.shape[1]
    capacity = tok_rows // 2
    query_width = NOPE + ROPE
    hidden_own = tokens[0].astype(F32)
    grad_own = cotangent[0].astype(F32)
    doc_ids = segments[0]

    lat_column = jnp.pad(norm_latent[:, None], ((0, own_rows - lat_rows), (0, 0)))
    at = LAT + ROPE
    route_columns = routes.reshape(own_rows, tok_rows * TOP // own_rows).astype(F32)
    packed = [w_latent, w_router, norm_attn[:, None], norm_ffn[:, None], lat_column, route_columns]
    packed = jnp.concatenate(packed, axis=1).astype(LOW)
    used = packed.shape[1]
    last = at + experts
    packed = jnp.pad(packed, ((0, 0), (0, -used % 128)))

    fold = lat_rows * (NOPE + VD) // own_rows
    query_parts = w_query.astype(LOW).reshape(own_rows, H, query_width).transpose(1, 0, 2)
    expand_parts = (
        w_expand.astype(LOW)
        .reshape(lat_rows, H, NOPE + VD)
        .transpose(1, 0, 2)
        .reshape(H, own_rows, fold)
    )
    head_parts = jnp.concatenate([query_parts, expand_parts], axis=2)
    hidden_low, small, head_parts, expert_sets, lone = gather_start(
        tokens[0],
        packed,
        head_parts,
        (
            w_expert_gate[0], w_expert_up[0], w_expert_down[0],
            w_shared_gate, w_shared_up, w_shared_down, w_output,
        ),
        groups,
        layers,
        1,
    )
    query_w = head_parts.reshape(width, query_width + fold)
    expand_w = head_parts[..., query_width:].reshape(LAT, NOPE + VD)
    router_w = jnp.pad(small[:, at:last], ((0, 0), (0, 128 - experts)))
    all_routes = small[:, last + 3 : used].reshape(groups, layers, -1)
    all_routes = lax.dynamic_index_in_dim(all_routes, lax.axis_index("fsdp"), 1, keepdims=False)
    all_routes = all_routes.reshape(groups, tok_rows, TOP)
    gains = small[:, last : last + 3].astype(F32).T
    gain_attn, gain_ffn = gains[0:1], gains[1:2]
    gain_latent = gains[2].reshape(groups * layers, own_rows)[:, :lat_rows].reshape(1, LAT)

    units = w_shared_gate.shape[1]
    padding = -units % 128
    spare = ((0, 0), (0, padding))
    shared_gate_w, shared_up_w, shared_down_w, output_w = lone
    shared_in_w = jnp.concatenate([jnp.pad(shared_gate_w, spare), jnp.pad(shared_up_w, spare)], axis=1)
    shared_down_w = jnp.pad(shared_down_w, ((0, padding), (0, 0)))

    grad_low = gather_rows(after(cotangent[0], hidden_low))

    table = jnp.asarray(rotary_table(seq_len))
    one_low, head_q, head_k, head_v, latent_low, latent_proj = project(
        hidden_low, gain_attn, query_w, small, gain_latent, expand_w, table
    )
    head_out, logs = attend_forward(head_q, head_k, head_v, doc_ids)
    def make_two(total, part, extras, outs):
        row_sum = extras[0][part].astype(F32) + total
        outs[0][part] = row_sum
        return norm_forward(row_sum, extras[1][...])[0].astype(LOW)

    own_shape = jax.ShapeDtypeStruct((tok_rows, width), F32)
    residual, two_low = ring_reduce(
        head_out, [tokens[0], gain_ffn], [own_shape], make_two, groups, 2, width, right=output_w
    )
    two_low = after(two_low, grad_low).reshape(seq_len, width)

    named = jnp.any(all_routes == place.astype(LOW), axis=-1)
    rank = jnp.cumsum(named.astype(jnp.int32), axis=1) - 1
    slots = jnp.arange(capacity, dtype=jnp.int32)
    chosen = named[:, None, :] & (rank[:, None, :] == slots[None, :, None])
    chosen = chosen.astype(LOW).reshape(groups * capacity, tok_rows)
    lanes = jnp.arange(128, dtype=jnp.int32)
    mine = jnp.stack(
        [(lanes == place), (lanes < experts), (lanes == place + experts)] + [lanes < 0] * 5
    ).astype(F32)
    slot_count, unit_count = groups * capacity, w_expert_gate.shape[2]
    expert_w = [(piece, None) for pieces in expert_sets for piece in pieces]
    counts = tuple(len(pieces) for pieces in expert_sets)
    expert_scratch = [
        pltpu.VMEM((width, unit_count), LOW),
        pltpu.VMEM((width, unit_count), LOW),
        pltpu.VMEM((unit_count, width), LOW),
        pltpu.SemaphoreType.DMA((len(expert_w),)),
    ]
    columns = shared_in_w.shape[1]

    def array(rows, columns, kind=LOW):
        return jax.ShapeDtypeStruct((rows, columns), kind)

    steps = groups // 4
    routed_flops = 6 * slot_count * width * unit_count
    probs, slot_gate, expert_in, gate_proj, up_proj, inner_low, made, shared_proj, shared_low, part_out = row_grid(
        functools.partial(ffn_kernel, layers == 2, counts),
        steps,
        [
            (two_low, False), (chosen, False), (mine, True), (router_w, True),
            (shared_in_w, True), (shared_down_w, True), *expert_w,
        ],
        [
            array(seq_len, 128, F32), array(slot_count, 1, F32), array(slot_count, width),
            array(slot_count, unit_count, F32), array(slot_count, unit_count, F32),
            array(slot_count, unit_count), array(slot_count, width), array(seq_len, columns, F32),
            array(seq_len, columns // 2), array(seq_len, width),
        ],
        [pltpu.VMEM((slot_count // steps, width), LOW)] + expert_scratch,
        routed_flops * 3 // 2,
    )
    ffn_out = scatter_rows(part_out).astype(F32)
    output = (residual + ffn_out).astype(LOW)

    made_grad, gate_grad, up_grad, shared_grads, part_grad = row_grid(
        functools.partial(ffn_back_kernel, layers == 2, counts),
        steps,
        [
            (grad_low, False), (chosen, False), (mine, True), (slot_gate, False), (made, False),
            (gate_proj, False), (up_proj, False), (shared_proj, False),
            (shared_in_w, True), (shared_down_w, True), *expert_w,
        ],
        [
            array(slot_count, width), array(slot_count, unit_count), array(slot_count, unit_count),
            array(seq_len, columns),
            jax.ShapeDtypeStruct((groups, tok_rows, width + 128), LOW),
        ],
        [pltpu.VMEM((slot_count // steps, width + 128), LOW)] + expert_scratch,
        routed_flops * 3 // 2,
    )

    if layers == 2:
        down_sent, down_kept = grad_out(inner_low, made_grad)
        gate_sent = grad_in(expert_in, gate_grad)
        up_sent = grad_in(expert_in, up_grad)
        part_grad = after(part_grad, down_sent, gate_sent, up_sent)
    else:
        down_kept, down_sent = spread_start(t_dot(inner_low, made_grad))
        gate_kept, gate_sent = spread_start(t_dot(expert_in, gate_grad))
        up_kept, up_sent = spread_start(t_dot(expert_in, up_grad))
    own_probs = lax.dynamic_slice_in_dim(probs, place * tok_rows, tok_rows, 0)

    def make_attn(total, part, extras, outs):
        probs = extras[0][part]
        score = total[:, width:]
        score = score + jnp.concatenate([score[:, experts:], score[:, :experts]], axis=1)
        logit = probs * (score - jnp.sum(probs * score, axis=-1, keepdims=True))
        high, rest = two_parts(logit)
        grad = total[:, :width] + dot_t(high, extras[4][...]) + dot_t(rest, extras[4][...])
        gain = extras[1][...]
        _, normed, factor = norm_forward(extras[2][part], gain)
        inner = grad * gain
        back = factor * (inner - normed * jnp.mean(inner * normed, axis=-1, keepdims=True))
        back = extras[3][part].astype(F32) + back
        outs[0][part] = back
        gain_sum = jnp.sum(grad * normed, axis=0, keepdims=True)
        outs[1][...] = gain_sum if part.start == 0 else outs[1][...] + gain_sum
        rest = rest.astype(F32)
        rest = jnp.concatenate([rest[:, 128 - experts :], rest[:, : 128 - experts]], axis=1)
        return jnp.concatenate([back, high.astype(F32) + rest], axis=1).astype(LOW)

    grad_ins = (expert_in, gate_grad, up_grad, two_low, shared_grads, shared_low, grad_low)
    grads = GradProducts(layers == 2, [array.shape for array in grad_ins])
    residual_grad, grad_gain_ffn, *made_grads, attn_grad = ring_reduce(
        part_grad,
        [own_probs, gain_ffn, residual, cotangent[0], router_w],
        [own_shape, jax.ShapeDtypeStruct((1, width), F32)],
        make_attn,
        groups,
        3,
        width + 128,
        None,
        grads,
        grad_ins,
    )
    shared_in_kept, shared_in_sent = spread_start(made_grads[-2])
    shared_down_kept, shared_down_sent = spread_start(made_grads[-1][:units])
    if layers == 2:
        gate_kept, up_kept = made_grads[:2]
    grad_expert_down = spread_end(down_kept, down_sent)
    grad_expert_gate = spread_end(gate_kept, gate_sent)
    grad_expert_up = spread_end(up_kept, up_sent)
    attn_grad = attn_grad.reshape(seq_len, width + 128)

    own_width = width // groups
    two_slice = lax.dynamic_slice_in_dim(two_low, place * own_width, own_width, 1)
    grad_router = t_dot(two_slice, attn_grad[:, width:])
    grad_router = grad_router[:, :experts] + grad_router[:, experts : 2 * experts]

    output_kept, output_sent = spread_start(t_dot(head_out, attn_grad)[:, :width])
    head_g = dot_t(attn_grad, jnp.pad(output_w, ((0, 0), (0, 128)))).astype(LOW)
    query_grad, key_grad, value_grad = attend_backward(
        head_q, head_k, head_v, doc_ids, logs, head_g
    )
    part_rows, grad_query_head, grad_expand_head = project_back(
        (query_grad, key_grad, value_grad),
        table, one_low, latent_low, query_w, expand_w, tok_rows,
    )
    grad_query_head = grad_query_head.reshape(groups, layers, own_rows, query_width)
    grad_expand_head = grad_expand_head.reshape(groups, layers, own_rows, fold)
    head_grads = jnp.concatenate([grad_query_head, grad_expand_head], axis=3).transpose(1, 0, 2, 3)
    head_grads = head_grads.astype(LOW)
    if layers != 2:
        head_grads = lax.psum_scatter(head_grads, "fsdp", scatter_dimension=0, tiled=True)
    own_latent = lax.dynamic_slice_in_dim(latent_proj, place * tok_rows, tok_rows, 0)
    own_table = lax.dynamic_slice_in_dim(table, place * tok_rows, tok_rows, 0)

    def make_latent(total, part, extras, outs):
        gain = extras[1][...]
        grad = total[:, width : width + LAT]
        _, normed, factor = norm_forward(extras[0][part], gain)
        inner = grad * gain
        back = factor * (inner - normed * jnp.mean(inner * normed, axis=-1, keepdims=True))
        turned = total[:, width + LAT : width + LAT + ROPE]
        turned = turned * extras[2][part, :ROPE] - swapped(turned) * extras[2][part, ROPE:]
        outs[0][part] = total[:, :width]
        gain_sum = jnp.sum(grad * normed, axis=0, keepdims=True)
        outs[1][...] = gain_sum if part.start == 0 else outs[1][...] + gain_sum
        return jnp.concatenate([back, turned, jnp.zeros_like(turned)], axis=1).astype(LOW)

    def make_input(part, extras, outs, ready):
        grad = outs[0][part] + dot_t(ready[part], extras[3][...])
        gain = extras[4][...]
        _, normed, factor = norm_forward(extras[5][part].astype(F32), gain)
        inner = grad * gain
        back = factor * (inner - normed * jnp.mean(inner * normed, axis=-1, keepdims=True))
        outs[2][part] = (extras[6][part] + back).astype(LOW)
        gain_sum = jnp.sum(grad * normed, axis=0, keepdims=True)
        outs[3][...] = gain_sum if part.start == 0 else outs[3][...] + gain_sum

    swaps = (shared_in_sent, shared_down_sent, output_sent) if layers == 2 else ()
    _, latent_gains, input_grad, grad_gain_attn, head_grads, *swapped_grads, latent_grad = ring_reduce(
        part_rows,
        [
            own_latent, gain_latent, own_table,
            small[:, : LAT + 2 * ROPE], gain_attn, tokens[0], residual_grad,
        ],
        [
            own_shape,
            jax.ShapeDtypeStruct((1, LAT), F32),
            jax.ShapeDtypeStruct((tok_rows, width), LOW),
            jax.ShapeDtypeStruct((1, width), F32),
        ],
        make_latent,
        groups,
        4,
        LAT + 2 * ROPE,
        head_grads,
        swaps=swaps,
        laterfn=make_input,
    )
    shared_kept = (shared_in_kept, shared_down_kept, output_kept)
    if layers == 2:
        shared_all = [kept + came.astype(F32) for kept, came in zip(shared_kept, swapped_grads)]
    else:
        shared_all = [spread_end(kept, None) for kept in shared_kept]
    grad_shared_in, grad_shared_down, grad_output = shared_all
    grad_query = (
        head_grads[..., :query_width].transpose(1, 0, 2).reshape(own_rows, H * query_width)
    ).astype(F32)
    grad_expand = (
        head_grads[..., query_width:]
        .reshape(H, lat_rows, NOPE + VD)
        .transpose(1, 0, 2)
        .reshape(lat_rows, H * (NOPE + VD))
    ).astype(F32)

    one_slice = lax.dynamic_slice_in_dim(one_low, place * own_width, own_width, 1)
    grad_latent = t_dot(one_slice, latent_grad.reshape(seq_len, LAT + 2 * ROPE))
    gain_sums = jnp.concatenate(
        [
            grad_gain_attn.reshape(groups, own_width),
            grad_gain_ffn.reshape(groups, own_width),
            jnp.pad(
                latent_gains.reshape(groups, layers, lat_rows),
                ((0, 0), (0, 0), (0, own_rows - lat_rows)),
            ).reshape(groups, own_width),
        ],
        axis=1,
    )
    gain_sums = lax.all_to_all(gain_sums, "seq", split_axis=0, concat_axis=0, tiled=True)
    gain_columns = jnp.sum(gain_sums, axis=0).reshape(3, own_width).T
    packed = jnp.concatenate([grad_latent[:, :at], grad_router, gain_columns], axis=1)
    packed = jnp.pad(packed, ((0, 0), (0, -packed.shape[1] % 128)))
    packed_kept, packed_sent = spread_start(packed, F32)
    if layers == 2:
        came = after(
            swap_layers(packed_sent), grad_expert_down, grad_expert_gate, grad_expert_up
        )
        packed = packed_kept + came
    else:
        packed = spread_end(packed_kept, packed_sent)
    return (
        output[None],
        input_grad[None],
        packed[:, last],
        grad_query,
        packed[:, :at],
        packed[:lat_rows, last + 2],
        grad_expand,
        grad_output,
        packed[:, last + 1],
        packed[:, at:last],
        grad_shared_in[:, :units],
        grad_shared_in[:, units + padding : 2 * units + padding],
        grad_shared_down,
        grad_expert_gate[None],
        grad_expert_up[None],
        grad_expert_down[None],
    )


def solution(mesh):
    flat = P(("seq", "fsdp"))
    rows = P(("seq", "fsdp"), None)
    tokens = P("fsdp", "seq", None)
    expert = P("seq", "fsdp", None)
    weights = (
        flat,
        rows,
        rows,
        flat,
        rows,
        rows,
        flat,
        rows,
        P("fsdp", "seq"),
        P("fsdp", "seq"),
        rows,
        expert,
        expert,
        expert,
    )
    return jax.shard_map(
        body,
        mesh=mesh,
        in_specs=(tokens, tokens, P("fsdp", None), tokens) + weights,
        out_specs=(tokens, tokens) + weights,
        check_vma=False,
    )
```

```python
import functools
import math

import jax
import jax.numpy as jnp
import numpy as np
from jax import lax
from jax.experimental import pallas as pl
from jax.experimental.pallas import tpu as pltpu
from jax.sharding import PartitionSpec as P

H = 16
NOPE = 128
ROPE = 64
VD = 128
LAT = 512
TOP = 6
EPSILON = 1e-06
HIGHEST = lax.Precision.HIGHEST
LOW = jnp.bfloat16
F32 = jnp.float32
MESH = pl.DeviceIdType.MESH


def rotary_table(count):
    powers = np.arange(ROPE // 2, dtype=np.float32) * np.float32(2.0 / ROPE)
    inverse = np.exp(powers * np.float32(-math.log(10000.0)))
    angles = np.arange(count, dtype=np.float32)[:, None] * inverse[None, :]
    cosine, sine = np.cos(angles), np.sin(angles)
    return np.concatenate([cosine, cosine, -sine, sine], axis=1)


def dot(left, right):
    return jnp.dot(left, right, preferred_element_type=F32)


def dot_t(left, right):
    return lax.dot_general(left, right, (((1,), (1,)), ((), ())), preferred_element_type=F32)


def t_dot(left, right):
    return lax.dot_general(left, right, (((0,), (0,)), ((), ())), preferred_element_type=F32)


def exact_t_dot(left, right):
    return lax.dot_general(
        left, right, (((0,), (0,)), ((), ())), precision=HIGHEST, preferred_element_type=F32
    )


def exact_dot_t(left, right):
    return lax.dot_general(
        left, right, (((1,), (1,)), ((), ())), precision=HIGHEST, preferred_element_type=F32
    )


def norm_forward(values, gain):
    factor = lax.rsqrt(jnp.mean(values * values, axis=-1, keepdims=True) + EPSILON)
    normed = values * factor
    return normed * gain, normed, factor


def norm_backward(grad_in, normed, factor, gain):
    inner = grad_in * gain
    gain_grad = jnp.sum(grad_in * normed, axis=0)
    back = factor * (inner - normed * jnp.mean(inner * normed, axis=-1, keepdims=True))
    return back, gain_grad


def swish_slope(value, sigmoid):
    return sigmoid * (1.0 + value * (1.0 - sigmoid))


def after(value, *others):
    return lax.optimization_barrier((value,) + others)[0]


def swap_layers(own):
    return lax.ppermute(own, "fsdp", ((0, 1), (1, 0)))


def layers_in_order(own, other, axis=0):
    first = lax.axis_index("fsdp") == 0
    return jnp.concatenate([jnp.where(first, own, other), jnp.where(first, other, own)], axis=axis)


def whole_over_layers(own):
    if lax.axis_size("fsdp") != 2:
        return lax.all_gather(own, "fsdp", axis=0, tiled=True)
    return layers_in_order(own, swap_layers(own))


def halves_over_layers(own):
    if lax.axis_size("fsdp") == 2:
        return own, swap_layers(own)
    whole = lax.all_gather(own, "fsdp", axis=0, tiled=True)
    half = whole.shape[0] // 2
    return whole[:half], whole[half:]


def spread_start(grad, kind=LOW):
    layers = lax.axis_size("fsdp")
    if layers != 2:
        return grad.astype(kind), None
    layer, half = lax.axis_index("fsdp"), grad.shape[0] // 2
    sent = lax.dynamic_slice_in_dim(grad, (1 - layer) * half, half, 0).astype(kind)
    return lax.dynamic_slice_in_dim(grad, layer * half, half, 0), sent


def spread_end(kept, sent):
    if sent is None:
        return lax.psum_scatter(kept, "fsdp", scatter_dimension=0, tiled=True).astype(F32)
    return kept + swap_layers(sent).astype(F32)


def spread_grad(grad, kind=LOW):
    return spread_end(*spread_start(grad, kind))


def gather_rows(block):
    return lax.all_gather(block, "seq", axis=0, tiled=True)


def scatter_rows(partial):
    return lax.psum_scatter(partial, "seq", scatter_dimension=0, tiled=True)


def ring_places(groups):
    ring = groups // 2
    me = lax.axis_index("seq")
    chip, core = me // 2, lax.rem(me, 2)
    odd = lax.rem(chip, 2)
    spot = (1 - odd) * (chip // 2) + odd * (ring - 1 - chip // 2)

    def chip_at(place):
        place = lax.rem(place + 2 * ring, ring)
        late = place // (ring // 2)
        return (1 - late) * (2 * place) + late * (2 * ring - 1 - 2 * place)

    def index_at(place, which):
        return 2 * chip_at(place) + which

    return spot, core, index_at


def enter(neighbours):
    barrier = pltpu.get_barrier_semaphore()
    for index in neighbours:
        pl.semaphore_signal(barrier, inc=1, device_id={"seq": index}, device_id_type=MESH)
    pl.semaphore_wait(barrier, len(neighbours))


class Gather:
    def __init__(self, groups, chunks, rows, source, out_ref, sems):
        self.groups, self.chunks, self.size = groups, chunks, rows // chunks
        self.source, self.out = source, out_ref
        self.send, self.recv, self.side_send, self.side_recv = sems
        self.spot, self.core, self.at = ring_places(groups)
        self.ring = groups // 2
        self.steps = groups // 4
        self.started = []

    def block(self, way, step):
        return self.at(self.spot - step if way == 0 else self.spot + step, self.core)

    def slice(self, ref, chunk):
        return ref.at[pl.ds(chunk * self.size, self.size)]

    def forward(self, step, chunk, way):
        index = self.block(way, step)
        own = self.slice(self.source if step == 0 else self.out.at[index], chunk)
        copy = pltpu.make_async_remote_copy(
            src_ref=own,
            dst_ref=self.slice(self.out.at[index], chunk),
            send_sem=self.send.at[way, step, chunk],
            recv_sem=self.recv.at[way, step, chunk],
            device_id={"seq": self.at(self.spot + (1 if way == 0 else -1), self.core)},
            device_id_type=MESH,
        )
        copy.start()
        self.started.append(copy)

    def arrived(self, step, chunk, way):
        index = self.block(way, step + 1)
        here = self.slice(self.out.at[index], chunk)
        pltpu.make_async_remote_copy(
            src_ref=here,
            dst_ref=here,
            send_sem=self.send.at[way, step, chunk],
            recv_sem=self.recv.at[way, step, chunk],
            device_id={"seq": self.at(self.spot, 1 - self.core)},
            device_id_type=MESH,
        ).wait_recv()

    def aside(self, distance, chunk):
        index = self.at(self.spot - distance, self.core)
        own = self.slice(self.source if distance == 0 else self.out.at[index], chunk)
        copy = pltpu.make_async_remote_copy(
            src_ref=own,
            dst_ref=self.slice(self.out.at[index], chunk),
            send_sem=self.side_send.at[distance, chunk],
            recv_sem=self.side_recv.at[distance, chunk],
            device_id={"seq": self.at(self.spot, 1 - self.core)},
            device_id_type=MESH,
        )
        copy.start()
        self.started.append(copy)

    def begin(self, chunk):
        for way in range(2):
            if self.steps > 1 or (chunk < self.chunks // 2) == (way == 0):
                self.forward(0, chunk, way)
        self.aside(0, chunk)

    def turn(self, step, beside=None):
        last = self.steps - 1
        for chunk in range(self.chunks):
            for way in range(2):
                half = (chunk < self.chunks // 2) == (way == 0)
                if step == last and not half:
                    continue
                self.arrived(step, chunk, way)
                if step < last and (step + 1 < last or half):
                    self.forward(step + 1, chunk, way)
                self.aside(step + 1 if way == 0 else self.ring - 1 - step, chunk)
                if beside is not None:
                    beside.step()

    def run(self, beside=None):
        for step in range(self.steps):
            self.turn(step, beside)

    def finish(self):
        for distance in range(self.ring):
            for chunk in range(self.chunks):
                here = self.slice(self.out.at[self.at(self.spot - distance, 1 - self.core)], chunk)
                pltpu.make_async_remote_copy(
                    src_ref=here,
                    dst_ref=here,
                    send_sem=self.side_send.at[distance, chunk],
                    recv_sem=self.side_recv.at[distance, chunk],
                    device_id={"seq": self.at(self.spot, 1 - self.core)},
                    device_id_type=MESH,
                ).wait_recv()
        for copy in self.started:
            copy.wait_send()


def gather_sems(groups, chunks):
    steps, ring = groups // 4, groups // 2
    return [
        pltpu.SemaphoreType.DMA((2, steps, chunks)),
        pltpu.SemaphoreType.DMA((2, steps, chunks)),
        pltpu.SemaphoreType.DMA((ring, chunks)),
        pltpu.SemaphoreType.DMA((ring, chunks)),
    ]


class Exchange:
    def __init__(self, groups, source, place_of, sems):
        self.groups, self.source, self.place_of = groups, source, place_of
        self.send, self.recv = sems
        self.me = lax.axis_index("seq")

    def copy(self, turn):
        other = lax.rem(self.me + turn, self.groups)
        return pltpu.make_async_remote_copy(
            src_ref=self.source.at[other],
            dst_ref=self.place_of(self.me),
            send_sem=self.send.at[turn],
            recv_sem=self.recv.at[turn],
            device_id={"seq": other},
            device_id_type=MESH,
        )

    def begin(self):
        for turn in range(1, self.groups):
            self.copy(turn).start()

    def arrived(self, turn):
        origin = lax.rem(self.me - turn + self.groups, self.groups)
        pltpu.make_async_remote_copy(
            src_ref=self.place_of(origin),
            dst_ref=self.place_of(origin),
            send_sem=self.send.at[turn],
            recv_sem=self.recv.at[turn],
            device_id={"seq": lax.rem(self.me + turn, self.groups)},
            device_id_type=MESH,
        ).wait_recv()
        return origin

    def finish(self):
        for turn in range(1, self.groups):
            self.copy(turn).wait_send()


def enter_all(groups, pair):
    barrier = pltpu.get_barrier_semaphore()
    me = lax.axis_index("seq")
    for turn in range(1, groups):
        pl.semaphore_signal(
            barrier, inc=1, device_id={"seq": lax.rem(me + turn, groups)}, device_id_type=MESH
        )
    if pair:
        other = {"fsdp": 1 - lax.axis_index("fsdp")}
        pl.semaphore_signal(barrier, inc=1, device_id=other, device_id_type=MESH)
    pl.semaphore_wait(barrier, groups if pair else groups - 1)


def across(source, target, send, recv):
    return pltpu.make_async_remote_copy(
        src_ref=source,
        dst_ref=target,
        send_sem=send,
        recv_sem=recv,
        device_id={"fsdp": 1 - lax.axis_index("fsdp")},
        device_id_type=MESH,
    )


def cast_cuts(rows):
    return 4 if rows % 64 == 0 else 1


class Cast:
    def __init__(self, source, target, wide, low, loads, stores):
        self.source, self.target, self.wide, self.low = source, target, wide, low
        self.loads, self.stores = loads, stores
        self.count = cast_cuts(source.shape[0])
        self.size = source.shape[0] // self.count

    def part(self, piece):
        return pl.ds(piece * self.size, self.size)

    def load(self, piece):
        return pltpu.make_async_copy(
            self.source.at[self.part(piece)], self.wide.at[piece % 2], self.loads.at[piece]
        )

    def store(self, piece):
        if isinstance(self.target, tuple):
            first = self.target[0].shape[0] // self.size
            target = self.target[0 if piece < first else 1]
            place = pl.ds((piece if piece < first else piece - first) * self.size, self.size)
        else:
            target, place = self.target, self.part(piece)
        return pltpu.make_async_copy(self.low.at[piece], target.at[place], self.stores.at[piece])

    def begin(self):
        for piece in range(min(2, self.count)):
            self.load(piece).start()

    def step(self, piece):
        if piece >= self.count:
            return
        self.load(piece).wait()
        self.low[piece] = self.wide[piece % 2].astype(LOW)
        self.store(piece).start()
        if piece + 2 < self.count:
            self.load(piece + 2).start()

    def finish(self):
        for piece in range(self.count):
            self.store(piece).wait()


def cast_scratch(array):
    rows, columns = array.shape
    count = cast_cuts(rows)
    return [
        pltpu.VMEM((2, rows // count, columns), F32),
        pltpu.VMEM((count, rows // count, columns), LOW),
        pltpu.SemaphoreType.DMA((count,)),
        pltpu.SemaphoreType.DMA((count,)),
    ]


def start_kernel(groups, chunks, pair, count, rows_ref, small_ref, heads_ref, *rest):
    sources, rest = rest[:count], rest[count:]
    rows_out, small_out, heads_out, *rest = rest
    targets, rest = rest[:count], rest[count:]
    if pair:
        bulk_out, *rest = rest
        lone_outs, rest = rest[: count - 3], rest[count - 3 :]
        gate_rest, *rest = rest
        targets = ((targets[0], gate_rest),) + tuple(targets[1:])
    casts = [
        Cast(source, target, *rest[4 * i : 4 * i + 4])
        for i, (source, target) in enumerate(zip(sources, targets))
    ]
    rest = rest[4 * count :]
    local_sems, small_y, bulk_y, lone_y, head_sems, head_recv, head_y, head_y_recv, *sems = rest
    me, layer = lax.axis_index("seq"), lax.axis_index("fsdp")
    mine = layer if pair else 0
    rows = Gather(groups, chunks, rows_ref.shape[0], rows_ref, rows_out, sems[:4])
    spare = small_ref.shape[0]
    block = small_out.at[me]
    part = block.at[pl.ds(pl.multiple_of(mine * spare, spare), spare)]
    small = Gather(groups, chunks, small_out.shape[1], block, small_out, sems[4:])
    heads = Exchange(
        groups, heads_ref, lambda index: heads_out.at[index, mine], (head_sems, head_recv)
    )
    for cast in casts:
        cast.begin()
    locals_ = [
        pltpu.make_async_copy(small_ref, part, local_sems.at[0]),
        pltpu.make_async_copy(rows_ref, rows_out.at[me], local_sems.at[1]),
        pltpu.make_async_copy(heads_ref.at[me], heads_out.at[me, mine], local_sems.at[2]),
    ]
    for copy in locals_:
        copy.start()

    def bulk(piece):
        size = casts[0].size
        return across(
            casts[0].low.at[piece],
            bulk_out.at[pl.ds(piece * size, size)],
            bulk_y.at[0, piece],
            bulk_y.at[1, piece],
        )

    def lone(index):
        low = casts[3 + index].low
        return across(low, lone_outs[index], lone_y.at[0, index], lone_y.at[1, index])

    enter_all(groups, pair)
    if pair:
        across(small_ref, part, small_y.at[0], small_y.at[1]).start()
    for chunk in range(chunks):
        rows.begin(chunk)
    heads.begin()
    if pair:
        across(heads_ref.at[me], heads_out.at[me, mine], head_y.at[0], head_y_recv.at[0]).start()
        theirs = block.at[pl.ds(pl.multiple_of((1 - mine) * spare, spare), spare)]
        across(theirs, theirs, small_y.at[0], small_y.at[1]).wait_recv()
    locals_[0].wait()
    for chunk in range(chunks):
        small.begin(chunk)
    for index, cast in enumerate(casts[3:]):
        for piece in range(cast.count):
            cast.step(piece)
        if pair:
            lone(index).start()
    shared = range(bulk_out.shape[0] // casts[0].size) if pair else ()
    for piece in range(casts[0].count):
        casts[0].step(piece)
        if piece in shared:
            bulk(piece).start()
    for step in range(rows.steps):
        casts[1].step(step)
        casts[2].step(step)
        small.turn(step)
        rows.turn(step)
        if step == 0:
            for turn in range(1, groups):
                origin = heads.arrived(turn)
                if pair:
                    own = heads_out.at[origin, mine]
                    across(own, own, head_y.at[turn], head_y_recv.at[turn]).start()
    small.finish()
    rows.finish()
    heads.finish()
    for copy in locals_[1:]:
        copy.wait()
    if pair:
        across(small_ref, part, small_y.at[0], small_y.at[1]).wait_send()
        for turn in range(groups):
            origin = lax.rem(me - turn + groups, groups)
            theirs = heads_out.at[origin, 1 - mine]
            copy = across(theirs, theirs, head_y.at[turn], head_y_recv.at[turn])
            copy.wait_send()
            copy.wait_recv()
        for piece in shared:
            bulk(piece).wait_send()
            bulk(piece).wait_recv()
        for index in range(count - 3):
            lone(index).wait_send()
            lone(index).wait_recv()
    for cast in casts:
        cast.finish()


def gather_start(rows, small, heads, weights, groups, layers, collective_id, chunks=4):
    pair = layers == 2
    if not pair:
        small = lax.all_gather(small, "fsdp", axis=0, tiled=True)
    height = small.shape[0] * (2 if pair else 1)
    dma = pltpu.SemaphoreType.DMA
    any_spec = pl.BlockSpec(memory_space=pl.ANY)
    share = weights[0].shape[0] // 4
    count = len(weights)
    outs = [
        jax.ShapeDtypeStruct((groups,) + rows.shape, LOW),
        jax.ShapeDtypeStruct((groups, height, small.shape[1]), LOW),
        jax.ShapeDtypeStruct((groups, 2 if pair else 1) + heads.shape[1:], LOW),
    ] + [jax.ShapeDtypeStruct(array.shape, LOW) for array in weights]
    gate_shape = weights[0].shape
    if pair:
        outs[3] = jax.ShapeDtypeStruct((share, gate_shape[1]), LOW)
        outs.append(outs[3])
        for array in weights[3:]:
            cuts = cast_cuts(array.shape[0])
            outs.append(
                jax.ShapeDtypeStruct((cuts, array.shape[0] // cuts, array.shape[1]), LOW)
            )
        outs.append(jax.ShapeDtypeStruct((gate_shape[0] - share, gate_shape[1]), LOW))
    rows_out, small_out, heads_out, *lows = pl.pallas_call(
        functools.partial(start_kernel, groups, chunks, pair, count),
        out_shape=outs,
        in_specs=[any_spec] * (3 + count),
        out_specs=[any_spec] * len(outs),
        scratch_shapes=[item for array in weights for item in cast_scratch(array)]
        + [dma((3,)), dma((2,)), dma((2, cast_cuts(weights[0].shape[0]))), dma((2, count))]
        + [dma((groups,))] * 4
        + gather_sems(groups, chunks)
        + gather_sems(groups, chunks),
        compiler_params=pltpu.CompilerParams(
            collective_id=collective_id, has_side_effects=True, vmem_limit_bytes=50 << 20
        ),
        cost_estimate=pl.CostEstimate(flops=0, bytes_accessed=4 << 20, transcendentals=0),
    )(rows, small, heads, *weights)
    if pair:
        gate = (lows[0], lows[-1], lows[count], swap_layers(lows[-1]))
        lone = [
            layers_in_order(own, other.reshape(own.shape))
            for own, other in zip(lows[3:count], lows[count + 1 : -1])
        ]
    else:
        lone = [whole_over_layers(own) for own in lows[3:]]
        heads_out = lax.all_gather(heads_out, "fsdp", axis=1, tiled=True)
        gate = halves_over_layers(lows[0])
    return (
        rows_out.reshape(groups * rows.shape[0], rows.shape[1]),
        small_out.reshape(groups * height, small.shape[1]),
        heads_out,
        (gate, halves_over_layers(lows[1]), halves_over_layers(lows[2])),
        lone,
    )


class Piece:
    def __init__(self, source, buffer, load_sem, products):
        self.load = pltpu.make_async_copy(source, buffer, load_sem)
        self.products = products


class Products:
    def __init__(self, held, pieces):
        self.held, self.pieces = held, pieces
        self.jobs = [(piece, which) for piece in pieces for which in range(len(piece.products))]
        self.at, self.busy = 0, {}

    def begin(self):
        for copy in self.held:
            copy.start()
        for piece in self.pieces[:2]:
            piece.load.start()

    def step(self):
        if self.at >= len(self.jobs):
            return
        piece, which = self.jobs[self.at]
        if self.at == 0:
            for copy in self.held:
                copy.wait()
        if which == 0:
            piece.load.wait()
        compute, key, stage, store = piece.products[which]
        if key in self.busy:
            self.busy[key].wait()
        stage[...] = compute()
        store.start()
        self.busy[key] = store
        self.at += 1
        if which == len(piece.products) - 1:
            later = self.pieces.index(piece) + 2
            if later < len(self.pieces):
                self.pieces[later].load.start()

    def finish(self):
        while self.at < len(self.jobs):
            self.step()
        for store in self.busy.values():
            store.wait()


class GradProducts:
    tile = 256

    def __init__(self, pair, shapes):
        self.pair = pair
        self.rows, self.width = shapes[0]
        self.units, self.tokens, self.columns = shapes[1][1], shapes[3][0], shapes[4][1]

    def outs(self):
        shared = [(self.width, self.columns), (self.columns // 2, self.width)]
        experts = [(self.width // 2, self.units)] * 2 if self.pair else []
        return [jax.ShapeDtypeStruct(shape, F32) for shape in experts + shared]

    def counts(self):
        experts = self.width // 2 // self.tile if self.pair else 0
        return experts, self.width // self.tile

    def scratch(self):
        experts, shared = self.counts()
        dma, tile = pltpu.SemaphoreType.DMA, self.tile
        scratch = [
            pltpu.VMEM((self.tokens, self.columns), LOW),
            pltpu.VMEM((self.tokens, self.columns // 2), LOW),
            pltpu.VMEM((2, self.tokens, tile), LOW),
            pltpu.VMEM((2, tile, self.columns), F32),
            pltpu.VMEM((2, self.columns // 2, tile), F32),
            dma((4,)),
            dma((experts + 2 * shared,)),
            dma((2 * experts + 2 * shared,)),
        ]
        if self.pair:
            scratch += [
                pltpu.VMEM((self.rows, self.units), LOW),
                pltpu.VMEM((self.rows, self.units), LOW),
                pltpu.VMEM((2, self.rows, tile), LOW),
                pltpu.VMEM((2, tile, self.units), F32),
            ]
        return scratch

    def build(self, ins, outs, scratch):
        rows_ref, gate_ref, up_ref, two_ref, dproj_ref, hs_ref, grads_ref = ins
        dproj, hs, pieces_buf, in_stage, out_stage, held_sems, load_sems, store_sems, *rest = scratch
        tile = self.tile
        held = [
            pltpu.make_async_copy(dproj_ref, dproj, held_sems.at[0]),
            pltpu.make_async_copy(hs_ref, hs, held_sems.at[1]),
        ]
        pieces, stored = [], 0
        experts, shared = self.counts()

        def columns(ref, index, base=0):
            return ref.at[:, pl.ds(pl.multiple_of(base + index * tile, tile), tile)]

        if self.pair:
            gate, up, slots, stage = rest
            held += [
                pltpu.make_async_copy(gate_ref, gate, held_sems.at[2]),
                pltpu.make_async_copy(up_ref, up, held_sems.at[3]),
            ]
            base = lax.axis_index("fsdp") * (self.width // 2)
            for index in range(experts):
                slot = slots.at[index % 2]
                products = []
                for number, right in enumerate((gate, up)):
                    target = outs[number].at[pl.ds(index * tile, tile)]
                    products.append(
                        (
                            functools.partial(lambda a, b: t_dot(a[...], b[...]), slot, right),
                            ("e", number),
                            stage.at[number],
                            pltpu.make_async_copy(stage.at[number], target, store_sems.at[stored]),
                        )
                    )
                    stored += 1
                pieces.append(
                    Piece(columns(rows_ref, index, base), slot, load_sems.at[len(pieces)], products)
                )
        for index in range(shared):
            slot, stage = pieces_buf.at[index % 2], in_stage.at[index % 2]
            target = outs[-2].at[pl.ds(index * tile, tile)]
            product = (
                functools.partial(lambda a, b: t_dot(a[...], b[...]), slot, dproj),
                ("i", index % 2),
                stage,
                pltpu.make_async_copy(stage, target, store_sems.at[stored]),
            )
            stored += 1
            pieces.append(Piece(columns(two_ref, index), slot, load_sems.at[len(pieces)], [product]))
        for index in range(shared):
            slot, stage = pieces_buf.at[index % 2], out_stage.at[index % 2]
            product = (
                functools.partial(lambda a, b: t_dot(b[...], a[...]), slot, hs),
                ("o", index % 2),
                stage,
                pltpu.make_async_copy(stage, columns(outs[-1], index), store_sems.at[stored]),
            )
            stored += 1
            pieces.append(Piece(columns(grads_ref, index), slot, load_sems.at[len(pieces)], [product]))
        return Products(held, pieces)


class Later:
    def __init__(self, laterfn, chunks, size, extras, outs, ready):
        self.todo = [pl.ds(chunk * size, size) for chunk in range(chunks)]
        self.run = functools.partial(laterfn, extras=extras, outs=outs, ready=ready)

    def step(self):
        if self.todo:
            self.run(self.todo.pop(0))

    def finish(self):
        while self.todo:
            self.step()


class HeadGrads:
    def __init__(
        self, groups, pair, swaps, grads_ref, out_ref, came, total, y_sems, send, recv, own_sem, swap_sems
    ):
        self.swaps, self.swap_sems = swaps, swap_sems
        self.pair, self.grads, self.out = pair, grads_ref, out_ref
        self.came, self.total, self.y_sems, self.own_sem = came, total, y_sems, own_sem
        self.mine = lax.axis_index("fsdp") if pair else 0
        self.groups = groups
        self.me = lax.axis_index("seq")
        self.spread = Exchange(groups, total, lambda index: out_ref.at[index], (send, recv))

    def cross(self):
        return across(self.grads.at[1 - self.mine], self.came, self.y_sems.at[0], self.y_sems.at[1])

    def swap(self, index):
        source, target = self.swaps[index]
        return across(source, target, self.swap_sems.at[0, index], self.swap_sems.at[1, index])

    def begin(self):
        if self.pair:
            self.cross().start()
            for index in range(len(self.swaps)):
                self.swap(index).start()

    def middle(self):
        if self.pair:
            self.cross().wait_recv()
            total = self.grads[self.mine].astype(F32) + self.came[...].astype(F32)
            self.total[...] = total.astype(LOW)
        else:
            self.total[...] = self.grads[0]
        self.spread.begin()
        self.local = pltpu.make_async_copy(
            self.total.at[self.me], self.out.at[self.me], self.own_sem
        )
        self.local.start()

    def finish(self):
        for turn in range(1, self.groups):
            self.spread.arrived(turn)
        self.spread.finish()
        self.local.wait()
        if self.pair:
            self.cross().wait_send()
            for index in range(len(self.swaps)):
                self.swap(index).wait_send()
                self.swap(index).wait_recv()


def reduce_kernel(
    groups, chunks, extras, outs, rowfn, laterfn, gathers, heads, grads, swap_count, product, *refs
):
    parts_ref = refs[0]
    if product:
        right_ref, refs = refs[1], refs[:1] + refs[2:]
    extra_refs = refs[1 : 1 + extras]
    if heads is not None:
        heads_ref, refs = refs[1 + extras], refs[: 1 + extras] + refs[2 + extras :]
        swap_ins = refs[1 + extras : 1 + extras + swap_count]
        refs = refs[: 1 + extras] + refs[1 + extras + swap_count :]
    beside = None
    if grads is not None:
        beside_ins, refs = refs[1 + extras : 8 + extras], refs[: 1 + extras] + refs[8 + extras :]
    out_refs = refs[1 + extras : 1 + extras + outs]
    rest = list(refs[1 + extras + outs :])
    if heads is not None:
        head_out = rest.pop(0)
        swaps, rest = list(zip(swap_ins, rest[:swap_count])), rest[swap_count:]
    if product:
        side_made = rest.pop()
    if grads is not None:
        count = len(grads.outs())
        beside_outs, rest = rest[:count], rest[count:]
        count = len(grads.scratch())
        beside = grads.build(beside_ins, beside_outs, rest[-count:])
        rest = rest[:-count]
        beside.begin()
    gather_ref = rest.pop(0) if gathers else None
    own, side, came, sent = rest[:4]
    own_sem, side_send, side_recv, send_sem, recv_sem = rest[4:9]
    ready = rest[9] if gathers else None
    rows = own.shape[1]
    size = rows // chunks
    ring, steps = groups // 2, groups // 4
    spot, core, at = ring_places(groups)
    sibling = {"seq": at(spot, 1 - core)}
    if heads is None:
        enter((at(spot - 1, core), at(spot + 1, core), at(spot, 1 - core)))
    else:
        head_grads = HeadGrads(groups, heads, swaps, heads_ref, head_out, *rest[-7:])
        enter_all(groups, heads)
        head_grads.begin()

    order = []
    for step in range(steps):
        order.append(steps - step)
        if step:
            order.append(ring - steps + step)
    order.append(0)
    started = []
    loads = {}

    def prepare(far):
        if product:

            def block(index):
                part = pl.ds(pl.multiple_of(index * rows, rows), rows)
                return dot(parts_ref[part], right_ref[...]).astype(LOW)

            side_made[far] = block(at(spot + far, 1 - core))
            source = side_made.at[far]
        else:
            source = parts_ref.at[at(spot + far, 1 - core)]
        copy = pltpu.make_async_remote_copy(
            src_ref=source,
            dst_ref=side.at[far],
            send_sem=side_send.at[far],
            recv_sem=side_recv.at[far],
            device_id=sibling,
            device_id_type=MESH,
        )
        copy.start()
        started.append(copy)
        if product:
            own[far] = block(at(spot + far, core))
            loads[far] = (None, copy)
            return
        load = pltpu.make_async_copy(
            parts_ref.at[at(spot + far, core)], own.at[far], own_sem.at[far]
        )
        load.start()
        loads[far] = (load, copy)

    if not product:
        for far in order:
            prepare(far)
    here = set()

    def both(far, chunk):
        if far not in here:
            here.add(far)
            if loads[far][0] is not None:
                loads[far][0].wait()
            loads[far][1].wait_recv()
        part = pl.ds(chunk * size, size)
        return own[far, part].astype(F32) + side[far, part].astype(F32)

    def neighbour_copy(way, step, chunk):
        part = pl.ds(chunk * size, size)
        return pltpu.make_async_remote_copy(
            src_ref=sent.at[way, step, part],
            dst_ref=came.at[way, step, part],
            send_sem=send_sem.at[way, step, chunk],
            recv_sem=recv_sem.at[way, step, chunk],
            device_id={"seq": at(spot + (1 if way == 0 else -1), core)},
            device_id_type=MESH,
        )

    def half(way, chunk):
        return (chunk < chunks // 2) == (way == 0)

    if product:
        prepare(steps)
    for step in range(steps):
        if product and step:
            prepare(steps - step)
            prepare(ring - steps + step)
        for chunk in range(chunks):
            for way in range(2):
                if step == 0 and not half(way, chunk):
                    continue
                far = steps - step if way == 0 else ring - (steps - step)
                part = pl.ds(chunk * size, size)
                total = both(far, chunk)
                if step > 1 or (step == 1 and half(way, chunk)):
                    neighbour_copy(way, step - 1, chunk).wait_recv()
                    total = total + came[way, step - 1, part].astype(F32)
                sent[way, step, part] = total.astype(sent.dtype)
                copy = neighbour_copy(way, step, chunk)
                copy.start()
                started.append(copy)
                if beside is not None and step and chunk == chunks - 1:
                    beside.step()
    if product:
        prepare(0)
    if heads is not None:
        head_grads.middle()
    gather = Gather(groups, chunks, rows, ready, gather_ref, rest[10:14]) if gathers else None
    for chunk in range(chunks):
        part = pl.ds(chunk * size, size)
        total = both(0, chunk)
        for way in range(2):
            if steps > 1 or half(way, chunk):
                neighbour_copy(way, steps - 1, chunk).wait_recv()
                total = total + came[way, steps - 1, part].astype(F32)
        made = rowfn(total, part, extra_refs, out_refs)
        if gathers:
            ready[part] = made
            gather.begin(chunk)
    if gathers:
        local = pltpu.make_async_copy(ready, gather_ref.at[at(spot, core)], rest[14])
        local.start()
        if laterfn is not None:
            beside = Later(laterfn, chunks, size, extra_refs, out_refs, ready)
        gather.run(beside)
        gather.finish()
        local.wait()
    if beside is not None:
        beside.finish()
    if heads is not None:
        head_grads.finish()
    for copy in started:
        copy.wait_send()


def ring_reduce(
    parts, extras, outs, rowfn, groups, collective_id, gathers=None, heads=None, grads=None,
    grad_ins=(), swaps=(), right=None, laterfn=None, chunks=4,
):
    if right is None:
        _, rows, columns = parts.shape
    else:
        rows, columns = parts.shape[0] // groups, right.shape[1]
    ring, steps = groups // 2, groups // 4
    scratch = [
        pltpu.VMEM((ring, rows, columns), LOW),
        pltpu.VMEM((ring, rows, columns), LOW),
        pltpu.VMEM((2, steps, rows, columns), LOW),
        pltpu.VMEM((2, steps, rows, columns), LOW),
        pltpu.SemaphoreType.DMA((ring,)),
        pltpu.SemaphoreType.DMA((ring,)),
        pltpu.SemaphoreType.DMA((ring,)),
        pltpu.SemaphoreType.DMA((2, steps, chunks)),
        pltpu.SemaphoreType.DMA((2, steps, chunks)),
    ]
    shapes = list(outs)
    specs = [pl.BlockSpec(memory_space=pltpu.VMEM)] * len(outs)
    extras = list(extras)
    count = len(extras)
    pair = None
    if heads is not None:
        pair = heads.shape[0] == 2
        extras.append(heads)
        shapes.append(jax.ShapeDtypeStruct(heads.shape[1:], LOW))
        specs.append(pl.BlockSpec(memory_space=pltpu.VMEM))
    any_spec = pl.BlockSpec(memory_space=pl.ANY)
    for array in swaps:
        shapes.append(jax.ShapeDtypeStruct(array.shape, LOW))
        specs.append(any_spec)
    if grads is not None:
        shapes += grads.outs()
        specs += [any_spec] * len(grads.outs())
    if gathers is not None:
        shapes.append(jax.ShapeDtypeStruct((groups, rows, gathers), LOW))
        specs.append(pl.BlockSpec(memory_space=pl.ANY))
        scratch.append(pltpu.VMEM((rows, gathers), LOW))
        scratch += gather_sems(groups, chunks)
        scratch.append(pltpu.SemaphoreType.DMA)
    if heads is not None:
        scratch += [pltpu.VMEM(heads.shape[1:], LOW)] * 2
        scratch += [pltpu.SemaphoreType.DMA((2,))]
        scratch += [pltpu.SemaphoreType.DMA((groups,))] * 2
        scratch += [pltpu.SemaphoreType.DMA, pltpu.SemaphoreType.DMA((2, max(1, len(swaps))))]
    if grads is not None:
        scratch += grads.scratch()
    if right is not None:
        scratch.append(pltpu.VMEM((ring, rows, columns), LOW))
    return pl.pallas_call(
        functools.partial(
            reduce_kernel, groups, chunks, count, len(outs), rowfn, laterfn, gathers is not None, pair, grads,
            len(swaps), right is not None,
        ),
        out_shape=shapes,
        in_specs=(
            [any_spec] if right is None else [pl.BlockSpec(memory_space=pltpu.VMEM)] * 2
        )
        + [pl.BlockSpec(memory_space=pltpu.VMEM)] * len(extras)
        + [any_spec] * (len(swaps) + len(grad_ins)),
        out_specs=specs,
        scratch_shapes=scratch,
        compiler_params=pltpu.CompilerParams(
            collective_id=collective_id, has_side_effects=True, vmem_limit_bytes=50 << 20
        ),
        cost_estimate=pl.CostEstimate(
            flops=0, bytes_accessed=4 << 20, transcendentals=0
        ),
    )(parts, *([] if right is None else [right]), *extras, *swaps, *grad_ins)


def attend_kernel(blocks, q_ref, k_ref, v_ref, col_ref, row_ref, out_ref, log_ref):
    size = q_ref.shape[0] // blocks
    scale = (NOPE + ROPE) ** (-0.5)
    for index in range(blocks):
        part = pl.ds(index * size, size)
        reach = (index + 1) * size
        scores = dot_t(q_ref[part], k_ref[:reach]) * scale
        rows = index * size + lax.broadcasted_iota(jnp.int32, (size, reach), 0)
        columns = lax.broadcasted_iota(jnp.int32, (size, reach), 1)
        allowed = (col_ref[part] == row_ref[:, :reach]) & (rows >= columns)
        scores = jnp.where(allowed, scores, -1e30)
        peak = jnp.max(scores, axis=-1, keepdims=True)
        raised = jnp.exp(scores - peak)
        total = jnp.sum(raised, axis=-1, keepdims=True)
        weights = (raised * (1.0 / total)).astype(LOW)
        out_ref[part] = dot(weights, v_ref[:reach]).astype(LOW)
        log_ref[part] = peak + jnp.log(total)


def attend_forward(head_q, head_k, head_v, doc_ids):
    seq_len = head_q.shape[0]
    return pl.pallas_call(
        functools.partial(attend_kernel, seq_len // 256),
        out_shape=[
            jax.ShapeDtypeStruct((seq_len, VD), LOW),
            jax.ShapeDtypeStruct((seq_len, 1), F32),
        ],
        compiler_params=pltpu.CompilerParams(vmem_limit_bytes=50 << 20),
        cost_estimate=pl.CostEstimate(
            flops=seq_len * seq_len * 400, bytes_accessed=4 << 20, transcendentals=seq_len * seq_len // 2
        ),
    )(head_q, head_k, head_v, doc_ids[:, None], doc_ids[None, :])


def attend_back_kernel(
    blocks, q_ref, k_ref, v_ref, g_ref, col_ref, row_ref, log_ref, dq_ref, dk_ref, dv_ref, ksum, vsum
):
    size = q_ref.shape[0] // blocks
    scale = (NOPE + ROPE) ** (-0.5)
    ksum[...] = jnp.zeros_like(ksum)
    vsum[...] = jnp.zeros_like(vsum)
    for index in range(blocks):
        part = pl.ds(index * size, size)
        reach = (index + 1) * size
        query, grad = q_ref[part], g_ref[part]
        scores = dot_t(k_ref[:reach], query) * scale
        keys = lax.broadcasted_iota(jnp.int32, (reach, size), 0)
        rows = index * size + lax.broadcasted_iota(jnp.int32, (reach, size), 1)
        allowed = (col_ref[:reach] == row_ref[:, part]) & (rows >= keys)
        weights = jnp.exp(jnp.where(allowed, scores, -1e30) - log_ref[:, part])
        vsum[:reach] += dot(weights.astype(LOW), grad)
        slopes = dot_t(v_ref[:reach], grad)
        inner = jnp.sum(weights * slopes, axis=0, keepdims=True)
        back = (weights * (slopes - inner)).astype(LOW)
        ksum[:reach] += dot(back, query)
        dq_ref[part] = (t_dot(back, k_ref[:reach]) * scale).astype(LOW)
    dk_ref[...] = (ksum[...] * scale).astype(LOW)
    dv_ref[...] = vsum[...].astype(LOW)


def attend_backward(head_q, head_k, head_v, doc_ids, logs, head_g):
    seq_len = head_q.shape[0]
    return pl.pallas_call(
        functools.partial(attend_back_kernel, seq_len // 256),
        out_shape=[
            jax.ShapeDtypeStruct((seq_len, NOPE + ROPE), LOW),
            jax.ShapeDtypeStruct((seq_len, NOPE + ROPE), LOW),
            jax.ShapeDtypeStruct((seq_len, VD), LOW),
        ],
        scratch_shapes=[
            pltpu.VMEM((seq_len, NOPE + ROPE), F32),
            pltpu.VMEM((seq_len, VD), F32),
        ],
        compiler_params=pltpu.CompilerParams(vmem_limit_bytes=56 << 20),
        cost_estimate=pl.CostEstimate(
            flops=seq_len * seq_len * 1000, bytes_accessed=6 << 20, transcendentals=seq_len * seq_len // 2
        ),
    )(head_q, head_k, head_v, head_g, doc_ids[:, None], doc_ids[None, :], logs.reshape(1, seq_len))


def swapped(values):
    half = values.shape[-1] // 2
    return jnp.concatenate([values[:, half:], values[:, :half]], axis=-1)


def project_kernel(
    x_ref, gain_ref, wq_ref, wl_ref, gain_lat_ref, we_ref, table_ref,
    one_ref, q_ref, k_ref, v_ref, m_ref, c_ref,
):
    one = norm_forward(x_ref[...].astype(F32), gain_ref[...])[0].astype(LOW)
    one_ref[...] = one
    cosine, sine = table_ref[:, :ROPE], table_ref[:, ROPE:]
    query = dot(one, wq_ref[:, : NOPE + ROPE])
    turned = query[:, NOPE:]
    q_ref[:, :NOPE] = query[:, :NOPE].astype(LOW)
    q_ref[:, NOPE:] = (turned * cosine + swapped(turned) * sine).astype(LOW)
    latent = dot(one, wl_ref[...])
    turned = latent[:, LAT : LAT + ROPE]
    k_ref[:, NOPE:] = (turned * cosine + swapped(turned) * sine).astype(LOW)
    c_ref[...] = latent[:, :LAT]
    scaled = norm_forward(latent[:, :LAT], gain_lat_ref[...])[0].astype(LOW)
    m_ref[...] = scaled
    expanded = dot(scaled, we_ref[...])
    k_ref[:, :NOPE] = expanded[:, :NOPE].astype(LOW)
    v_ref[...] = expanded[:, NOPE:].astype(LOW)


def project(rows, gain, query_w, small, gain_latent, expand_w, table, tile=256):
    seq_len, width = rows.shape

    def cut(columns):
        return pl.BlockSpec((tile, columns), lambda i: (i, 0))

    def whole(array):
        return pl.BlockSpec(array.shape, lambda i: (0, 0))

    outs = [(width, LOW), (NOPE + ROPE, LOW), (NOPE + ROPE, LOW), (VD, LOW), (LAT, LOW), (LAT, F32)]
    return pl.pallas_call(
        project_kernel,
        grid=(seq_len // tile,),
        out_shape=[jax.ShapeDtypeStruct((seq_len, c), t) for c, t in outs],
        in_specs=[
            cut(width), whole(gain), whole(query_w), whole(small), whole(gain_latent),
            whole(expand_w), cut(2 * ROPE),
        ],
        out_specs=[cut(c) for c, _ in outs],
        compiler_params=pltpu.CompilerParams(vmem_limit_bytes=50 << 20),
        cost_estimate=pl.CostEstimate(
            flops=seq_len * width * 1800, bytes_accessed=28 << 20, transcendentals=0
        ),
    )(rows, gain, query_w, small, gain_latent, expand_w, table)


def project_back_kernel(
    dq_ref, dk_ref, dv_ref, table_ref, one_ref, m_ref, wq_ref, we_ref,
    parts_ref, gq_ref, ge_ref, dq_low, de_low,
):
    cosine, sine = table_ref[:, :ROPE], table_ref[:, ROPE:]
    turned = dq_ref[:, NOPE:].astype(F32)
    dq_low[:, :NOPE] = dq_ref[:, :NOPE]
    dq_low[:, NOPE:] = (turned * cosine - swapped(turned) * sine).astype(LOW)
    de_low[:, :NOPE] = dk_ref[:, :NOPE]
    de_low[:, NOPE:] = dv_ref[...]
    blocks, rows, wide = parts_ref.shape
    width, last = one_ref.shape[1], LAT + ROPE
    parts_ref[:, :, :width] = dot_t(dq_low[...], wq_ref[:, : NOPE + ROPE]).astype(LOW).reshape(blocks, rows, width)
    parts_ref[:, :, width : width + LAT] = (
        dot_t(de_low[...], we_ref[...]).astype(LOW).reshape(blocks, rows, LAT)
    )
    parts_ref[:, :, width + LAT : width + last] = dk_ref[:, NOPE:].reshape(blocks, rows, ROPE)
    parts_ref[:, :, width + last :] = jnp.zeros((blocks, rows, wide - width - last), LOW)

    @pl.when(pl.program_id(0) == 0)
    def _():
        gq_ref[...] = jnp.zeros_like(gq_ref)
        ge_ref[...] = jnp.zeros_like(ge_ref)

    gq_ref[...] += t_dot(one_ref[...], dq_low[...])
    ge_ref[...] += t_dot(m_ref[...], de_low[...])


def project_back(grads, table, one_low, latent_low, query_w, expand_w, tok_rows, tile=256):
    seq_len, width = one_low.shape
    wide = width + LAT + 2 * ROPE

    def cut(columns):
        return pl.BlockSpec((tile, columns), lambda i: (i, 0))

    def whole(shape):
        return pl.BlockSpec(shape, lambda i: (0, 0))

    return pl.pallas_call(
        project_back_kernel,
        grid=(seq_len // tile,),
        out_shape=[
            jax.ShapeDtypeStruct((seq_len // tok_rows, tok_rows, wide), LOW),
            jax.ShapeDtypeStruct((width, NOPE + ROPE), F32),
            jax.ShapeDtypeStruct(expand_w.shape, F32),
        ],
        in_specs=[
            cut(NOPE + ROPE), cut(NOPE + ROPE), cut(VD), cut(2 * ROPE), cut(width), cut(LAT),
            whole(query_w.shape), whole(expand_w.shape),
        ],
        out_specs=[
            pl.BlockSpec((tile // tok_rows, tok_rows, wide), lambda i: (i, 0, 0)),
            whole((width, NOPE + ROPE)),
            whole(expand_w.shape),
        ],
        scratch_shapes=[pltpu.VMEM((tile, NOPE + ROPE), LOW), pltpu.VMEM((tile, NOPE + VD), LOW)],
        compiler_params=pltpu.CompilerParams(vmem_limit_bytes=50 << 20),
        cost_estimate=pl.CostEstimate(
            flops=seq_len * width * 1300, bytes_accessed=28 << 20, transcendentals=0
        ),
    )(*grads, table, one_low, latent_low, query_w, expand_w)


def blocks_of(ref, count):
    size = ref.shape[0] // count
    return [pl.ds(block * size, size) for block in range(count)]


def two_parts(values):
    high = values.astype(LOW)
    return high, (values - high.astype(F32)).astype(LOW)


class Weights:
    def __init__(self, pair, counts, refs, wholes, sems):
        self.copies, at, number = [], 0, 0
        first = lax.axis_index("fsdp") if pair else 0
        for whole, pieces in zip(wholes, counts):
            half, done, copies = whole.shape[0] // 2, 0, []
            for piece in refs[at : at + pieces]:
                side, offset = done // half, done % half
                start = (first if side == 0 else 1 - first) * half + offset
                place = pl.ds(pl.multiple_of(start, 64), piece.shape[0])
                copies.append(pltpu.make_async_copy(piece, whole.at[place], sems.at[number]))
                number += 1
                done += piece.shape[0]
            self.copies.append(copies)
            at += pieces

    def on_first(self, act):
        @pl.when(pl.program_id(0) == 0)
        def _():
            act()

    def begin(self, order):
        self.on_first(lambda: [copy.start() for which in order for copy in self.copies[which]])

    def ready(self, which):
        self.on_first(lambda: [copy.wait() for copy in self.copies[which]])


def ffn_kernel(
    pair, counts, rows_ref, chosen_ref, mine_ref, router_ref, wi_ref, wo_ref, *refs,
):
    pieces = sum(counts)
    parts, refs = refs[:pieces], refs[pieces:]
    (
        probs_ref, slot_gate_ref, in_ref, gate_ref, up_ref, inner_ref, made_ref, proj_ref, hs_ref,
        out_ref, spread, wg_ref, wu_ref, wd_ref, sems,
    ) = refs
    count = 4
    weights = Weights(pair, counts, parts, (wg_ref, wu_ref, wd_ref), sems)
    weights.begin((0, 1, 2))
    tokens, slots = blocks_of(rows_ref, count), blocks_of(chosen_ref, count)
    lanes = lax.broadcasted_iota(jnp.int32, mine_ref.shape, 1)
    logits = jnp.where(mine_ref[1:2] > 0, dot(rows_ref[...], router_ref[...]), -1e30)
    raised = jnp.exp(logits - jnp.max(logits, axis=-1, keepdims=True))
    probs = raised / jnp.sum(raised, axis=-1, keepdims=True)
    probs_ref[...] = probs
    high, rest = two_parts(jnp.sum(probs * mine_ref[0:1], axis=-1, keepdims=True))
    high, rest = high.astype(F32), rest.astype(F32)
    columns = jnp.where(lanes[0:1] == 0, high, jnp.where(lanes[0:1] == 1, rest, 0.0)).astype(LOW)
    for token, slot in zip(tokens, slots):
        size = token.size
        picked = columns[token.start : token.start + size]
        chosen = chosen_ref[slot]
        slot_gate_ref[slot] = jnp.sum(dot(chosen, picked), axis=-1, keepdims=True)
        in_ref[slot] = dot(chosen, rows_ref[token]).astype(LOW)
    weights.ready(0)
    gate = dot(in_ref[...], wg_ref[...])
    weights.ready(1)
    up = dot(in_ref[...], wu_ref[...])
    gate_ref[...] = gate
    up_ref[...] = up
    inner_ref[...] = (gate * jax.nn.sigmoid(gate) * up).astype(LOW)
    weights.ready(2)
    made = dot(inner_ref[...], wd_ref[...]).astype(LOW)
    made_ref[...] = made
    spread[...] = (slot_gate_ref[...] * made.astype(F32)).astype(LOW)
    proj = dot(rows_ref[...], wi_ref[...])
    proj_ref[...] = proj
    half = proj.shape[1] // 2
    gate, up = proj[:, :half], proj[:, half:]
    hs_ref[...] = (gate * jax.nn.sigmoid(gate) * up).astype(LOW)
    for token, slot in zip(tokens, slots):
        total = t_dot(chosen_ref[slot], spread[slot]) + dot(hs_ref[token], wo_ref[...])
        out_ref[token] = total.astype(LOW)


def ffn_back_kernel(
    pair, counts, grads_ref, chosen_ref, mine_ref, slot_gate_ref, made_ref, gate_ref, up_ref,
    proj_ref, wi_ref, wo_ref, *refs,
):
    pieces = sum(counts)
    parts, refs = refs[:pieces], refs[pieces:]
    dy_ref, dgate_ref, dup_ref, dproj_ref, parts_ref, spread, wg_ref, wu_ref, wd_ref, sems = refs
    count = 4
    width = grads_ref.shape[1]
    weights = Weights(pair, counts, parts, (wg_ref, wu_ref, wd_ref), sems)
    weights.begin((2, 0, 1))
    tokens, slots = blocks_of(grads_ref, count), blocks_of(chosen_ref, count)
    mine, shifted = mine_ref[0:1], mine_ref[2:3]
    for token, slot in zip(tokens, slots):
        picked = dot(chosen_ref[slot], grads_ref[token])
        dy_ref[slot] = (slot_gate_ref[slot] * picked).astype(LOW)
        score = jnp.sum(picked * made_ref[slot].astype(F32), axis=-1, keepdims=True)
        high, rest = two_parts(score)
        spread[slot, width:] = (high.astype(F32) * mine + rest.astype(F32) * shifted).astype(LOW)
    weights.ready(2)
    inner = dot_t(dy_ref[...], wd_ref[...])
    gate = gate_ref[...]
    sigmoid = jax.nn.sigmoid(gate)
    dgate_ref[...] = (inner * up_ref[...] * swish_slope(gate, sigmoid)).astype(LOW)
    dup_ref[...] = (inner * gate * sigmoid).astype(LOW)
    weights.ready(0)
    weights.ready(1)
    back = dot_t(dgate_ref[...], wg_ref[...]) + dot_t(dup_ref[...], wu_ref[...])
    spread[:, :width] = back.astype(LOW)
    half = proj_ref.shape[1] // 2
    gate, up = proj_ref[:, :half], proj_ref[:, half:]
    sigmoid = jax.nn.sigmoid(gate)
    inner = dot_t(grads_ref[...], wo_ref[...])
    dproj_ref[:, :half] = (inner * up * swish_slope(gate, sigmoid)).astype(LOW)
    dproj_ref[:, half:] = (inner * gate * sigmoid).astype(LOW)
    for block, (token, slot) in enumerate(zip(tokens, slots)):
        total = t_dot(chosen_ref[slot], spread[slot])
        parts_ref[block, :, :width] = (
            total[:, :width] + dot_t(dproj_ref[token], wi_ref[...])
        ).astype(LOW)
        parts_ref[block, :, width:] = total[:, width:].astype(LOW)


def row_grid(kernel, steps, cuts, outs, scratch, flops):
    def cut(shape):
        rest = (0,) * (len(shape) - 1)
        return pl.BlockSpec((shape[0] // steps,) + tuple(shape[1:]), lambda i: (i,) + rest)

    def whole(shape):
        rest = (0,) * len(shape)
        return pl.BlockSpec(tuple(shape), lambda i: rest, pipeline_mode=pl.Buffered(1))

    operands = [array for array, _ in cuts]
    return pl.pallas_call(
        kernel,
        grid=(steps,),
        out_shape=outs,
        in_specs=[
            pl.BlockSpec(memory_space=pl.ANY)
            if fixed is None
            else whole(a.shape) if fixed else cut(a.shape)
            for a, fixed in cuts
        ],
        out_specs=[cut(o.shape) for o in outs],
        scratch_shapes=scratch,
        compiler_params=pltpu.CompilerParams(vmem_limit_bytes=60 << 20),
        cost_estimate=pl.CostEstimate(flops=flops, bytes_accessed=60 << 20, transcendentals=0),
    )(*operands)


def grad_in_kernel(layer_ref, rows_ref, grads_ref, sent_ref):
    sent_ref[...] = t_dot(rows_ref[...], grads_ref[...]).astype(LOW)


def grad_in(rows, grads, tile=512):
    count, width = rows.shape
    columns = grads.shape[1]
    half = width // 2 // tile
    layer = lax.axis_index("fsdp").reshape(1)
    return pl.pallas_call(
        grad_in_kernel,
        grid_spec=pltpu.PrefetchScalarGridSpec(
            num_scalar_prefetch=1,
            grid=(half,),
            in_specs=[
                pl.BlockSpec((count, tile), lambda i, layer: (0, i + (1 - layer[0]) * half)),
                pl.BlockSpec((count, columns), lambda i, _: (0, 0)),
            ],
            out_specs=pl.BlockSpec((tile, columns), lambda i, _: (i, 0)),
        ),
        out_shape=jax.ShapeDtypeStruct((width // 2, columns), LOW),
        compiler_params=pltpu.CompilerParams(vmem_limit_bytes=50 << 20),
        cost_estimate=pl.CostEstimate(
            flops=count * width * columns, bytes_accessed=10 << 20, transcendentals=0
        ),
    )(layer, rows, grads)


def grad_out_kernel(layer_ref, inner_ref, grads_ref, sent_ref, kept_ref, made):
    half = sent_ref.shape[0]
    layer = layer_ref[0]
    made[...] = t_dot(inner_ref[...], grads_ref[...])
    sent_ref[...] = made[pl.ds(pl.multiple_of((1 - layer) * half, 8), half)].astype(LOW)
    kept_ref[...] = made[pl.ds(pl.multiple_of(layer * half, 8), half)]


def grad_out(inner, grads, tile=512):
    count, units = inner.shape
    width = grads.shape[1]
    layer = lax.axis_index("fsdp").reshape(1)
    return pl.pallas_call(
        grad_out_kernel,
        grid_spec=pltpu.PrefetchScalarGridSpec(
            num_scalar_prefetch=1,
            grid=(width // tile,),
            in_specs=[
                pl.BlockSpec((count, units), lambda i, _: (0, 0)),
                pl.BlockSpec((count, tile), lambda i, _: (0, i)),
            ],
            out_specs=[
                pl.BlockSpec((units // 2, tile), lambda i, _: (0, i)),
                pl.BlockSpec((units // 2, tile), lambda i, _: (0, i)),
            ],
            scratch_shapes=[pltpu.VMEM((units, tile), F32)],
        ),
        out_shape=[
            jax.ShapeDtypeStruct((units // 2, width), LOW),
            jax.ShapeDtypeStruct((units // 2, width), F32),
        ],
        compiler_params=pltpu.CompilerParams(vmem_limit_bytes=50 << 20),
        cost_estimate=pl.CostEstimate(
            flops=2 * count * width * units, bytes_accessed=16 << 20, transcendentals=0
        ),
    )(layer, inner, grads)


def body(
    tokens,
    cotangent,
    segments,
    routes,
    norm_attn,
    w_query,
    w_latent,
    norm_latent,
    w_expand,
    w_output,
    norm_ffn,
    w_router,
    w_shared_gate,
    w_shared_up,
    w_shared_down,
    w_expert_gate,
    w_expert_up,
    w_expert_down,
):
    groups = lax.axis_size("seq")
    layers = lax.axis_size("fsdp")
    both = ("seq", "fsdp")
    place = lax.axis_index("seq")
    tok_rows, width = tokens.shape[1], tokens.shape[2]
    seq_len = segments.shape[1]
    own_rows = w_query.shape[0]
    lat_rows = w_expand.shape[0]
    experts = w_router.shape[1]
    capacity = tok_rows // 2
    query_width = NOPE + ROPE
    hidden_own = tokens[0].astype(F32)
    grad_own = cotangent[0].astype(F32)
    doc_ids = segments[0]

    lat_column = jnp.pad(norm_latent[:, None], ((0, own_rows - lat_rows), (0, 0)))
    at = LAT + ROPE
    route_columns = routes.reshape(own_rows, tok_rows * TOP // own_rows).astype(F32)
    packed = [w_latent, w_router, norm_attn[:, None], norm_ffn[:, None], lat_column, route_columns]
    packed = jnp.concatenate(packed, axis=1).astype(LOW)
    used = packed.shape[1]
    last = at + experts
    packed = jnp.pad(packed, ((0, 0), (0, -used % 128)))

    fold = lat_rows * (NOPE + VD) // own_rows
    query_parts = w_query.astype(LOW).reshape(own_rows, H, query_width).transpose(1, 0, 2)
    expand_parts = (
        w_expand.astype(LOW)
        .reshape(lat_rows, H, NOPE + VD)
        .transpose(1, 0, 2)
        .reshape(H, own_rows, fold)
    )
    head_parts = jnp.concatenate([query_parts, expand_parts], axis=2)
    hidden_low, small, head_parts, expert_sets, lone = gather_start(
        tokens[0],
        packed,
        head_parts,
        (
            w_expert_gate[0], w_expert_up[0], w_expert_down[0],
            jnp.concatenate([w_shared_gate, w_shared_up], axis=1), w_shared_down, w_output,
        ),
        groups,
        layers,
        1,
    )
    query_w = head_parts.reshape(width, query_width + fold)
    expand_w = head_parts[..., query_width:].reshape(LAT, NOPE + VD)
    router_w = jnp.pad(small[:, at:last], ((0, 0), (0, 128 - experts)))
    all_routes = small[:, last + 3 : used].reshape(groups, layers, -1)
    all_routes = lax.dynamic_index_in_dim(all_routes, lax.axis_index("fsdp"), 1, keepdims=False)
    all_routes = all_routes.reshape(groups, tok_rows, TOP)
    gains = small[:, last : last + 3].astype(F32).T
    gain_attn, gain_ffn = gains[0:1], gains[1:2]
    gain_latent = gains[2].reshape(groups * layers, own_rows)[:, :lat_rows].reshape(1, LAT)

    units = w_shared_gate.shape[1]
    padding = -units % 128
    spare = ((0, 0), (0, padding))
    shared_pair_w, shared_down_w, output_w = lone
    shared_gate_w, shared_up_w = shared_pair_w[:, :units], shared_pair_w[:, units:]
    shared_in_w = jnp.concatenate([jnp.pad(shared_gate_w, spare), jnp.pad(shared_up_w, spare)], axis=1)
    shared_down_w = jnp.pad(shared_down_w, ((0, padding), (0, 0)))

    grad_low = gather_rows(after(cotangent[0], hidden_low))

    table = jnp.asarray(rotary_table(seq_len))
    one_low, head_q, head_k, head_v, latent_low, latent_proj = project(
        hidden_low, gain_attn, query_w, small, gain_latent, expand_w, table
    )
    head_out, logs = attend_forward(head_q, head_k, head_v, doc_ids)
    def make_two(total, part, extras, outs):
        row_sum = extras[0][part].astype(F32) + total
        outs[0][part] = row_sum
        return norm_forward(row_sum, extras[1][...])[0].astype(LOW)

    own_shape = jax.ShapeDtypeStruct((tok_rows, width), F32)
    residual, two_low = ring_reduce(
        head_out, [tokens[0], gain_ffn], [own_shape], make_two, groups, 2, width, right=output_w
    )
    two_low = after(two_low, grad_low).reshape(seq_len, width)

    named = jnp.any(all_routes == place.astype(LOW), axis=-1)
    rank = jnp.cumsum(named.astype(jnp.int32), axis=1) - 1
    slots = jnp.arange(capacity, dtype=jnp.int32)
    chosen = named[:, None, :] & (rank[:, None, :] == slots[None, :, None])
    chosen = chosen.astype(LOW).reshape(groups * capacity, tok_rows)
    lanes = jnp.arange(128, dtype=jnp.int32)
    mine = jnp.stack(
        [(lanes == place), (lanes < experts), (lanes == place + experts)] + [lanes < 0] * 5
    ).astype(F32)
    slot_count, unit_count = groups * capacity, w_expert_gate.shape[2]
    expert_w = [(piece, None) for pieces in expert_sets for piece in pieces]
    counts = tuple(len(pieces) for pieces in expert_sets)
    expert_scratch = [
        pltpu.VMEM((width, unit_count), LOW),
        pltpu.VMEM((width, unit_count), LOW),
        pltpu.VMEM((unit_count, width), LOW),
        pltpu.SemaphoreType.DMA((len(expert_w),)),
    ]
    columns = shared_in_w.shape[1]

    def array(rows, columns, kind=LOW):
        return jax.ShapeDtypeStruct((rows, columns), kind)

    steps = groups // 4
    routed_flops = 6 * slot_count * width * unit_count
    probs, slot_gate, expert_in, gate_proj, up_proj, inner_low, made, shared_proj, shared_low, part_out = row_grid(
        functools.partial(ffn_kernel, layers == 2, counts),
        steps,
        [
            (two_low, False), (chosen, False), (mine, True), (router_w, True),
            (shared_in_w, True), (shared_down_w, True), *expert_w,
        ],
        [
            array(seq_len, 128, F32), array(slot_count, 1, F32), array(slot_count, width),
            array(slot_count, unit_count, F32), array(slot_count, unit_count, F32),
            array(slot_count, unit_count), array(slot_count, width), array(seq_len, columns, F32),
            array(seq_len, columns // 2), array(seq_len, width),
        ],
        [pltpu.VMEM((slot_count // steps, width), LOW)] + expert_scratch,
        routed_flops * 3 // 2,
    )
    ffn_out = scatter_rows(part_out).astype(F32)
    output = (residual + ffn_out).astype(LOW)

    made_grad, gate_grad, up_grad, shared_grads, part_grad = row_grid(
        functools.partial(ffn_back_kernel, layers == 2, counts),
        steps,
        [
            (grad_low, False), (chosen, False), (mine, True), (slot_gate, False), (made, False),
            (gate_proj, False), (up_proj, False), (shared_proj, False),
            (shared_in_w, True), (shared_down_w, True), *expert_w,
        ],
        [
            array(slot_count, width), array(slot_count, unit_count), array(slot_count, unit_count),
            array(seq_len, columns),
            jax.ShapeDtypeStruct((groups, tok_rows, width + 128), LOW),
        ],
        [pltpu.VMEM((slot_count // steps, width + 128), LOW)] + expert_scratch,
        routed_flops * 3 // 2,
    )

    if layers == 2:
        down_sent, down_kept = grad_out(inner_low, made_grad)
        gate_sent = grad_in(expert_in, gate_grad)
        up_sent = grad_in(expert_in, up_grad)
        part_grad = after(part_grad, down_sent, gate_sent, up_sent)
    else:
        down_kept, down_sent = spread_start(t_dot(inner_low, made_grad))
        gate_kept, gate_sent = spread_start(t_dot(expert_in, gate_grad))
        up_kept, up_sent = spread_start(t_dot(expert_in, up_grad))
    own_probs = lax.dynamic_slice_in_dim(probs, place * tok_rows, tok_rows, 0)

    def make_attn(total, part, extras, outs):
        probs = extras[0][part]
        score = total[:, width:]
        score = score + jnp.concatenate([score[:, experts:], score[:, :experts]], axis=1)
        logit = probs * (score - jnp.sum(probs * score, axis=-1, keepdims=True))
        high, rest = two_parts(logit)
        grad = total[:, :width] + dot_t(high, extras[4][...]) + dot_t(rest, extras[4][...])
        gain = extras[1][...]
        _, normed, factor = norm_forward(extras[2][part], gain)
        inner = grad * gain
        back = factor * (inner - normed * jnp.mean(inner * normed, axis=-1, keepdims=True))
        back = extras[3][part].astype(F32) + back
        outs[0][part] = back
        gain_sum = jnp.sum(grad * normed, axis=0, keepdims=True)
        outs[1][...] = gain_sum if part.start == 0 else outs[1][...] + gain_sum
        rest = rest.astype(F32)
        rest = jnp.concatenate([rest[:, 128 - experts :], rest[:, : 128 - experts]], axis=1)
        return jnp.concatenate([back, high.astype(F32) + rest], axis=1).astype(LOW)

    grad_ins = (expert_in, gate_grad, up_grad, two_low, shared_grads, shared_low, grad_low)
    grads = GradProducts(layers == 2, [array.shape for array in grad_ins])
    residual_grad, grad_gain_ffn, *made_grads, attn_grad = ring_reduce(
        part_grad,
        [own_probs, gain_ffn, residual, cotangent[0], router_w],
        [own_shape, jax.ShapeDtypeStruct((1, width), F32)],
        make_attn,
        groups,
        3,
        width + 128,
        None,
        grads,
        grad_ins,
    )
    shared_in_kept, shared_in_sent = spread_start(made_grads[-2])
    shared_down_kept, shared_down_sent = spread_start(made_grads[-1][:units])
    if layers == 2:
        gate_kept, up_kept = made_grads[:2]
    grad_expert_down = spread_end(down_kept, down_sent)
    grad_expert_gate = spread_end(gate_kept, gate_sent)
    grad_expert_up = spread_end(up_kept, up_sent)
    attn_grad = attn_grad.reshape(seq_len, width + 128)

    own_width = width // groups
    two_slice = lax.dynamic_slice_in_dim(two_low, place * own_width, own_width, 1)
    grad_router = t_dot(two_slice, attn_grad[:, width:])
    grad_router = grad_router[:, :experts] + grad_router[:, experts : 2 * experts]

    output_kept, output_sent = spread_start(t_dot(head_out, attn_grad)[:, :width])
    head_g = dot_t(attn_grad, jnp.pad(output_w, ((0, 0), (0, 128)))).astype(LOW)
    query_grad, key_grad, value_grad = attend_backward(
        head_q, head_k, head_v, doc_ids, logs, head_g
    )
    part_rows, grad_query_head, grad_expand_head = project_back(
        (query_grad, key_grad, value_grad),
        table, one_low, latent_low, query_w, expand_w, tok_rows,
    )
    grad_query_head = grad_query_head.reshape(groups, layers, own_rows, query_width)
    grad_expand_head = grad_expand_head.reshape(groups, layers, own_rows, fold)
    head_grads = jnp.concatenate([grad_query_head, grad_expand_head], axis=3).transpose(1, 0, 2, 3)
    head_grads = head_grads.astype(LOW)
    if layers != 2:
        head_grads = lax.psum_scatter(head_grads, "fsdp", scatter_dimension=0, tiled=True)
    own_latent = lax.dynamic_slice_in_dim(latent_proj, place * tok_rows, tok_rows, 0)
    own_table = lax.dynamic_slice_in_dim(table, place * tok_rows, tok_rows, 0)

    def make_latent(total, part, extras, outs):
        gain = extras[1][...]
        grad = total[:, width : width + LAT]
        _, normed, factor = norm_forward(extras[0][part], gain)
        inner = grad * gain
        back = factor * (inner - normed * jnp.mean(inner * normed, axis=-1, keepdims=True))
        turned = total[:, width + LAT : width + LAT + ROPE]
        turned = turned * extras[2][part, :ROPE] - swapped(turned) * extras[2][part, ROPE:]
        outs[0][part] = total[:, :width]
        gain_sum = jnp.sum(grad * normed, axis=0, keepdims=True)
        outs[1][...] = gain_sum if part.start == 0 else outs[1][...] + gain_sum
        return jnp.concatenate([back, turned, jnp.zeros_like(turned)], axis=1).astype(LOW)

    def make_input(part, extras, outs, ready):
        grad = outs[0][part] + dot_t(ready[part], extras[3][...])
        gain = extras[4][...]
        _, normed, factor = norm_forward(extras[5][part].astype(F32), gain)
        inner = grad * gain
        back = factor * (inner - normed * jnp.mean(inner * normed, axis=-1, keepdims=True))
        outs[2][part] = (extras[6][part] + back).astype(LOW)
        gain_sum = jnp.sum(grad * normed, axis=0, keepdims=True)
        outs[3][...] = gain_sum if part.start == 0 else outs[3][...] + gain_sum

    swaps = (shared_in_sent, shared_down_sent, output_sent) if layers == 2 else ()
    _, latent_gains, input_grad, grad_gain_attn, head_grads, *swapped_grads, latent_grad = ring_reduce(
        part_rows,
        [
            own_latent, gain_latent, own_table,
            small[:, : LAT + 2 * ROPE], gain_attn, tokens[0], residual_grad,
        ],
        [
            own_shape,
            jax.ShapeDtypeStruct((1, LAT), F32),
            jax.ShapeDtypeStruct((tok_rows, width), LOW),
            jax.ShapeDtypeStruct((1, width), F32),
        ],
        make_latent,
        groups,
        4,
        LAT + 2 * ROPE,
        head_grads,
        swaps=swaps,
        laterfn=make_input,
    )
    shared_kept = (shared_in_kept, shared_down_kept, output_kept)
    if layers == 2:
        shared_all = [kept + came.astype(F32) for kept, came in zip(shared_kept, swapped_grads)]
    else:
        shared_all = [spread_end(kept, None) for kept in shared_kept]
    grad_shared_in, grad_shared_down, grad_output = shared_all
    grad_query = (
        head_grads[..., :query_width].transpose(1, 0, 2).reshape(own_rows, H * query_width)
    ).astype(F32)
    grad_expand = (
        head_grads[..., query_width:]
        .reshape(H, lat_rows, NOPE + VD)
        .transpose(1, 0, 2)
        .reshape(lat_rows, H * (NOPE + VD))
    ).astype(F32)

    one_slice = lax.dynamic_slice_in_dim(one_low, place * own_width, own_width, 1)
    grad_latent = t_dot(one_slice, latent_grad.reshape(seq_len, LAT + 2 * ROPE))
    gain_sums = jnp.concatenate(
        [
            grad_gain_attn.reshape(groups, own_width),
            grad_gain_ffn.reshape(groups, own_width),
            jnp.pad(
                latent_gains.reshape(groups, layers, lat_rows),
                ((0, 0), (0, 0), (0, own_rows - lat_rows)),
            ).reshape(groups, own_width),
        ],
        axis=1,
    )
    gain_sums = lax.all_to_all(gain_sums, "seq", split_axis=0, concat_axis=0, tiled=True)
    gain_columns = jnp.sum(gain_sums, axis=0).reshape(3, own_width).T
    packed = jnp.concatenate([grad_latent[:, :at], grad_router, gain_columns], axis=1)
    packed = jnp.pad(packed, ((0, 0), (0, -packed.shape[1] % 128)))
    packed_kept, packed_sent = spread_start(packed, F32)
    if layers == 2:
        came = after(
            swap_layers(packed_sent), grad_expert_down, grad_expert_gate, grad_expert_up
        )
        packed = packed_kept + came
    else:
        packed = spread_end(packed_kept, packed_sent)
    return (
        output[None],
        input_grad[None],
        packed[:, last],
        grad_query,
        packed[:, :at],
        packed[:lat_rows, last + 2],
        grad_expand,
        grad_output,
        packed[:, last + 1],
        packed[:, at:last],
        grad_shared_in[:, :units],
        grad_shared_in[:, units + padding : 2 * units + padding],
        grad_shared_down,
        grad_expert_gate[None],
        grad_expert_up[None],
        grad_expert_down[None],
    )


def solution(mesh):
    flat = P(("seq", "fsdp"))
    rows = P(("seq", "fsdp"), None)
    tokens = P("fsdp", "seq", None)
    expert = P("seq", "fsdp", None)
    weights = (
        flat,
        rows,
        rows,
        flat,
        rows,
        rows,
        flat,
        rows,
        P("fsdp", "seq"),
        P("fsdp", "seq"),
        rows,
        expert,
        expert,
        expert,
    )
    return jax.shard_map(
        body,
        mesh=mesh,
        in_specs=(tokens, tokens, P("fsdp", None), tokens) + weights,
        out_specs=(tokens, tokens) + weights,
        check_vma=False,
    )
```
